256 devices in a mesh: gx: 8 (over z_hi, y), gy: 8 (over z_lo, core), gz: 4 (over x).
Axes of the slice: x: 4, y: 4, z: 8 (z_hi: 2, z_lo: 4; z = z_hi * 4 + z_lo), core: 2. Of those that a mesh axis runs over, the one named last changes fastest.
Arguments:
- charge: float32 [64, 128, 1024], P('gx', 'gy', 'gz'), may hold values from -6 to 6
- dielectric: float32 [64, 128, 1024], P('gx', 'gy', 'gz'), may hold values from 1 to 80
Outputs:
- potential: float32 [64, 128, 1024], P('gx', 'gy', 'gz')
The draws below stay inside these ranges and needn't reach their ends.
All inputs are finite; a program needn't handle non-finite values.
Results may differ from the reference program's by a relative error of at most 0.0001.
Values sent between devices are 32-bit elements; how exact they have to be, the bound alone decides.
A program may use at most 64 MiB of HBM per device.

```python
import math
import jax
import jax.numpy as jnp
from jax import lax

DEPTH = 3
SMOOTH = 2
COARSE_SWEEPS = 8
NX = 64
NY = 128
NZ = 1024


def draw_charge(key, part):
    key = jax.random.fold_in(key, 11)
    return jax.random.truncated_normal(key, -6.0, 6.0, (NX, NY, NZ), jnp.float32)


def shard_levels(own_key, dims, cuts, smallest, largest):
    def one(position, parts):
        steps = jax.random.uniform(jax.random.fold_in(jax.random.fold_in(own_key, 6), position), (parts,), jnp.float32, smallest / len(cuts), largest / len(cuts))
        return jnp.repeat(jnp.exp(steps), dims[position] // parts).reshape((-1,) + (1,) * (len(dims) - position - 1))

    gain = one(*cuts[0])
    for cut in cuts[1:]:
        gain = gain * one(*cut)
    return gain


def setup_inputs(seed: int = 0) -> dict:
    seeds = jax.random.split(jax.random.key(seed), 3)
    return {
        "charge": draw_charge(jax.random.fold_in(seeds[2], 71), 0),
        "dielectric": jnp.clip(jnp.exp(math.log(80.0) - 4.3820266 * jax.random.uniform(seeds[1], (NX, NY, NZ), jnp.float32) ** shard_levels(seeds[1], (NX, NY, NZ), ((0, 8), (1, 8), (2, 4)), -0.2, 0.2)), 1.0, 80.0),
    }


OMEGA = 0.8
FOURPI = 4.0 * math.pi
EDGE_VALUE = 1.0


def harmonic(first, second):
    return 2.0 * first * second / (first + second)


def coefficients(shell):
    face_x = harmonic(shell[1:, 1:-1, 1:-1], shell[:-1, 1:-1, 1:-1])
    face_y = harmonic(shell[1:-1, 1:, 1:-1], shell[1:-1, :-1, 1:-1])
    face_z = harmonic(shell[1:-1, 1:-1, 1:], shell[1:-1, 1:-1, :-1])
    diagonal = face_x[1:] + face_x[:-1] + face_y[:, 1:] + face_y[:, :-1] + face_z[:, :, 1:] + face_z[:, :, :-1]
    return (face_x, face_y, face_z, diagonal)


def operate(padded, coeffs, factor):
    face_x, face_y, face_z, diagonal = coeffs
    centre = padded[1:-1, 1:-1, 1:-1]
    beside_all = face_x[1:] * padded[2:, 1:-1, 1:-1] + face_x[:-1] * padded[:-2, 1:-1, 1:-1]
    beside_all = beside_all + face_y[:, 1:] * padded[1:-1, 2:, 1:-1] + face_y[:, :-1] * padded[1:-1, :-2, 1:-1]
    beside_all = beside_all + face_z[:, :, 1:] * padded[1:-1, 1:-1, 2:] + face_z[:, :, :-1] * padded[1:-1, 1:-1, :-2]
    return factor * (diagonal * centre - beside_all)


def relax(padded, source, coeffs, factor):
    centre = padded[1:-1, 1:-1, 1:-1]
    return centre + OMEGA * (source - operate(padded, coeffs, factor)) / (factor * coeffs[3])


def coarsen(values):
    size_x, size_y, size_z = values.shape
    return values.reshape(size_x // 2, 2, size_y // 2, 2, size_z // 2, 2).mean(axis=(1, 3, 5))


def refine_axis(padded, dimension):
    length_cells = padded.shape[dimension] - 2
    centre = lax.slice_in_dim(padded, 1, length_cells + 1, axis=dimension)
    before_cells = lax.slice_in_dim(padded, 0, length_cells, axis=dimension)
    after_cells = lax.slice_in_dim(padded, 2, length_cells + 2, axis=dimension)
    first_child = 0.75 * centre + 0.25 * before_cells
    second_child = 0.75 * centre + 0.25 * after_cells
    stacked = jnp.stack([first_child, second_child], axis=dimension + 1)
    new_shape = list(centre.shape)
    new_shape[dimension] = 2 * length_cells
    return stacked.reshape(new_shape)


def prolong(padded):
    return refine_axis(refine_axis(refine_axis(padded, 0), 1), 2)


def cycle(source, level_index, coeff_list, pad_potential, pad_correction, solve_coarse):
    if level_index == DEPTH:
        return solve_coarse(source)
    coeffs = coeff_list[level_index]
    factor = 0.25 ** level_index
    estimate = OMEGA * source / (factor * coeffs[3])
    for sweep_index in range(SMOOTH - 1):
        estimate = relax(pad_potential(estimate), source, coeffs, factor)
    residue = source - operate(pad_potential(estimate), coeffs, factor)
    correction = cycle(coarsen(residue), level_index + 1, coeff_list, pad_potential, pad_correction, solve_coarse)
    estimate = estimate + prolong(pad_correction(correction))
    for sweep_index in range(SMOOTH):
        estimate = relax(pad_potential(estimate), source, coeffs, factor)
    return estimate


def zero_pad(values):
    return jnp.pad(values, 1)


def reference(charge, dielectric):
    dielectrics = [dielectric]
    for level_index in range(DEPTH):
        dielectrics.append(coarsen(dielectrics[-1]))
    coeff_list = [coefficients(jnp.pad(level_eps, 1, constant_values=EDGE_VALUE)) for level_eps in dielectrics]

    def solve_coarse(source):
        coeffs = coeff_list[DEPTH]
        factor = 0.25 ** DEPTH
        estimate = OMEGA * source / (factor * coeffs[3])
        for sweep_index in range(COARSE_SWEEPS - 1):
            estimate = relax(zero_pad(estimate), source, coeffs, factor)
        return estimate

    return cycle(FOURPI * charge, 0, coeff_list, zero_pad, zero_pad, solve_coarse)
```

```python
import functools
import itertools
import math

import jax
import jax.numpy as jnp
from jax import lax
from jax.experimental import pallas as pl
from jax.experimental.pallas import tpu as pltpu
from jax.sharding import PartitionSpec as P

MESH = pl.DeviceIdType.MESH
F32 = jnp.float32
OMEGA = 0.8
KEEP = 1.0 - OMEGA
FOURPI = 4.0 * math.pi
COARSE_SWEEPS = 8
NX, NY, NZ = 64, 128, 1024
GX, GY, GZ = 8, 8, 4
DIRS = [d for d in itertools.product((-1, 0, 1), repeat=3) if d != (0, 0, 0)]
FLAT = [d for d in itertools.product((-1, 0, 1), repeat=2) if d != (0, 0)]


def roll(values, shift, axis):
    return pltpu.roll(values, shift % values.shape[axis], axis)


def dot(a, b):
    return jnp.dot(a, b, preferred_element_type=F32, precision=lax.Precision.HIGHEST)


def place(index, own, size):
    half = (size - own) // 2
    return jnp.where(index < own + half, index, index - size)


def iota(shape, axis):
    return lax.broadcasted_iota(jnp.int32, shape, axis)


def restrict_z(own, size, out_own, out_size, weight):
    shape = (size, out_size)
    p = place(iota(shape, 0), own, size)
    q = place(iota(shape, 1), out_own, out_size)
    return jnp.where((p >> 1) == q, weight, 0.0).astype(F32)


def pair_rows(groups, own, weight):
    shape = (groups * own // 2, groups * own)
    return jnp.where((iota(shape, 1) >> 1) == iota(shape, 0), weight, 0.0).astype(F32)


def spread(q, p):
    parent = p >> 1
    other = jnp.where((p & 1) == 0, parent - 1, parent + 1)
    return jnp.where(q == parent, 0.75, jnp.where(q == other, 0.25, 0.0)).astype(F32)


def prolong_z(own, size, out_own, out_size):
    shape = (size, out_size)
    return spread(place(iota(shape, 0), own, size), place(iota(shape, 1), out_own, out_size))


def prolong_y(own, size, out_own, out_size):
    shape = (out_size, size)
    return spread(place(iota(shape, 1), own, size), place(iota(shape, 0), out_own, out_size))


def kernel(f_in, e_in, out, s):
    s = dict(zip(NAMES, s, strict=True))
    gx, gy, gz = (lax.axis_index(a) for a in ("gx", "gy", "gz"))
    core = gy & 1
    column = gx * 4 + (gy >> 1)
    has = [
        {-1: gx > 0, 0: True, 1: gx < GX - 1},
        {-1: gy > 0, 0: True, 1: gy < GY - 1},
        {-1: gz > 0, 0: True, 1: gz < GZ - 1},
    ]

    def there(d):
        found = [has[i][c] for i, c in enumerate(d) if c]
        return functools.reduce(jnp.logical_and, found)

    def peer(d):
        return (gx + d[0], gy + d[1], gz + (d[2] if len(d) > 2 else 0))

    def flip(d):
        return tuple(-c for c in d)

    def column_peer(k):
        other = (column + k) & 31
        return (other >> 2, ((other & 3) << 1) + core, gz)

    sibling = (gx, gy + 1 - 2 * core, gz)

    barrier = pltpu.get_barrier_semaphore()

    def greet(device):
        pl.semaphore_signal(barrier, inc=1, device_id=device, device_id_type=MESH)

    for d in DIRS:
        pl.when(there(d))(functools.partial(greet, peer(d)))

    def greet_column(k, carry):
        greet(column_peer(k))
        return carry

    lax.fori_loop(1, 32, greet_column, 0)

    def count(i):
        return 1 + has[i][-1].astype(jnp.int32) + has[i][1].astype(jnp.int32)

    lane128 = iota((16, 128), 1)
    row256 = iota((8, 256), 0)

    def pack(x, carry):
        f, e = f_in[x], e_in[x]
        s["sz"][0, x] = jnp.where(lane128 < 64, f[:, :128], roll(e[:, :128], 64, 1))
        s["sz"][1, x] = jnp.where(lane128 >= 64, f[:, 128:], roll(e[:, 128:], 64, 1))
        s["sy"][0, x] = jnp.where(row256 < 4, f[:8], roll(e[:8], 4, 0))
        s["sy"][1, x] = jnp.where(row256 >= 4, f[8:], roll(e[8:], 4, 0))
        return carry

    lax.fori_loop(0, 8, pack, 0)

    s["my0"][...] = pair_rows(4, 16, 0.5)
    s["mz0"][...] = restrict_z(256, 256, 128, 128, 1.0)

    def eps_pairs(k, carry):
        s["rs0"][pl.ds(pl.multiple_of(k * 16, 16), 16)] = e_in[2 * k] + e_in[2 * k + 1]
        return carry

    lax.fori_loop(0, 4, eps_pairs, 0)
    own_e1 = dot(dot(s["my0"][...], s["rs0"][...]), s["mz0"][...]) * 0.25
    s["e1"][4, 4:8] = own_e1.reshape(4, 8, 128)

    pl.semaphore_wait(barrier, count(0) * count(1) * count(2) - 1 + 31)

    def send(src, dst, name, index, device):
        return pltpu.make_async_remote_copy(
            src_ref=src,
            dst_ref=dst,
            send_sem=s[name + "_s"].at[index],
            recv_sem=s[name + "_r"].at[index],
            device_id=device,
            device_id_type=MESH,
        )

    def cut(dx, n, whole, base):
        if dx == 0:
            return pl.ds(0, whole), pl.ds(base, whole)
        if dx < 0:
            return pl.ds(0, n), pl.ds(base + whole, n)
        return pl.ds(whole - n, n), pl.ds(base - n, n)

    def round0(d):
        dx, dy, dz = d
        index = DIRS.index(d)
        if dy == 0 and dz == 0:
            a, b = cut(dx, 3, 8, 4)
            own = (pl.ds(0, 16), pl.ds(0, 256))
            first = send(f_in.at[a], s["f0"].at[(b, *own)], "c0", index, peer(d))
            a, b = cut(dx, 4, 8, 4)
            second = send(e_in.at[a], s["e0"].at[(b, *own)], "c0", 26 + (dx > 0), peer(d))
            return [first, second]
        if dy == 0:
            a, b = cut(dx, 3, 8, 4)
            side = int(dz > 0)
            return [send(s["sz"].at[side, a], s["rz"].at[1 - side, b], "c0", index, peer(d))]
        side = int(dy > 0)
        if dz == 0:
            a, b = cut(dx, 3, 8, 4)
            return [send(s["sy"].at[side, a], s["ry"].at[1 - side, b], "c0", index, peer(d))]
        a, b = cut(dx, 2, 8, 4)
        end = int(dz > 0)
        source = s["sy"].at[side, a, :, pl.ds(128 * end, 128)]
        return [send(source, s["ryz"].at[1 - side, 1 - end, b], "c0", index, peer(d))]

    def block1(name, wide):
        def copies(d):
            dx, dy, dz = d
            a, b = cut(dx, wide - abs(dy), 4, 4)
            own = pl.ds(4 + a.start, a.size)
            slot = (1 - dy) * 3 + 1 - dz
            buffer = s[name]
            return [send(buffer.at[4, own], buffer.at[slot, b], name, DIRS.index(d), peer(d))]

        return copies

    def flat1(d):
        dx, dy = d
        a, b = cut(dx, 4 - abs(dy), 4, 4)
        own = pl.ds(4 + a.start, a.size)
        return [send(s["v1"].at[1, own], s["v1"].at[1 - dy, b], "v1", FLAT.index(d), peer(d))]

    def start_all(dirs, copies):
        for d in dirs:

            @pl.when(there(d))
            def _(d=d):
                for copy in copies(d):
                    copy.start()

    def arrive_all(dirs, copies):
        for d in dirs:

            @pl.when(there(flip(d)))
            def _(d=d):
                for copy in copies(d):
                    copy.wait_recv()

    def leave_all(dirs, copies):
        for d in dirs:

            @pl.when(there(d))
            def _(d=d):
                for copy in copies(d):
                    copy.wait_send()

    def gather_start(name):
        mine = s[name].at[core, column]

        def one(k, carry):
            send(mine, mine, name, 0, column_peer(k)).start()
            return carry

        lax.fori_loop(1, 32, one, 0)

    def gather_many(name):
        part = s[name].at[core, pl.ds(0, 31)]
        return send(part, part, name, 0, sibling)

    def gather_pair(name):
        mine, theirs = s[name].at[core], s[name].at[1 - core]
        return send(mine, mine, name, 1, sibling), send(theirs, theirs, name, 1, sibling)

    order = sorted(DIRS, key=lambda d: (-abs(d[0]), abs(d[1]) + abs(d[2])))
    start_all(order, round0)
    start_all(order, block1("e1", 4))

    s["my1"][...] = pair_rows(2, 8, 0.5)
    s["mz1"][...] = restrict_z(128, 256, 64, 128, 1.0)
    s["my2"][...] = pair_rows(1, 32, 0.5)
    s["mz2"][...] = restrict_z(64, 128, 32, 128, 1.0)
    s["pz3"][...] = prolong_z(32, 128, 64, 128)
    s["py3"][...] = prolong_y(16, 16, 32, 32)
    s["pz2"][...] = prolong_z(64, 128, 128, 256)
    fine = place(iota((16, 32), 0), 8, 16) + 8 * gy
    s["py2"][...] = spread(iota((16, 32), 1), fine)
    s["pz1"][...] = prolong_z(128, 256, 256, 384)
    s["py1"][...] = prolong_y(8, 16, 16, 24)

    def inside(shape, own, index, total, axis):
        p = place(iota(shape, axis), own, shape[axis]) + own * index
        return (p >= 0) & (p < total)

    def x_inside(x, own, total):
        p = x + own * gx
        return (p >= 0) & (p < total)

    def mask(shape, own_y, own_z, total_y, total_z):
        return inside(shape, own_y, gy, total_y, 0) & inside(shape, own_z, gz, total_z, 1)

    def both(a, flag):
        return jnp.logical_and(a, jnp.broadcast_to(flag, a.shape))

    def beside(v, cx_low, cx, cy, cz, low, high):
        total = cx_low * low + cx * high
        total = total + cy * roll(v, -1, 0) + roll(cy * v, 1, 0)
        return total + cz * roll(v, -1, 1) + roll(cz * v, 1, 1)

    arrive_all(order, round0)
    m0 = mask((24, 384), 16, 256, NY, NZ)
    ones0 = jnp.ones((24, 384), F32)
    low_lane = iota((16, 128), 1) < 64
    low_lane8 = iota((8, 128), 1) < 64
    low_row = iota((8, 256), 0) < 4
    low_row8 = iota((8, 128), 0) < 4

    def fill(x, wide_f, yz):
        m = both(m0, x_inside(x - 4, 8, NX))
        if isinstance(x, int) and (x == 0 or x == 15):
            e = jnp.concatenate([s["e0"][x, :16, :256], jnp.ones((16, 128), F32)], 1)
            e = jnp.concatenate([e, jnp.ones((8, 384), F32)], 0)
            s["e0"][x] = 1.0 / jnp.where(m, e, 1.0)
            return
        z0, z1 = s["rz"][0, x], s["rz"][1, x]
        y0, y1 = s["ry"][0, x], s["ry"][1, x]
        f_z = jnp.where(low_lane, z1, z0)
        e_z = roll(jnp.where(low_lane, z0, z1), 64, 1)
        f_y = jnp.where(low_row, y1, y0)
        e_y = roll(jnp.where(low_row, y0, y1), 4, 0)
        if yz:
            c0 = jnp.where(low_lane8, s["ryz"][0, 1, x], s["ryz"][0, 0, x])
            c1 = jnp.where(low_lane8, s["ryz"][1, 1, x], s["ryz"][1, 0, x])
            f_c = jnp.where(low_row8, c1, c0)
            e_c = roll(jnp.where(low_row8, c0, c1), 4, 0)
        else:
            f_c = jnp.zeros((8, 128), F32)
            e_c = jnp.ones((8, 128), F32)
        if isinstance(x, int):
            f_own, e_own = s["f0"][x, :16, :256], s["e0"][x, :16, :256]
        else:
            f_own, e_own = f_in[x - 4], e_in[x - 4]

        def join(own, z, y, c):
            top = jnp.concatenate([own, z], 1)
            return jnp.concatenate([top, jnp.concatenate([y, c], 1)], 0)

        f = join(f_own, f_z, f_y, f_c)
        e = join(e_own, e_z, e_y, e_c)
        s["f0"][x] = jnp.where(m, f, 0.0) * FOURPI
        s["e0"][x] = 1.0 / jnp.where(m, e, 1.0)

    for x in (0, 1, 2, 3, 12, 13, 14, 15):
        fill(x, True, 2 <= x <= 13)

    def fill_own(x, carry):
        fill(x, True, True)
        return carry

    lax.fori_loop(4, 12, fill_own, 0)

    def coefficients(ie, x, m, ic, cx_low):
        inext = ie[x + 1]
        cx = 2.0 / (ic + inext)
        cy = 2.0 / (ic + roll(ic, -1, 0))
        cz = 2.0 / (ic + roll(ic, -1, 1))
        diagonal = cx + cx_low + cy + roll(cy, 1, 0) + cz + roll(cz, 1, 1)
        weight = jnp.where(m, OMEGA / diagonal, 0.0)
        return inext, cx, cy, cz, diagonal, weight

    ic = s["e0"][1]
    s["cx0"][0] = 2.0 / (s["e0"][0] + ic)

    def make0(x, carry):
        ic, cx_low = carry
        m = both(m0, x_inside(x - 4, 8, NX))
        ic, cx, cy, cz, diagonal, weight = coefficients(s["e0"], x, m, ic, cx_low)
        s["cx0"][x], s["cy0"][x], s["cz0"][x] = cx, cy, cz
        s["d0"][x], s["w0"][x] = diagonal, weight
        s["a0"][x] = weight * s["f0"][x]
        return ic, cx

    lax.fori_loop(1, 15, make0, (ic, s["cx0"][0]))

    def total(level, src, x):
        c = str(level)
        v = s[src][x]
        return v, s["f" + c][x] + beside(
            v, s["cx" + c][x - 1], s["cx" + c][x], s["cy" + c][x], s["cz" + c][x],
            s[src][x - 1], s[src][x + 1],
        )

    def sweeps(level, src, dst, start, stop):
        def one(x, carry):
            v, u = total(level, src, x)
            s[dst][x] = KEEP * v + s[f"w{level}"][x] * u
            return carry

        lax.fori_loop(start, stop, one, 0)

    def residue(level, src, x):
        v, u = total(level, src, x)
        return u - s[f"d{level}"][x] * v

    sweeps(0, "a0", "b0", 2, 14)

    def pairs0(k, carry):
        r = residue(0, "b0", 4 + 2 * k) + residue(0, "b0", 5 + 2 * k)
        s["rs0"][pl.ds(pl.multiple_of(k * 16, 16), 16)] = r[:16, :256]
        return carry

    lax.fori_loop(0, 4, pairs0, 0)
    own_f1 = dot(dot(s["my0"][...], s["rs0"][...]), s["mz0"][...])
    s["f1b"][4, 4:8] = own_f1.reshape(4, 8, 128)
    start_all(order, block1("f1b", 3))

    m1 = mask((16, 256), 8, 128, NY // 2, NZ // 2)

    def join1(name, x, other, yhalo):
        b = s[name]

        def across(y):
            low = jnp.where(low_lane8, b[y * 3 + 2, x], b[y * 3 + 0, x])
            return jnp.concatenate([b[y * 3 + 1, x], low], 1)

        top = across(1)
        if yhalo:
            under = jnp.where(low_row, across(2), across(0))
        else:
            under = jnp.full((8, 256), other, F32)
        both_rows = jnp.concatenate([top, under], 0)
        return jnp.where(both(m1, x_inside(x - 4, 4, NX // 2)), both_rows, other)

    arrive_all(order, block1("e1", 4))
    for x in range(12):
        e = join1("e1", x, 1.0, 1 <= x <= 10)
        s["ie1"][x] = 1.0 / e
        if 4 <= x < 8:
            half = (x - 4) // 2 * 8
            if x % 2 == 0:
                s["rs1"][half : half + 8] = e[:8]
            else:
                s["rs1"][half : half + 8] += e[:8]
    s["ge"][core, column] = dot(dot(s["my1"][...], s["rs1"][...]), s["mz1"][...]) * 0.25
    gather_start("ge")

    s["cx1"][0] = 2.0 / (s["ie1"][0] + s["ie1"][1])

    def make1(x, carry):
        ic, cx_low = carry
        m = both(m1, x_inside(x - 4, 4, NX // 2))
        ic, cx, cy, cz, diagonal, weight = coefficients(s["ie1"], x, m, ic, cx_low)
        s["cx1"][x], s["cy1"][x], s["cz1"][x] = cx, cy, cz
        s["d1"][x], s["w1"][x] = diagonal, weight
        return ic, cx

    lax.fori_loop(1, 11, make1, (s["ie1"][1], s["cx1"][0]))

    arrive_all(order, block1("f1b", 3))
    for x in range(1, 11):
        f = join1("f1b", x, 0.0, 2 <= x <= 9)
        s["f1"][x] = f
        s["a1"][x] = s["w1"][x] * f
    sweeps(1, "a1", "b1", 3, 9)
    for k in range(2):
        r = residue(1, "b1", 4 + 2 * k) + residue(1, "b1", 5 + 2 * k)
        s["rs1"][8 * k : 8 * k + 8] = r[:8]
    s["gf"][core, column] = dot(dot(s["my1"][...], s["rs1"][...]), s["mz1"][...])
    gather_start("gf")
    for x in range(4, 8):
        s["v1"][1, x] = s["b1"][x, :8]
    start_all(FLAT, flat1)

    row8 = iota((8, 128), 0) < 4

    def arrange(name, write):
        def one(k, carry):
            even, odd = s[name][0, k], s[name][1, k]
            x = 2 * (k >> 2)
            rows = pl.ds(pl.multiple_of((k & 3) * 8, 8), 8)
            write(x + 4, rows, jnp.where(row8, even, roll(odd, 4, 0)))
            write(x + 5, rows, jnp.where(row8, roll(even, 4, 0), odd))
            return carry

        lax.fori_loop(0, 32, one, 0)

    def collect(name):
        gather_many(name).wait_recv()
        mine, theirs = gather_pair(name)
        mine.start()
        theirs.wait_recv()

    collect("ge")

    def put_e2(x, rows, values):
        s["e2"][x, rows] = values
        s["ie2"][x, rows] = 1.0 / values

    arrange("ge", put_e2)
    shape2 = (32, 128)
    last2, first2 = iota(shape2, 0) == 31, iota(shape2, 0) == 0
    in_z2 = inside(shape2, 64, gz, NZ // 4, 1)
    s["ie2"][3] = jnp.ones(shape2, F32)
    s["ie2"][20] = jnp.ones(shape2, F32)

    def edge_faces(ic, first, last):
        cy = 2.0 / (ic + jnp.where(last, 1.0, roll(ic, -1, 0)))
        below = jnp.where(first, 2.0 / (ic + 1.0), roll(cy, 1, 0))
        return cy, below

    s["cx2"][3] = 2.0 / (1.0 + s["ie2"][4])

    def make2(x, carry):
        ic, cx_low = carry
        inext = s["ie2"][x + 1]
        cx = 2.0 / (ic + inext)
        cy, below = edge_faces(ic, first2, last2)
        cz = 2.0 / (ic + roll(ic, -1, 1))
        diagonal = cx + cx_low + cy + below + cz + roll(cz, 1, 1)
        s["cx2"][x], s["cz2"][x] = cx, cz
        s["cy2"][x] = jnp.where(last2, 0.0, cy)
        s["d2"][x] = diagonal
        s["w2"][x] = jnp.where(in_z2, OMEGA / diagonal, 0.0)
        return inext, cx

    lax.fori_loop(4, 20, make2, (s["ie2"][4], s["cx2"][3]))
    for x in range(4):
        for name in ("a2", "b2"):
            s[name][x] = jnp.zeros(shape2, F32)
            s[name][20 + x] = jnp.zeros(shape2, F32)

    def down3(pair):
        def one(k, carry):
            rows = pl.ds(pl.multiple_of(k * 16, 16), 16)
            s["rs3"][rows] = dot(s["my2"][...], pair(k))
            return carry

        lax.fori_loop(0, 8, one, 0)
        return dot(s["rs3"][...], s["mz2"][...]).reshape(8, 16, 128)

    shape3 = (8, 16, 128)
    p3 = place(iota(shape3, 2), 32, 128)
    near3 = (p3 >= -16) & (p3 < 48)
    e3 = down3(lambda k: s["e2"][4 + 2 * k] + s["e2"][5 + 2 * k]) * 0.25
    ie3 = 1.0 / jnp.where(near3, e3, 1.0)
    first3, last3 = iota(shape3, 1) == 0, iota(shape3, 1) == 15
    edge = jnp.ones((1, 16, 128), F32)
    none = jnp.zeros((1, 16, 128), F32)

    def roll3(values, shift, axis):
        return roll(values.reshape(128, 128), shift, 1).reshape(shape3) if axis == 2 else jnp.stack(
            [roll(values[k], shift, 0) for k in range(8)]
        )

    around = jnp.concatenate([edge, ie3, edge], 0)
    cx3 = 2.0 / (around[1:] + around[:-1])
    cy3 = 2.0 / (ie3 + jnp.where(last3, 1.0, roll3(ie3, -1, 1)))
    below3 = jnp.where(first3, 2.0 / (ie3 + 1.0), roll3(cy3, 1, 1))
    cz3 = 2.0 / (ie3 + roll3(ie3, -1, 2))
    d3 = cx3[1:] + cx3[:-1] + cy3 + below3 + cz3 + roll3(cz3, 1, 2)
    q3 = p3 + 32 * gz
    s["w3"][...] = jnp.where((q3 >= 0) & (q3 < NZ // 8), OMEGA / d3, 0.0)
    s["cx3"][...] = cx3
    s["cy3"][...] = jnp.where(last3, 0.0, cy3)
    s["cz3"][...] = cz3

    collect("gf")

    def put_f2(x, rows, values):
        s["f2"][x, rows] = values
        s["a2"][x, rows] = s["w2"][x, rows] * values

    arrange("gf", put_f2)
    sweeps(2, "a2", "b2", 4, 20)
    f3 = down3(lambda k: residue(2, "b2", 4 + 2 * k) + residue(2, "b2", 5 + 2 * k))
    s["f3"][...] = f3

    def coarse(_, v):
        cx, cy, cz = s["cx3"][...], s["cy3"][...], s["cz3"][...]
        after = jnp.concatenate([v[1:], none], 0)
        before = jnp.concatenate([none, v[:-1]], 0)
        u = s["f3"][...] + cx[1:] * after + cx[:-1] * before
        u = u + cy * roll3(v, -1, 1) + roll3(cy * v, 1, 1)
        u = u + cz * roll3(v, -1, 2) + roll3(cz * v, 1, 2)
        return KEEP * v + s["w3"][...] * u

    v3 = lax.fori_loop(0, COARSE_SWEEPS - 1, coarse, s["w3"][...] * f3)

    wide = dot(v3.reshape(128, 128), s["pz3"][...]).reshape(8, 16, 128)
    rows3 = [dot(s["py3"][...], wide[k]) for k in range(8)]
    nothing = jnp.zeros(shape2, F32)
    for k in range(8):
        low = rows3[k - 1] if k else nothing
        high = rows3[k + 1] if k < 7 else nothing
        for i, other in ((0, low), (1, high)):
            x = 4 + 2 * k + i
            add = 0.75 * rows3[k] + 0.25 * other
            s["b2"][x] += jnp.where(in_z2, add, 0.0)
    sweeps(2, "b2", "a2", 4, 20)
    sweeps(2, "a2", "b2", 4, 20)

    for k in range(8):
        s["up1"][16 * k : 16 * k + 16] = dot(s["py2"][...], s["b2"][2 * gx + 1 + k])
    up1 = dot(s["up1"][...], s["pz2"][...])
    arrive_all(FLAT, flat1)
    up1 = up1.reshape(8, 16, 256)
    for x in range(12):
        k = (x - 4) // 2 + 3
        other = up1[k - 1] if x % 2 == 0 else up1[k + 1]
        add = 0.75 * up1[k] + 0.25 * other
        under = jnp.zeros((8, 256), F32)
        if 1 <= x <= 10:
            under = jnp.where(low_row, s["v1"][2, x], s["v1"][0, x])
        v = jnp.concatenate([s["v1"][1, x], under], 0) + add
        s["a1"][x] = jnp.where(both(m1, x_inside(x - 4, 4, NX // 2)), v, 0.0)
    sweeps(1, "a1", "b1", 1, 11)
    sweeps(1, "b1", "a1", 2, 10)

    for k in range(8):
        s["up0"][24 * k : 24 * k + 24] = dot(s["py1"][...], s["a1"][2 + k])
    up0 = dot(s["up0"][...], s["pz1"][...]).reshape(8, 24, 384)
    for x in range(2, 14):
        k = (x - 4) // 2 + 2
        other = up0[k - 1] if x % 2 == 0 else up0[k + 1]
        add = 0.75 * up0[k] + 0.25 * other
        s["b0"][x] += jnp.where(both(m0, x_inside(x - 4, 8, NX)), add, 0.0)
    sweeps(0, "b0", "a0", 3, 13)

    def finish(x, carry):
        v, u = total(0, "a0", x)
        out[x - 4] = (KEEP * v + s["w0"][x] * u)[:16, :256]
        return carry

    lax.fori_loop(4, 12, finish, 0)

    leave_all(order, round0)
    leave_all(order, block1("e1", 4))
    leave_all(order, block1("f1b", 3))
    leave_all(FLAT, flat1)
    for name in ("ge", "gf"):
        gather_many(name).wait_send()
        gather_pair(name)[0].wait_send()


def buffers():
    def vmem(*shape):
        return pltpu.VMEM(shape, F32)

    table = {
        "sz": vmem(2, 8, 16, 128), "rz": vmem(2, 16, 16, 128),
        "sy": vmem(2, 8, 8, 256), "ry": vmem(2, 16, 8, 256),
        "ryz": vmem(2, 2, 16, 8, 128),
        "e1": vmem(9, 12, 8, 128), "f1b": vmem(9, 12, 8, 128), "v1": vmem(3, 12, 8, 256),
        "ge": vmem(2, 32, 8, 128), "gf": vmem(2, 32, 8, 128),
        "my0": vmem(32, 64), "mz0": vmem(256, 128), "my1": vmem(8, 16), "mz1": vmem(256, 128),
        "my2": vmem(16, 32), "mz2": vmem(128, 128), "pz3": vmem(128, 128), "py3": vmem(32, 16),
        "pz2": vmem(128, 256), "py2": vmem(16, 32), "pz1": vmem(256, 384), "py1": vmem(24, 16),
        "rs0": vmem(64, 256), "rs1": vmem(16, 256), "rs3": vmem(128, 128),
        "up1": vmem(128, 128), "up0": vmem(192, 256),
        "ie1": vmem(12, 16, 256), "e2": vmem(24, 32, 128), "ie2": vmem(24, 32, 128),
        "f3": vmem(8, 16, 128), "w3": vmem(8, 16, 128), "cx3": vmem(9, 16, 128),
        "cy3": vmem(8, 16, 128), "cz3": vmem(8, 16, 128),
    }
    shapes = {"0": (16, 24, 384), "1": (12, 16, 256), "2": (24, 32, 128)}
    for level, shape in shapes.items():
        for name in ("f", "cx", "cy", "cz", "d", "w", "a", "b"):
            table[name + level] = vmem(*shape)
    table["e0"] = vmem(16, 24, 384)
    for name, number in (("c0", 28), ("e1", 26), ("f1b", 26), ("v1", 8), ("ge", 2), ("gf", 2)):
        table[name + "_s"] = pltpu.SemaphoreType.DMA((number,))
        table[name + "_r"] = pltpu.SemaphoreType.DMA((number,))
    return table


NAMES = list(buffers())


def on_device(charge, dielectric):
    return pl.pallas_call(
        lambda f, e, o, *s: kernel(f, e, o, s),
        out_shape=jax.ShapeDtypeStruct((8, 16, 256), F32),
        in_specs=[pl.BlockSpec(memory_space=pltpu.VMEM)] * 2,
        out_specs=pl.BlockSpec(memory_space=pltpu.VMEM),
        scratch_shapes=list(buffers().values()),
        compiler_params=pltpu.CompilerParams(
            collective_id=0, has_side_effects=True, vmem_limit_bytes=40 * 2**20
        ),
    )(charge, dielectric)


def solution(mesh):
    placed = (P("gx", "gy", "gz"), P("gx", "gy", "gz"))
    return jax.shard_map(
        on_device, mesh=mesh, in_specs=placed, out_specs=P("gx", "gy", "gz"), check_vma=False
    )
```

```python
import functools
import itertools
import math

import jax
import jax.numpy as jnp
from jax import lax
from jax.experimental import pallas as pl
from jax.experimental.pallas import tpu as pltpu
from jax.sharding import PartitionSpec as P

MESH = pl.DeviceIdType.MESH
F32 = jnp.float32
OMEGA = 0.8
KEEP = 1.0 - OMEGA
FOURPI = 4.0 * math.pi
COARSE_SWEEPS = 8
NX, NY, NZ = 64, 128, 1024
GX, GY, GZ = 8, 8, 4
DIRS = [d for d in itertools.product((-1, 0, 1), repeat=3) if d != (0, 0, 0)]
FLAT = [d for d in itertools.product((-1, 0, 1), repeat=2) if d != (0, 0)]


def loop(start, stop, body, init):
    return lax.fori_loop(start, stop, body, init, unroll=True)


def roll(values, shift, axis):
    return pltpu.roll(values, shift % values.shape[axis], axis)


def dot(a, b):
    return jnp.dot(a, b, preferred_element_type=F32, precision=lax.Precision.HIGHEST)


def place(index, own, size):
    half = (size - own) // 2
    return jnp.where(index < own + half, index, index - size)


def iota(shape, axis):
    return lax.broadcasted_iota(jnp.int32, shape, axis)


def restrict_z(own, size, out_own, out_size, weight):
    shape = (size, out_size)
    p = place(iota(shape, 0), own, size)
    q = place(iota(shape, 1), out_own, out_size)
    return jnp.where((p >> 1) == q, weight, 0.0).astype(F32)


def pair_rows(groups, own, weight):
    shape = (groups * own // 2, groups * own)
    return jnp.where((iota(shape, 1) >> 1) == iota(shape, 0), weight, 0.0).astype(F32)


def spread(q, p):
    parent = p >> 1
    other = jnp.where((p & 1) == 0, parent - 1, parent + 1)
    return jnp.where(q == parent, 0.75, jnp.where(q == other, 0.25, 0.0)).astype(F32)


def prolong_z(own, size, out_own, out_size):
    shape = (size, out_size)
    return spread(place(iota(shape, 0), own, size), place(iota(shape, 1), out_own, out_size))


def prolong_y(own, size, out_own, out_size):
    shape = (out_size, size)
    return spread(place(iota(shape, 1), own, size), place(iota(shape, 0), out_own, out_size))


def kernel(f_in, e_in, out, s):
    s = dict(zip(NAMES, s, strict=True))
    gx, gy, gz = (lax.axis_index(a) for a in ("gx", "gy", "gz"))
    core = gy & 1
    column = gx * 4 + (gy >> 1)
    has = [
        {-1: gx > 0, 0: True, 1: gx < GX - 1},
        {-1: gy > 0, 0: True, 1: gy < GY - 1},
        {-1: gz > 0, 0: True, 1: gz < GZ - 1},
    ]

    def there(d):
        found = [has[i][c] for i, c in enumerate(d) if c]
        return functools.reduce(jnp.logical_and, found)

    def peer(d):
        return (gx + d[0], gy + d[1], gz + (d[2] if len(d) > 2 else 0))

    def flip(d):
        return tuple(-c for c in d)

    def column_peer(k):
        other = (column + k) & 31
        return (other >> 2, ((other & 3) << 1) + core, gz)

    sibling = (gx, gy + 1 - 2 * core, gz)

    barrier = pltpu.get_barrier_semaphore()

    def greet(device):
        pl.semaphore_signal(barrier, inc=1, device_id=device, device_id_type=MESH)

    for d in DIRS:
        pl.when(there(d))(functools.partial(greet, peer(d)))

    def greet_column(k, carry):
        greet(column_peer(k))
        return carry

    loop(1, 32, greet_column, 0)

    def count(i):
        return 1 + has[i][-1].astype(jnp.int32) + has[i][1].astype(jnp.int32)

    lane128 = iota((16, 128), 1)
    row256 = iota((8, 256), 0)

    def pack(x, carry):
        f, e = f_in[x], e_in[x]
        s["sz"][0, x] = jnp.where(lane128 < 64, f[:, :128], roll(e[:, :128], 64, 1))
        s["sz"][1, x] = jnp.where(lane128 >= 64, f[:, 128:], roll(e[:, 128:], 64, 1))
        s["sy"][0, x] = jnp.where(row256 < 4, f[:8], roll(e[:8], 4, 0))
        s["sy"][1, x] = jnp.where(row256 >= 4, f[8:], roll(e[8:], 4, 0))
        return carry

    loop(0, 8, pack, 0)

    s["my0"][...] = pair_rows(4, 16, 0.5)
    s["mz0"][...] = restrict_z(256, 256, 128, 128, 1.0)

    def eps_pairs(k, carry):
        s["rs0"][pl.ds(pl.multiple_of(k * 16, 16), 16)] = e_in[2 * k] + e_in[2 * k + 1]
        return carry

    loop(0, 4, eps_pairs, 0)
    own_e1 = dot(dot(s["my0"][...], s["rs0"][...]), s["mz0"][...]) * 0.25
    s["e1"][4, 4:8] = own_e1.reshape(4, 8, 128)

    pl.semaphore_wait(barrier, count(0) * count(1) * count(2) - 1 + 31)

    def send(src, dst, name, index, device):
        return pltpu.make_async_remote_copy(
            src_ref=src,
            dst_ref=dst,
            send_sem=s[name + "_s"].at[index],
            recv_sem=s[name + "_r"].at[index],
            device_id=device,
            device_id_type=MESH,
        )

    def cut(dx, n, whole, base):
        if dx == 0:
            return pl.ds(0, whole), pl.ds(base, whole)
        if dx < 0:
            return pl.ds(0, n), pl.ds(base + whole, n)
        return pl.ds(whole - n, n), pl.ds(base - n, n)

    def round0(d):
        dx, dy, dz = d
        index = DIRS.index(d)
        if dy == 0 and dz == 0:
            a, b = cut(dx, 3, 8, 4)
            own = (pl.ds(0, 16), pl.ds(0, 256))
            first = send(f_in.at[a], s["f0"].at[(b, *own)], "c0", index, peer(d))
            a, b = cut(dx, 4, 8, 4)
            second = send(e_in.at[a], s["e0"].at[(b, *own)], "c0", 26 + (dx > 0), peer(d))
            return [first, second]
        if dy == 0:
            a, b = cut(dx, 3, 8, 4)
            side = int(dz > 0)
            return [send(s["sz"].at[side, a], s["rz"].at[1 - side, b], "c0", index, peer(d))]
        side = int(dy > 0)
        if dz == 0:
            a, b = cut(dx, 3, 8, 4)
            return [send(s["sy"].at[side, a], s["ry"].at[1 - side, b], "c0", index, peer(d))]
        a, b = cut(dx, 2, 8, 4)
        end = int(dz > 0)
        source = s["sy"].at[side, a, :, pl.ds(128 * end, 128)]
        return [send(source, s["ryz"].at[1 - side, 1 - end, b], "c0", index, peer(d))]

    def block1(name, wide):
        def copies(d):
            dx, dy, dz = d
            a, b = cut(dx, wide - abs(dy), 4, 4)
            own = pl.ds(4 + a.start, a.size)
            slot = (1 - dy) * 3 + 1 - dz
            buffer = s[name]
            return [send(buffer.at[4, own], buffer.at[slot, b], name, DIRS.index(d), peer(d))]

        return copies

    def flat1(d):
        dx, dy = d
        a, b = cut(dx, 4 - abs(dy), 4, 4)
        own = pl.ds(4 + a.start, a.size)
        return [send(s["v1"].at[1, own], s["v1"].at[1 - dy, b], "v1", FLAT.index(d), peer(d))]

    def start_all(dirs, copies):
        for d in dirs:

            @pl.when(there(d))
            def _(d=d):
                for copy in copies(d):
                    copy.start()

    def arrive_all(dirs, copies):
        for d in dirs:

            @pl.when(there(flip(d)))
            def _(d=d):
                for copy in copies(d):
                    copy.wait_recv()

    def leave_all(dirs, copies):
        for d in dirs:

            @pl.when(there(d))
            def _(d=d):
                for copy in copies(d):
                    copy.wait_send()

    def gather_start(name):
        mine = s[name].at[core, column]

        def one(k, carry):
            send(mine, mine, name, 0, column_peer(k)).start()
            return carry

        loop(1, 32, one, 0)

    def gather_many(name):
        part = s[name].at[core, pl.ds(0, 31)]
        return send(part, part, name, 0, sibling)

    def gather_pair(name):
        mine, theirs = s[name].at[core], s[name].at[1 - core]
        return send(mine, mine, name, 1, sibling), send(theirs, theirs, name, 1, sibling)

    order = sorted(DIRS, key=lambda d: (-abs(d[0]), abs(d[1]) + abs(d[2])))
    start_all(order, round0)
    start_all(order, block1("e1", 4))

    s["my1"][...] = pair_rows(2, 8, 0.5)
    s["mz1"][...] = restrict_z(128, 256, 64, 128, 1.0)
    s["my2"][...] = pair_rows(1, 32, 0.5)
    s["mz2"][...] = restrict_z(64, 128, 32, 128, 1.0)
    s["pz3"][...] = prolong_z(32, 128, 64, 128)
    s["py3"][...] = prolong_y(16, 16, 32, 32)
    s["pz2"][...] = prolong_z(64, 128, 128, 256)
    fine = place(iota((16, 32), 0), 8, 16) + 8 * gy
    s["py2"][...] = spread(iota((16, 32), 1), fine)
    s["pz1"][...] = prolong_z(128, 256, 256, 384)
    s["py1"][...] = prolong_y(8, 16, 16, 24)

    def inside(shape, own, index, total, axis):
        p = place(iota(shape, axis), own, shape[axis]) + own * index
        return (p >= 0) & (p < total)

    def x_inside(x, own, total):
        p = x + own * gx
        return (p >= 0) & (p < total)

    def mask(shape, own_y, own_z, total_y, total_z):
        return inside(shape, own_y, gy, total_y, 0) & inside(shape, own_z, gz, total_z, 1)

    def both(a, flag):
        return jnp.logical_and(a, jnp.broadcast_to(flag, a.shape))

    def beside(v, cx_low, cx, cy, cz, low, high):
        total = cx_low * low + cx * high
        total = total + cy * roll(v, -1, 0) + roll(cy * v, 1, 0)
        return total + cz * roll(v, -1, 1) + roll(cz * v, 1, 1)

    arrive_all(order, round0)
    m0 = mask((24, 384), 16, 256, NY, NZ)
    ones0 = jnp.ones((24, 384), F32)
    low_lane = iota((16, 128), 1) < 64
    low_lane8 = iota((8, 128), 1) < 64
    low_row = iota((8, 256), 0) < 4
    low_row8 = iota((8, 128), 0) < 4

    def fill(x, wide_f, yz):
        m = both(m0, x_inside(x - 4, 8, NX))
        if isinstance(x, int) and (x == 0 or x == 15):
            e = jnp.concatenate([s["e0"][x, :16, :256], jnp.ones((16, 128), F32)], 1)
            e = jnp.concatenate([e, jnp.ones((8, 384), F32)], 0)
            s["e0"][x] = 1.0 / jnp.where(m, e, 1.0)
            return
        z0, z1 = s["rz"][0, x], s["rz"][1, x]
        y0, y1 = s["ry"][0, x], s["ry"][1, x]
        f_z = jnp.where(low_lane, z1, z0)
        e_z = roll(jnp.where(low_lane, z0, z1), 64, 1)
        f_y = jnp.where(low_row, y1, y0)
        e_y = roll(jnp.where(low_row, y0, y1), 4, 0)
        if yz:
            c0 = jnp.where(low_lane8, s["ryz"][0, 1, x], s["ryz"][0, 0, x])
            c1 = jnp.where(low_lane8, s["ryz"][1, 1, x], s["ryz"][1, 0, x])
            f_c = jnp.where(low_row8, c1, c0)
            e_c = roll(jnp.where(low_row8, c0, c1), 4, 0)
        else:
            f_c = jnp.zeros((8, 128), F32)
            e_c = jnp.ones((8, 128), F32)
        if isinstance(x, int):
            f_own, e_own = s["f0"][x, :16, :256], s["e0"][x, :16, :256]
        else:
            f_own, e_own = f_in[x - 4], e_in[x - 4]

        def join(own, z, y, c):
            top = jnp.concatenate([own, z], 1)
            return jnp.concatenate([top, jnp.concatenate([y, c], 1)], 0)

        f = join(f_own, f_z, f_y, f_c)
        e = join(e_own, e_z, e_y, e_c)
        s["f0"][x] = jnp.where(m, f, 0.0) * FOURPI
        s["e0"][x] = 1.0 / jnp.where(m, e, 1.0)

    for x in (0, 1, 2, 3, 12, 13, 14, 15):
        fill(x, True, 2 <= x <= 13)

    def fill_own(x, carry):
        fill(x, True, True)
        return carry

    loop(4, 12, fill_own, 0)

    def coefficients(ie, x, m, ic, cx_low):
        inext = ie[x + 1]
        cx = 2.0 / (ic + inext)
        cy = 2.0 / (ic + roll(ic, -1, 0))
        cz = 2.0 / (ic + roll(ic, -1, 1))
        diagonal = cx + cx_low + cy + roll(cy, 1, 0) + cz + roll(cz, 1, 1)
        weight = jnp.where(m, OMEGA / diagonal, 0.0)
        return inext, cx, cy, cz, diagonal, weight

    ic = s["e0"][1]
    s["cx0"][0] = 2.0 / (s["e0"][0] + ic)

    def make0(x, carry):
        ic, cx_low = carry
        m = both(m0, x_inside(x - 4, 8, NX))
        ic, cx, cy, cz, diagonal, weight = coefficients(s["e0"], x, m, ic, cx_low)
        s["cx0"][x], s["cy0"][x], s["cz0"][x] = cx, cy, cz
        s["d0"][x], s["w0"][x] = diagonal, weight
        s["a0"][x] = weight * s["f0"][x]
        return ic, cx

    loop(1, 15, make0, (ic, s["cx0"][0]))

    def total(level, src, x):
        c = str(level)
        v = s[src][x]
        return v, s["f" + c][x] + beside(
            v, s["cx" + c][x - 1], s["cx" + c][x], s["cy" + c][x], s["cz" + c][x],
            s[src][x - 1], s[src][x + 1],
        )

    def sweeps(level, src, dst, start, stop):
        def one(x, carry):
            v, u = total(level, src, x)
            s[dst][x] = KEEP * v + s[f"w{level}"][x] * u
            return carry

        loop(start, stop, one, 0)

    def residue(level, src, x):
        v, u = total(level, src, x)
        return u - s[f"d{level}"][x] * v

    sweeps(0, "a0", "b0", 2, 14)

    def pairs0(k, carry):
        r = residue(0, "b0", 4 + 2 * k) + residue(0, "b0", 5 + 2 * k)
        s["rs0"][pl.ds(pl.multiple_of(k * 16, 16), 16)] = r[:16, :256]
        return carry

    loop(0, 4, pairs0, 0)
    own_f1 = dot(dot(s["my0"][...], s["rs0"][...]), s["mz0"][...])
    s["f1b"][4, 4:8] = own_f1.reshape(4, 8, 128)
    start_all(order, block1("f1b", 3))

    m1 = mask((16, 256), 8, 128, NY // 2, NZ // 2)

    def join1(name, x, other, yhalo):
        b = s[name]

        def across(y):
            low = jnp.where(low_lane8, b[y * 3 + 2, x], b[y * 3 + 0, x])
            return jnp.concatenate([b[y * 3 + 1, x], low], 1)

        top = across(1)
        if yhalo:
            under = jnp.where(low_row, across(2), across(0))
        else:
            under = jnp.full((8, 256), other, F32)
        both_rows = jnp.concatenate([top, under], 0)
        return jnp.where(both(m1, x_inside(x - 4, 4, NX // 2)), both_rows, other)

    arrive_all(order, block1("e1", 4))
    for x in range(12):
        e = join1("e1", x, 1.0, 1 <= x <= 10)
        s["ie1"][x] = 1.0 / e
        if 4 <= x < 8:
            half = (x - 4) // 2 * 8
            if x % 2 == 0:
                s["rs1"][half : half + 8] = e[:8]
            else:
                s["rs1"][half : half + 8] += e[:8]
    s["ge"][core, column] = dot(dot(s["my1"][...], s["rs1"][...]), s["mz1"][...]) * 0.25
    gather_start("ge")

    s["cx1"][0] = 2.0 / (s["ie1"][0] + s["ie1"][1])

    def make1(x, carry):
        ic, cx_low = carry
        m = both(m1, x_inside(x - 4, 4, NX // 2))
        ic, cx, cy, cz, diagonal, weight = coefficients(s["ie1"], x, m, ic, cx_low)
        s["cx1"][x], s["cy1"][x], s["cz1"][x] = cx, cy, cz
        s["d1"][x], s["w1"][x] = diagonal, weight
        return ic, cx

    loop(1, 11, make1, (s["ie1"][1], s["cx1"][0]))

    arrive_all(order, block1("f1b", 3))
    for x in range(1, 11):
        f = join1("f1b", x, 0.0, 2 <= x <= 9)
        s["f1"][x] = f
        s["a1"][x] = s["w1"][x] * f
    sweeps(1, "a1", "b1", 3, 9)
    for k in range(2):
        r = residue(1, "b1", 4 + 2 * k) + residue(1, "b1", 5 + 2 * k)
        s["rs1"][8 * k : 8 * k + 8] = r[:8]
    s["gf"][core, column] = dot(dot(s["my1"][...], s["rs1"][...]), s["mz1"][...])
    gather_start("gf")
    for x in range(4, 8):
        s["v1"][1, x] = s["b1"][x, :8]
    start_all(FLAT, flat1)

    row8 = iota((8, 128), 0) < 4

    def arrange(name, write):
        def one(k, carry):
            even, odd = s[name][0, k], s[name][1, k]
            x = 2 * (k >> 2)
            rows = pl.ds(pl.multiple_of((k & 3) * 8, 8), 8)
            write(x + 4, rows, jnp.where(row8, even, roll(odd, 4, 0)))
            write(x + 5, rows, jnp.where(row8, roll(even, 4, 0), odd))
            return carry

        loop(0, 32, one, 0)

    def collect(name):
        gather_many(name).wait_recv()
        mine, theirs = gather_pair(name)
        mine.start()
        theirs.wait_recv()

    collect("ge")

    def put_e2(x, rows, values):
        s["e2"][x, rows] = values
        s["ie2"][x, rows] = 1.0 / values

    arrange("ge", put_e2)
    shape2 = (32, 128)
    last2, first2 = iota(shape2, 0) == 31, iota(shape2, 0) == 0
    in_z2 = inside(shape2, 64, gz, NZ // 4, 1)
    s["ie2"][3] = jnp.ones(shape2, F32)
    s["ie2"][20] = jnp.ones(shape2, F32)

    def edge_faces(ic, first, last):
        cy = 2.0 / (ic + jnp.where(last, 1.0, roll(ic, -1, 0)))
        below = jnp.where(first, 2.0 / (ic + 1.0), roll(cy, 1, 0))
        return cy, below

    s["cx2"][3] = 2.0 / (1.0 + s["ie2"][4])

    def make2(x, carry):
        ic, cx_low = carry
        inext = s["ie2"][x + 1]
        cx = 2.0 / (ic + inext)
        cy, below = edge_faces(ic, first2, last2)
        cz = 2.0 / (ic + roll(ic, -1, 1))
        diagonal = cx + cx_low + cy + below + cz + roll(cz, 1, 1)
        s["cx2"][x], s["cz2"][x] = cx, cz
        s["cy2"][x] = jnp.where(last2, 0.0, cy)
        s["d2"][x] = diagonal
        s["w2"][x] = jnp.where(in_z2, OMEGA / diagonal, 0.0)
        return inext, cx

    loop(4, 20, make2, (s["ie2"][4], s["cx2"][3]))
    for x in range(4):
        for name in ("a2", "b2"):
            s[name][x] = jnp.zeros(shape2, F32)
            s[name][20 + x] = jnp.zeros(shape2, F32)

    def down3(pair):
        def one(k, carry):
            rows = pl.ds(pl.multiple_of(k * 16, 16), 16)
            s["rs3"][rows] = dot(s["my2"][...], pair(k))
            return carry

        loop(0, 8, one, 0)
        return dot(s["rs3"][...], s["mz2"][...]).reshape(8, 16, 128)

    shape3 = (8, 16, 128)
    p3 = place(iota(shape3, 2), 32, 128)
    near3 = (p3 >= -16) & (p3 < 48)
    e3 = down3(lambda k: s["e2"][4 + 2 * k] + s["e2"][5 + 2 * k]) * 0.25
    ie3 = 1.0 / jnp.where(near3, e3, 1.0)
    first3, last3 = iota(shape3, 1) == 0, iota(shape3, 1) == 15
    edge = jnp.ones((1, 16, 128), F32)
    none = jnp.zeros((1, 16, 128), F32)

    def roll3(values, shift, axis):
        return roll(values.reshape(128, 128), shift, 1).reshape(shape3) if axis == 2 else jnp.stack(
            [roll(values[k], shift, 0) for k in range(8)]
        )

    around = jnp.concatenate([edge, ie3, edge], 0)
    cx3 = 2.0 / (around[1:] + around[:-1])
    cy3 = 2.0 / (ie3 + jnp.where(last3, 1.0, roll3(ie3, -1, 1)))
    below3 = jnp.where(first3, 2.0 / (ie3 + 1.0), roll3(cy3, 1, 1))
    cz3 = 2.0 / (ie3 + roll3(ie3, -1, 2))
    d3 = cx3[1:] + cx3[:-1] + cy3 + below3 + cz3 + roll3(cz3, 1, 2)
    q3 = p3 + 32 * gz
    s["w3"][...] = jnp.where((q3 >= 0) & (q3 < NZ // 8), OMEGA / d3, 0.0)
    s["cx3"][...] = cx3
    s["cy3"][...] = jnp.where(last3, 0.0, cy3)
    s["cz3"][...] = cz3

    collect("gf")

    def put_f2(x, rows, values):
        s["f2"][x, rows] = values
        s["a2"][x, rows] = s["w2"][x, rows] * values

    arrange("gf", put_f2)
    sweeps(2, "a2", "b2", 4, 20)
    f3 = down3(lambda k: residue(2, "b2", 4 + 2 * k) + residue(2, "b2", 5 + 2 * k))
    s["f3"][...] = f3

    def coarse(_, v):
        cx, cy, cz = s["cx3"][...], s["cy3"][...], s["cz3"][...]
        after = jnp.concatenate([v[1:], none], 0)
        before = jnp.concatenate([none, v[:-1]], 0)
        u = s["f3"][...] + cx[1:] * after + cx[:-1] * before
        u = u + cy * roll3(v, -1, 1) + roll3(cy * v, 1, 1)
        u = u + cz * roll3(v, -1, 2) + roll3(cz * v, 1, 2)
        return KEEP * v + s["w3"][...] * u

    v3 = loop(0, COARSE_SWEEPS - 1, coarse, s["w3"][...] * f3)

    wide = dot(v3.reshape(128, 128), s["pz3"][...]).reshape(8, 16, 128)
    rows3 = [dot(s["py3"][...], wide[k]) for k in range(8)]
    nothing = jnp.zeros(shape2, F32)
    for k in range(8):
        low = rows3[k - 1] if k else nothing
        high = rows3[k + 1] if k < 7 else nothing
        for i, other in ((0, low), (1, high)):
            x = 4 + 2 * k + i
            add = 0.75 * rows3[k] + 0.25 * other
            s["b2"][x] += jnp.where(in_z2, add, 0.0)
    sweeps(2, "b2", "a2", 4, 20)
    sweeps(2, "a2", "b2", 4, 20)

    for k in range(8):
        s["up1"][16 * k : 16 * k + 16] = dot(s["py2"][...], s["b2"][2 * gx + 1 + k])
    up1 = dot(s["up1"][...], s["pz2"][...])
    arrive_all(FLAT, flat1)
    up1 = up1.reshape(8, 16, 256)
    for x in range(12):
        k = (x - 4) // 2 + 3
        other = up1[k - 1] if x % 2 == 0 else up1[k + 1]
        add = 0.75 * up1[k] + 0.25 * other
        under = jnp.zeros((8, 256), F32)
        if 1 <= x <= 10:
            under = jnp.where(low_row, s["v1"][2, x], s["v1"][0, x])
        v = jnp.concatenate([s["v1"][1, x], under], 0) + add
        s["a1"][x] = jnp.where(both(m1, x_inside(x - 4, 4, NX // 2)), v, 0.0)
    sweeps(1, "a1", "b1", 1, 11)
    sweeps(1, "b1", "a1", 2, 10)

    for k in range(8):
        s["up0"][24 * k : 24 * k + 24] = dot(s["py1"][...], s["a1"][2 + k])
    up0 = dot(s["up0"][...], s["pz1"][...]).reshape(8, 24, 384)
    for x in range(2, 14):
        k = (x - 4) // 2 + 2
        other = up0[k - 1] if x % 2 == 0 else up0[k + 1]
        add = 0.75 * up0[k] + 0.25 * other
        s["b0"][x] += jnp.where(both(m0, x_inside(x - 4, 8, NX)), add, 0.0)
    sweeps(0, "b0", "a0", 3, 13)

    def finish(x, carry):
        v, u = total(0, "a0", x)
        out[x - 4] = (KEEP * v + s["w0"][x] * u)[:16, :256]
        return carry

    loop(4, 12, finish, 0)

    leave_all(order, round0)
    leave_all(order, block1("e1", 4))
    leave_all(order, block1("f1b", 3))
    leave_all(FLAT, flat1)
    for name in ("ge", "gf"):
        gather_many(name).wait_send()
        gather_pair(name)[0].wait_send()


def buffers():
    def vmem(*shape):
        return pltpu.VMEM(shape, F32)

    table = {
        "sz": vmem(2, 8, 16, 128), "rz": vmem(2, 16, 16, 128),
        "sy": vmem(2, 8, 8, 256), "ry": vmem(2, 16, 8, 256),
        "ryz": vmem(2, 2, 16, 8, 128),
        "e1": vmem(9, 12, 8, 128), "f1b": vmem(9, 12, 8, 128), "v1": vmem(3, 12, 8, 256),
        "ge": vmem(2, 32, 8, 128), "gf": vmem(2, 32, 8, 128),
        "my0": vmem(32, 64), "mz0": vmem(256, 128), "my1": vmem(8, 16), "mz1": vmem(256, 128),
        "my2": vmem(16, 32), "mz2": vmem(128, 128), "pz3": vmem(128, 128), "py3": vmem(32, 16),
        "pz2": vmem(128, 256), "py2": vmem(16, 32), "pz1": vmem(256, 384), "py1": vmem(24, 16),
        "rs0": vmem(64, 256), "rs1": vmem(16, 256), "rs3": vmem(128, 128),
        "up1": vmem(128, 128), "up0": vmem(192, 256),
        "ie1": vmem(12, 16, 256), "e2": vmem(24, 32, 128), "ie2": vmem(24, 32, 128),
        "f3": vmem(8, 16, 128), "w3": vmem(8, 16, 128), "cx3": vmem(9, 16, 128),
        "cy3": vmem(8, 16, 128), "cz3": vmem(8, 16, 128),
    }
    shapes = {"0": (16, 24, 384), "1": (12, 16, 256), "2": (24, 32, 128)}
    for level, shape in shapes.items():
        for name in ("f", "cx", "cy", "cz", "d", "w", "a", "b"):
            table[name + level] = vmem(*shape)
    table["e0"] = vmem(16, 24, 384)
    for name, number in (("c0", 28), ("e1", 26), ("f1b", 26), ("v1", 8), ("ge", 2), ("gf", 2)):
        table[name + "_s"] = pltpu.SemaphoreType.DMA((number,))
        table[name + "_r"] = pltpu.SemaphoreType.DMA((number,))
    return table


NAMES = list(buffers())


def on_device(charge, dielectric):
    return pl.pallas_call(
        lambda f, e, o, *s: kernel(f, e, o, s),
        out_shape=jax.ShapeDtypeStruct((8, 16, 256), F32),
        in_specs=[pl.BlockSpec(memory_space=pltpu.VMEM)] * 2,
        out_specs=pl.BlockSpec(memory_space=pltpu.VMEM),
        scratch_shapes=list(buffers().values()),
        compiler_params=pltpu.CompilerParams(
            collective_id=0, has_side_effects=True, vmem_limit_bytes=40 * 2**20
        ),
    )(charge, dielectric)


def solution(mesh):
    placed = (P("gx", "gy", "gz"), P("gx", "gy", "gz"))
    return jax.shard_map(
        on_device, mesh=mesh, in_specs=placed, out_specs=P("gx", "gy", "gz"), check_vma=False
    )
```

```python
import functools
import itertools
import math

import jax
import jax.numpy as jnp
from jax import lax
from jax.experimental import pallas as pl
from jax.experimental.pallas import tpu as pltpu
from jax.sharding import PartitionSpec as P

MESH = pl.DeviceIdType.MESH
F32 = jnp.float32
BF16 = jnp.bfloat16
OMEGA = 0.8
KEEP = 1.0 - OMEGA
FOURPI = 4.0 * math.pi
COARSE_SWEEPS = 8
NX, NY, NZ = 64, 128, 1024
GX, GY, GZ = 8, 8, 4
DIRS = [d for d in itertools.product((-1, 0, 1), repeat=3) if d != (0, 0, 0)]
EDGES = [d for d in DIRS if 0 in d]
FLAT = [d for d in itertools.product((-1, 0, 1), repeat=2) if d != (0, 0)]


def loop(start, stop, body, init):
    return lax.fori_loop(start, stop, body, init, unroll=True)


def roll(values, shift, axis):
    return pltpu.roll(values, shift % values.shape[axis], axis)


def halves(values):
    high = values.astype(BF16)
    return high, (values - high.astype(F32)).astype(BF16)


def dot(a, b):
    if b.dtype == BF16:
        high, low = halves(a)
        return jnp.dot(high, b, preferred_element_type=F32) + jnp.dot(
            low, b, preferred_element_type=F32
        )
    high, low = halves(b)
    a = a.astype(BF16)
    return jnp.dot(a, high, preferred_element_type=F32) + jnp.dot(
        a, low, preferred_element_type=F32
    )


def place(index, own, size):
    half = (size - own) // 2
    return jnp.where(index < own + half, index, index - size)


def iota(shape, axis):
    return lax.broadcasted_iota(jnp.int32, shape, axis)


def restrict_z(own, size, out_own, out_size, weight):
    shape = (size, out_size)
    p = place(iota(shape, 0), own, size)
    q = place(iota(shape, 1), out_own, out_size)
    return jnp.where((p >> 1) == q, weight, 0.0).astype(BF16)


def pair_rows(groups, own, weight):
    shape = (groups * own // 2, groups * own)
    return jnp.where((iota(shape, 1) >> 1) == iota(shape, 0), weight, 0.0).astype(F32)


def spread(q, p):
    parent = p >> 1
    other = jnp.where((p & 1) == 0, parent - 1, parent + 1)
    return jnp.where(q == parent, 0.75, jnp.where(q == other, 0.25, 0.0)).astype(F32)


def prolong_z(own, size, out_own, out_size):
    shape = (size, out_size)
    weights = spread(place(iota(shape, 0), own, size), place(iota(shape, 1), out_own, out_size))
    return weights.astype(BF16)


def prolong_y(own, size, out_own, out_size):
    shape = (out_size, size)
    return spread(place(iota(shape, 1), own, size), place(iota(shape, 0), out_own, out_size))


def kernel(f_in, e_in, out, s):
    s = dict(zip(NAMES, s, strict=True))
    gx, gy, gz = (lax.axis_index(a) for a in ("gx", "gy", "gz"))
    core = gy & 1
    column = gx * 4 + (gy >> 1)
    has = [
        {-1: gx > 0, 0: True, 1: gx < GX - 1},
        {-1: gy > 0, 0: True, 1: gy < GY - 1},
        {-1: gz > 0, 0: True, 1: gz < GZ - 1},
    ]

    def there(d):
        found = [has[i][c] for i, c in enumerate(d) if c]
        return functools.reduce(jnp.logical_and, found)

    def peer(d):
        return (gx + d[0], gy + d[1], gz + (d[2] if len(d) > 2 else 0))

    def flip(d):
        return tuple(-c for c in d)

    def column_peer(k):
        other = (column + k) & 31
        return (other >> 2, ((other & 3) << 1) + core, gz)

    sibling = (gx, gy + 1 - 2 * core, gz)

    barrier = pltpu.get_barrier_semaphore()

    def greet(device):
        pl.semaphore_signal(barrier, inc=1, device_id=device, device_id_type=MESH)

    for d in DIRS:
        pl.when(there(d))(functools.partial(greet, peer(d)))

    def greet_column(k, carry):
        greet(column_peer(k))
        return carry

    loop(1, 32, greet_column, 0)

    def count(i):
        return 1 + has[i][-1].astype(jnp.int32) + has[i][1].astype(jnp.int32)

    lane128 = iota((16, 128), 1)
    row256 = iota((8, 256), 0)

    def pack(x, carry):
        f, e = f_in[x], e_in[x]
        s["sz"][0, x] = jnp.where(lane128 < 64, f[:, :128], roll(e[:, :128], 64, 1))
        s["sz"][1, x] = jnp.where(lane128 >= 64, f[:, 128:], roll(e[:, 128:], 64, 1))
        s["sy"][0, x] = jnp.where(row256 < 4, f[:8], roll(e[:8], 4, 0))
        s["sy"][1, x] = jnp.where(row256 >= 4, f[8:], roll(e[8:], 4, 0))
        return carry

    loop(0, 8, pack, 0)

    row8 = iota((8, 256), 0)
    for xs in range(2):
        one, two = (0, 1) if xs == 0 else (7, 6)
        near = slice(0, 1), slice(15, 16)
        s["ey"][xs, 0] = jnp.where(
            (row8 == 2) | (row8 == 3), roll(s["sy"][0, two], -2, 0), s["sy"][0, one]
        )
        s["ey"][xs, 1] = jnp.where(
            (row8 == 4) | (row8 == 5), roll(s["sy"][1, two], 2, 0), s["sy"][1, one]
        )
        s["ez"][xs, 0] = jnp.where(
            (lane128 >= 32) & (lane128 < 64), roll(s["sz"][0, two], -32, 1), s["sz"][0, one]
        )
        s["ez"][xs, 1] = jnp.where(
            (lane128 >= 64) & (lane128 < 96), roll(s["sz"][1, two], 32, 1), s["sz"][1, one]
        )
        for ys in range(2):
            s["ec"][xs, ys, 0] = e_in[one, near[ys], :128]
            s["ec"][xs, ys, 1] = e_in[one, near[ys], 128:]

    pl.semaphore_wait(barrier, count(0) * count(1) * count(2) - 1 + 31)

    def send(src, dst, name, index, device):
        return pltpu.make_async_remote_copy(
            src_ref=src,
            dst_ref=dst,
            send_sem=s[name + "_s"].at[index],
            recv_sem=s[name + "_r"].at[index],
            device_id=device,
            device_id_type=MESH,
        )

    def cut(dx, n, whole, base):
        if dx == 0:
            return pl.ds(0, whole), pl.ds(base, whole)
        if dx < 0:
            return pl.ds(0, n), pl.ds(base + whole, n)
        return pl.ds(whole - n, n), pl.ds(base - n, n)

    def round0(d):
        dx, dy, dz = d
        index = DIRS.index(d)
        xs, ys, zs = (int(c > 0) for c in d)
        if dy == 0 and dz == 0:
            a, b = cut(dx, 2, 8, 4)
            own = (pl.ds(0, 16), pl.ds(0, 256))
            first = send(f_in.at[a], s["f0"].at[(b, *own)], "c0", index, peer(d))
            a, b = cut(dx, 3, 8, 4)
            second = send(e_in.at[a], s["e0"].at[(b, *own)], "c0", 26 + (dx > 0), peer(d))
            return [first, second]
        if dx and dy and dz:
            source, target = s["ec"].at[xs, ys, zs], s["rec"].at[1 - xs, 1 - ys, 1 - zs]
        elif dx and dy:
            source, target = s["ey"].at[xs, ys], s["rey"].at[1 - xs, 1 - ys]
        elif dx:
            source, target = s["ez"].at[xs, zs], s["rez"].at[1 - xs, 1 - zs]
        elif dy and dz:
            source = s["sy"].at[ys, :, :, pl.ds(128 * zs, 128)]
            target = s["ryz"].at[1 - ys, 1 - zs]
        elif dy:
            source, target = s["sy"].at[ys], s["ry"].at[1 - ys]
        else:
            source, target = s["sz"].at[zs], s["rz"].at[1 - zs]
        return [send(source, target, "c0", index, peer(d))]

    def iterate0(d):
        dx, dy, dz = d
        xs, ys, zs = (int(c > 0) for c in d)
        x = pl.ds(4, 8)
        if dx:
            wide = 1 if dy or dz else 2
            x = pl.ds(12 - wide if dx > 0 else 4, wide)
        rows = pl.ds(8 * ys, 8) if dy else pl.ds(0, 16)
        lanes = pl.ds(128 * zs, 128) if dz else pl.ds(0, 256)
        name = "v" + "x" * (dx != 0) + "y" * (dy != 0) + "z" * (dz != 0)
        slot = tuple(1 - i for i, c in zip((xs, ys, zs), d) if c)
        source, target = s["b0"].at[x, rows, lanes], s[name].at[slot]
        return [send(source, target, "v0", EDGES.index(d), peer(d))]

    def shrink(name, slab):
        width = slab(0).shape[1]
        row = iota((8, width), 0)
        for xs in range(2):
            one, two, three = (slab(k if xs == 0 else 3 - k) for k in range(3))
            tile = jnp.where(row >= 3, roll(two, 3, 0), one)
            s[name][xs, 0] = jnp.where(row >= 5, roll(three, 5, 0), tile)
            tile = jnp.where(row <= 4, roll(two, -3, 0), one)
            s[name][xs, 1] = jnp.where(row <= 2, roll(three, -5, 0), tile)

    def grow(tile, ys, distance):
        shift = (0, 3, 5)[distance - 1]
        return roll(tile, -shift if ys else shift, 0) if shift else tile

    def block1(name, wide):
        def copies(d):
            dx, dy, dz = d
            index = DIRS.index(d)
            if dx and dy:
                xs, ys = int(dx > 0), int(dy > 0)
                source, target = s["p" + name].at[xs, ys], s["r" + name].at[1 - xs, 1 - ys, 1 - dz]
                return [send(source, target, name, index, peer(d))]
            a, b = cut(dx, wide, 4, 4)
            own = pl.ds(4 + a.start, a.size)
            slot = (1 - dy) * 3 + 1 - dz
            buffer = s[name]
            return [send(buffer.at[4, own], buffer.at[slot, b], name, index, peer(d))]

        return copies

    def flat1(d):
        dx, dy = d
        if dx and dy:
            xs, ys = int(dx > 0), int(dy > 0)
            source, target = s["pv1"].at[xs, ys], s["rv1"].at[1 - xs, 1 - ys]
            return [send(source, target, "v1", FLAT.index(d), peer(d))]
        a, b = cut(dx, 4, 4, 4)
        own = pl.ds(4 + a.start, a.size)
        return [send(s["v1"].at[1, own], s["v1"].at[1 - dy, b], "v1", FLAT.index(d), peer(d))]

    def start_all(dirs, copies):
        for d in dirs:

            @pl.when(there(d))
            def _(d=d):
                for copy in copies(d):
                    copy.start()

    def arrive_all(dirs, copies):
        for d in dirs:

            @pl.when(there(flip(d)))
            def _(d=d):
                for copy in copies(d):
                    copy.wait_recv()

    def leave_all(dirs, copies):
        for d in dirs:

            @pl.when(there(d))
            def _(d=d):
                for copy in copies(d):
                    copy.wait_send()

    def gather_start(name):
        mine = s[name].at[core, column]

        def one(k, carry):
            send(mine, mine, name, 0, column_peer(k)).start()
            return carry

        loop(1, 32, one, 0)

    def gather_many(name):
        part = s[name].at[core, pl.ds(0, 31)]
        return send(part, part, name, 0, sibling)

    def gather_pair(name):
        mine, theirs = s[name].at[core], s[name].at[1 - core]
        return send(mine, mine, name, 1, sibling), send(theirs, theirs, name, 1, sibling)

    order = sorted(DIRS, key=lambda d: (-abs(d[0]), abs(d[1]) + abs(d[2])))
    start_all(order, round0)

    s["my0"][...] = pair_rows(4, 16, 0.5)
    s["mz0"][...] = restrict_z(256, 256, 128, 128, 1.0)
    for k in range(4):
        s["rs0"][16 * k : 16 * k + 16] = e_in[2 * k] + e_in[2 * k + 1]
    own_e1 = (dot(dot(s["my0"][...], s["rs0"][...]), s["mz0"][...]) * 0.25).reshape(4, 8, 128)
    s["e1"][4, 4:8] = own_e1
    shrink("pe1", lambda k: own_e1[k])
    start_all(order, block1("e1", 4))

    s["my1"][...] = pair_rows(2, 8, 0.5)
    s["mz1"][...] = restrict_z(128, 256, 64, 128, 1.0)
    s["my2"][...] = pair_rows(1, 32, 0.5)
    s["mz2"][...] = restrict_z(64, 128, 32, 128, 1.0)
    s["pz3"][...] = prolong_z(32, 128, 64, 128)
    s["py3"][...] = prolong_y(16, 16, 32, 32)
    s["pz2"][...] = prolong_z(64, 128, 128, 256)
    fine = place(iota((16, 32), 0), 8, 16) + 8 * gy
    s["py2"][...] = spread(iota((16, 32), 1), fine)
    s["pz1"][...] = prolong_z(128, 256, 256, 384)
    s["py1"][...] = prolong_y(8, 16, 16, 24)

    def inside(shape, own, index, total, axis):
        p = place(iota(shape, axis), own, shape[axis]) + own * index
        return (p >= 0) & (p < total)

    def x_inside(x, own, total):
        p = x + own * gx
        return (p >= 0) & (p < total)

    def mask(shape, own_y, own_z, total_y, total_z):
        return inside(shape, own_y, gy, total_y, 0) & inside(shape, own_z, gz, total_z, 1)

    def both(a, flag):
        return jnp.logical_and(a, jnp.broadcast_to(flag, a.shape))

    def beside(v, cx_low, cx, cy, cz, low, high):
        total = cx_low * low + cx * high
        total = total + cy * roll(v, -1, 0) + roll(cy * v, 1, 0)
        return total + cz * roll(v, -1, 1) + roll(cz * v, 1, 1)

    arrive_all(order, round0)
    m0 = mask((24, 384), 16, 256, NY, NZ)
    ones0 = jnp.ones((24, 384), F32)
    low_lane = iota((16, 128), 1) < 64
    low_lane8 = iota((8, 128), 1) < 64
    low_row = iota((8, 256), 0) < 4
    low_row8 = iota((8, 128), 0) < 4

    def fill(x):
        m = both(m0, x_inside(x - 4, 8, NX))
        if 4 <= x < 12:
            distance, xs, f_own, e_own = 0, 0, f_in[x - 4], e_in[x - 4]
            k = x - 4
            z0, z1, y0, y1 = s["rz"][0, k], s["rz"][1, k], s["ry"][0, k], s["ry"][1, k]
        else:
            xs, distance = (0, 4 - x) if x < 4 else (1, x - 11)
            f_own, e_own = s["f0"][x, :16, :256], s["e0"][x, :16, :256]
            if distance == 3:
                e = jnp.concatenate([e_own, jnp.ones((16, 128), F32)], 1)
                e = jnp.concatenate([e, jnp.ones((8, 384), F32)], 0)
                s["e0"][x] = 1.0 / jnp.where(m, e, 1.0)
                return
            z0, z1, y0, y1 = s["rez"][xs, 0], s["rez"][xs, 1], s["rey"][xs, 0], s["rey"][xs, 1]
            if distance == 2:
                z0, z1, y0, y1 = roll(z0, -32, 1), roll(z1, 32, 1), roll(y0, -2, 0), roll(y1, 2, 0)
        f_z = jnp.where(low_lane, z1, z0)
        e_z = roll(jnp.where(low_lane, z0, z1), 64, 1)
        f_y = jnp.where(low_row, y1, y0)
        e_y = roll(jnp.where(low_row, y0, y1), 4, 0)
        f_c = jnp.zeros((8, 128), F32)
        e_c = jnp.ones((8, 128), F32)
        if distance == 0:
            c0 = jnp.where(low_lane8, s["ryz"][0, 1, k], s["ryz"][0, 0, k])
            c1 = jnp.where(low_lane8, s["ryz"][1, 1, k], s["ryz"][1, 0, k])
            f_c = jnp.where(low_row8, c1, c0)
            e_c = roll(jnp.where(low_row8, c0, c1), 4, 0)
        elif distance == 1:
            c = s["rec"]
            c0 = jnp.where(low_lane8, c[xs, 0, 1], c[xs, 0, 0])
            c1 = jnp.where(low_lane8, c[xs, 1, 1], c[xs, 1, 0])
            e_c = jnp.where(low_row8, c1, c0)

        f, e = join(f_own, f_z, f_y, f_c), join(e_own, e_z, e_y, e_c)
        s["f0"][x] = jnp.where(m, f, 0.0) * FOURPI
        s["e0"][x] = 1.0 / jnp.where(m, e, 1.0)

    def join(own, z, y, c):
        top = jnp.concatenate([own, z], 1)
        return jnp.concatenate([top, jnp.concatenate([y, c], 1)], 0)

    for x in range(1, 15):
        fill(x)

    def coefficients(ie, x, m, ic, cx_low):
        inext = ie[x + 1]
        cx = 2.0 / (ic + inext)
        cy = 2.0 / (ic + roll(ic, -1, 0))
        cz = 2.0 / (ic + roll(ic, -1, 1))
        diagonal = cx + cx_low + cy + roll(cy, 1, 0) + cz + roll(cz, 1, 1)
        weight = jnp.where(m, OMEGA / diagonal, 0.0)
        return inext, cx, cy, cz, diagonal, weight

    ic = s["e0"][2]
    s["cx0"][1] = 2.0 / (s["e0"][1] + ic)

    def make0(x, carry):
        ic, cx_low = carry
        m = both(m0, x_inside(x - 4, 8, NX))
        ic, cx, cy, cz, diagonal, weight = coefficients(s["e0"], x, m, ic, cx_low)
        s["cx0"][x], s["cy0"][x], s["cz0"][x] = cx, cy, cz
        s["d0"][x], s["w0"][x] = diagonal, weight
        s["a0"][x] = weight * s["f0"][x]
        return ic, cx

    loop(2, 14, make0, (ic, s["cx0"][1]))

    def total(level, src, x):
        c = str(level)
        v = s[src][x]
        return v, s["f" + c][x] + beside(
            v, s["cx" + c][x - 1], s["cx" + c][x], s["cy" + c][x], s["cz" + c][x],
            s[src][x - 1], s[src][x + 1],
        )

    def sweeps(level, src, dst, start, stop):
        def one(x, carry):
            v, u = total(level, src, x)
            s[dst][x] = KEEP * v + s[f"w{level}"][x] * u
            return carry

        loop(start, stop, one, 0)

    def residue(level, src, x):
        v, u = total(level, src, x)
        return u - s[f"d{level}"][x] * v

    sweeps(0, "a0", "b0", 3, 13)

    def pairs0(k, carry):
        r = residue(0, "b0", 4 + 2 * k) + residue(0, "b0", 5 + 2 * k)
        s["rs0"][pl.ds(pl.multiple_of(k * 16, 16), 16)] = r[:16, :256]
        return carry

    loop(0, 4, pairs0, 0)
    own_f1 = dot(dot(s["my0"][...], s["rs0"][...]), s["mz0"][...]).reshape(4, 8, 128)
    s["f1b"][4, 4:8] = own_f1
    shrink("pf1b", lambda k: own_f1[k])
    start_all(order, block1("f1b", 3))
    start_all(EDGES, iterate0)

    m1 = mask((16, 256), 8, 128, NY // 2, NZ // 2)

    def join1(name, x, other, reach):
        b = s[name]
        distance = 4 - x if x < 4 else x - 7 if x > 7 else 0

        def across(y):
            tiles = [b[y * 3 + i, x] for i in range(3)]
            if distance and y != 1:
                r, xs, ys = s["r" + name], int(x > 7), int(y == 2)
                tiles = [grow(r[xs, ys, i], ys, distance) for i in range(3)]
            return jnp.concatenate([tiles[1], jnp.where(low_lane8, tiles[2], tiles[0])], 1)

        under = jnp.full((8, 256), other, F32)
        if distance < reach:
            under = jnp.where(low_row, across(2), across(0))
        both_rows = jnp.concatenate([across(1), under], 0)
        return jnp.where(both(m1, x_inside(x - 4, 4, NX // 2)), both_rows, other)

    arrive_all(order, block1("e1", 4))
    for x in range(12):
        e = join1("e1", x, 1.0, 4)
        s["ie1"][x] = 1.0 / e
        if 4 <= x < 8:
            half = (x - 4) // 2 * 8
            if x % 2 == 0:
                s["rs1"][half : half + 8] = e[:8]
            else:
                s["rs1"][half : half + 8] += e[:8]
    s["ge"][core, column] = dot(dot(s["my1"][...], s["rs1"][...]), s["mz1"][...]) * 0.25
    gather_start("ge")

    s["cx1"][0] = 2.0 / (s["ie1"][0] + s["ie1"][1])

    def make1(x, carry):
        ic, cx_low = carry
        m = both(m1, x_inside(x - 4, 4, NX // 2))
        ic, cx, cy, cz, diagonal, weight = coefficients(s["ie1"], x, m, ic, cx_low)
        s["cx1"][x], s["cy1"][x], s["cz1"][x] = cx, cy, cz
        s["d1"][x], s["w1"][x] = diagonal, weight
        return ic, cx

    loop(1, 11, make1, (s["ie1"][1], s["cx1"][0]))

    arrive_all(order, block1("f1b", 3))
    for x in range(1, 11):
        f = join1("f1b", x, 0.0, 3)
        s["f1"][x] = f
        s["a1"][x] = s["w1"][x] * f
    sweeps(1, "a1", "b1", 3, 9)
    for k in range(2):
        r = residue(1, "b1", 4 + 2 * k) + residue(1, "b1", 5 + 2 * k)
        s["rs1"][8 * k : 8 * k + 8] = r[:8]
    s["gf"][core, column] = dot(dot(s["my1"][...], s["rs1"][...]), s["mz1"][...])
    gather_start("gf")
    for x in range(4, 8):
        s["v1"][1, x] = s["b1"][x, :8]
    shrink("pv1", lambda k: s["v1"][1, 4 + k])
    start_all(FLAT, flat1)

    row8 = iota((8, 128), 0) < 4

    def arrange(name, write):
        def one(k, carry):
            even, odd = s[name][0, k], s[name][1, k]
            x = 2 * (k >> 2)
            rows = pl.ds(pl.multiple_of((k & 3) * 8, 8), 8)
            write(x + 4, rows, jnp.where(row8, even, roll(odd, 4, 0)))
            write(x + 5, rows, jnp.where(row8, roll(even, 4, 0), odd))
            return carry

        loop(0, 32, one, 0)

    def collect(name):
        gather_many(name).wait_recv()
        mine, theirs = gather_pair(name)
        mine.start()
        theirs.wait_recv()

    collect("ge")

    def put_e2(x, rows, values):
        s["e2"][x, rows] = values
        s["ie2"][x, rows] = 1.0 / values

    arrange("ge", put_e2)
    shape2 = (32, 128)
    last2, first2 = iota(shape2, 0) == 31, iota(shape2, 0) == 0
    in_z2 = inside(shape2, 64, gz, NZ // 4, 1)
    s["ie2"][3] = jnp.ones(shape2, F32)
    s["ie2"][20] = jnp.ones(shape2, F32)

    def edge_faces(ic, first, last):
        cy = 2.0 / (ic + jnp.where(last, 1.0, roll(ic, -1, 0)))
        below = jnp.where(first, 2.0 / (ic + 1.0), roll(cy, 1, 0))
        return cy, below

    s["cx2"][3] = 2.0 / (1.0 + s["ie2"][4])

    def make2(x, carry):
        ic, cx_low = carry
        inext = s["ie2"][x + 1]
        cx = 2.0 / (ic + inext)
        cy, below = edge_faces(ic, first2, last2)
        cz = 2.0 / (ic + roll(ic, -1, 1))
        diagonal = cx + cx_low + cy + below + cz + roll(cz, 1, 1)
        s["cx2"][x], s["cz2"][x] = cx, cz
        s["cy2"][x] = jnp.where(last2, 0.0, cy)
        s["d2"][x] = diagonal
        s["w2"][x] = jnp.where(in_z2, OMEGA / diagonal, 0.0)
        return inext, cx

    loop(4, 20, make2, (s["ie2"][4], s["cx2"][3]))
    for x in range(4):
        for name in ("a2", "b2"):
            s[name][x] = jnp.zeros(shape2, F32)
            s[name][20 + x] = jnp.zeros(shape2, F32)

    def down3(pair):
        def one(k, carry):
            rows = pl.ds(pl.multiple_of(k * 16, 16), 16)
            s["rs3"][rows] = dot(s["my2"][...], pair(k))
            return carry

        loop(0, 8, one, 0)
        return dot(s["rs3"][...], s["mz2"][...]).reshape(8, 16, 128)

    shape3 = (8, 16, 128)
    p3 = place(iota(shape3, 2), 32, 128)
    near3 = (p3 >= -16) & (p3 < 48)
    e3 = down3(lambda k: s["e2"][4 + 2 * k] + s["e2"][5 + 2 * k]) * 0.25
    ie3 = 1.0 / jnp.where(near3, e3, 1.0)
    first3, last3 = iota(shape3, 1) == 0, iota(shape3, 1) == 15
    edge = jnp.ones((1, 16, 128), F32)
    none = jnp.zeros((1, 16, 128), F32)

    def roll3(values, shift, axis):
        return roll(values.reshape(128, 128), shift, 1).reshape(shape3) if axis == 2 else jnp.stack(
            [roll(values[k], shift, 0) for k in range(8)]
        )

    around = jnp.concatenate([edge, ie3, edge], 0)
    cx3 = 2.0 / (around[1:] + around[:-1])
    cy3 = 2.0 / (ie3 + jnp.where(last3, 1.0, roll3(ie3, -1, 1)))
    below3 = jnp.where(first3, 2.0 / (ie3 + 1.0), roll3(cy3, 1, 1))
    cz3 = 2.0 / (ie3 + roll3(ie3, -1, 2))
    d3 = cx3[1:] + cx3[:-1] + cy3 + below3 + cz3 + roll3(cz3, 1, 2)
    q3 = p3 + 32 * gz
    s["w3"][...] = jnp.where((q3 >= 0) & (q3 < NZ // 8), OMEGA / d3, 0.0)
    s["cx3"][...] = cx3
    s["cy3"][...] = jnp.where(last3, 0.0, cy3)
    s["cz3"][...] = cz3

    collect("gf")

    def put_f2(x, rows, values):
        s["f2"][x, rows] = values
        s["a2"][x, rows] = s["w2"][x, rows] * values

    arrange("gf", put_f2)
    sweeps(2, "a2", "b2", 4, 20)
    f3 = down3(lambda k: residue(2, "b2", 4 + 2 * k) + residue(2, "b2", 5 + 2 * k))
    s["f3"][...] = f3

    def coarse(_, v):
        cx, cy, cz = s["cx3"][...], s["cy3"][...], s["cz3"][...]
        after = jnp.concatenate([v[1:], none], 0)
        before = jnp.concatenate([none, v[:-1]], 0)
        u = s["f3"][...] + cx[1:] * after + cx[:-1] * before
        u = u + cy * roll3(v, -1, 1) + roll3(cy * v, 1, 1)
        u = u + cz * roll3(v, -1, 2) + roll3(cz * v, 1, 2)
        return KEEP * v + s["w3"][...] * u

    v3 = loop(0, COARSE_SWEEPS - 1, coarse, s["w3"][...] * f3)

    wide = dot(v3.reshape(128, 128), s["pz3"][...]).reshape(8, 16, 128)
    rows3 = [dot(s["py3"][...], wide[k]) for k in range(8)]
    nothing = jnp.zeros(shape2, F32)
    for k in range(8):
        low = rows3[k - 1] if k else nothing
        high = rows3[k + 1] if k < 7 else nothing
        for i, other in ((0, low), (1, high)):
            x = 4 + 2 * k + i
            add = 0.75 * rows3[k] + 0.25 * other
            s["b2"][x] += jnp.where(in_z2, add, 0.0)
    sweeps(2, "b2", "a2", 4, 20)
    sweeps(2, "a2", "b2", 4, 20)

    for k in range(8):
        s["up1"][16 * k : 16 * k + 16] = dot(s["py2"][...], s["b2"][2 * gx + 1 + k])
    up1 = dot(s["up1"][...], s["pz2"][...])
    arrive_all(FLAT, flat1)
    up1 = up1.reshape(8, 16, 256)
    for x in range(12):
        k = (x - 4) // 2 + 3
        other = up1[k - 1] if x % 2 == 0 else up1[k + 1]
        add = 0.75 * up1[k] + 0.25 * other
        distance = 4 - x if x < 4 else x - 7 if x > 7 else 0
        under = jnp.zeros((8, 256), F32)
        if distance == 0:
            under = jnp.where(low_row, s["v1"][2, x], s["v1"][0, x])
        elif distance < 4:
            r = s["rv1"]
            after, before = (grow(r[int(x > 7), ys], ys, distance) for ys in (1, 0))
            under = jnp.where(low_row, after, before)
        v = jnp.concatenate([s["v1"][1, x], under], 0) + add
        s["a1"][x] = jnp.where(both(m1, x_inside(x - 4, 4, NX // 2)), v, 0.0)
    sweeps(1, "a1", "b1", 1, 11)
    sweeps(1, "b1", "a1", 2, 10)

    arrive_all(EDGES, iterate0)

    def whole0(x):
        nothing = [jnp.zeros(shape, F32) for shape in ((16, 128), (8, 256), (8, 128))]
        if 4 <= x < 12:
            k = x - 4
            z = jnp.where(low_lane, s["vz"][1, k], s["vz"][0, k])
            y = jnp.where(low_row, s["vy"][1, k], s["vy"][0, k])
            c = [jnp.where(low_lane8, s["vyz"][i, 1, k], s["vyz"][i, 0, k]) for i in range(2)]
            return join(s["b0"][x, :16, :256], z, y, jnp.where(low_row8, c[1], c[0]))
        xs, distance = (0, 4 - x) if x < 4 else (1, x - 11)
        own = s["vx"][xs, 2 - distance if xs == 0 else distance - 1]
        if distance == 2:
            return join(own, *nothing)
        z = jnp.where(low_lane, s["vxz"][xs, 1, 0], s["vxz"][xs, 0, 0])
        y = jnp.where(low_row, s["vxy"][xs, 1, 0], s["vxy"][xs, 0, 0])
        return join(own, z, y, nothing[2])

    for k in range(8):
        s["up0"][24 * k : 24 * k + 24] = dot(s["py1"][...], s["a1"][2 + k])
    up0 = dot(s["up0"][...], s["pz1"][...]).reshape(8, 24, 384)
    for x in range(2, 14):
        k = (x - 4) // 2 + 2
        other = up0[k - 1] if x % 2 == 0 else up0[k + 1]
        add = 0.75 * up0[k] + 0.25 * other
        v = whole0(x) + add
        s["a0"][x] = jnp.where(both(m0, x_inside(x - 4, 8, NX)), v, 0.0)
    sweeps(0, "a0", "g0", 3, 13)

    def finish(x, carry):
        v, u = total(0, "g0", x)
        out[x - 4] = (KEEP * v + s["w0"][x] * u)[:16, :256]
        return carry

    loop(4, 12, finish, 0)

    leave_all(order, round0)
    leave_all(order, block1("e1", 4))
    leave_all(order, block1("f1b", 3))
    leave_all(FLAT, flat1)
    leave_all(EDGES, iterate0)
    for name in ("ge", "gf"):
        gather_many(name).wait_send()
        gather_pair(name)[0].wait_send()


def buffers():
    def vmem(*shape):
        return pltpu.VMEM(shape, F32)

    def half(*shape):
        return pltpu.VMEM(shape, BF16)

    table = {
        "sz": vmem(2, 8, 16, 128), "rz": vmem(2, 8, 16, 128),
        "sy": vmem(2, 8, 8, 256), "ry": vmem(2, 8, 8, 256), "ryz": vmem(2, 2, 8, 8, 128),
        "ey": vmem(2, 2, 8, 256), "rey": vmem(2, 2, 8, 256),
        "ez": vmem(2, 2, 16, 128), "rez": vmem(2, 2, 16, 128),
        "ec": vmem(2, 2, 2, 1, 128), "rec": vmem(2, 2, 2, 1, 128),
        "vx": vmem(2, 2, 16, 256), "vy": vmem(2, 8, 8, 256), "vz": vmem(2, 8, 16, 128),
        "vxy": vmem(2, 2, 1, 8, 256), "vxz": vmem(2, 2, 1, 16, 128), "vyz": vmem(2, 2, 8, 8, 128),
        "pe1": vmem(2, 2, 8, 128), "re1": vmem(2, 2, 3, 8, 128),
        "pf1b": vmem(2, 2, 8, 128), "rf1b": vmem(2, 2, 3, 8, 128),
        "pv1": vmem(2, 2, 8, 256), "rv1": vmem(2, 2, 8, 256), "g0": vmem(16, 24, 384),
        "e1": vmem(9, 12, 8, 128), "f1b": vmem(9, 12, 8, 128), "v1": vmem(3, 12, 8, 256),
        "ge": vmem(2, 32, 8, 128), "gf": vmem(2, 32, 8, 128),
        "my0": vmem(32, 64), "mz0": half(256, 128), "my1": vmem(8, 16), "mz1": half(256, 128),
        "my2": vmem(16, 32), "mz2": half(128, 128), "pz3": half(128, 128), "py3": vmem(32, 16),
        "pz2": half(128, 256), "py2": vmem(16, 32), "pz1": half(256, 384), "py1": vmem(24, 16),
        "rs0": vmem(64, 256), "rs1": vmem(16, 256), "rs3": vmem(128, 128),
        "up1": vmem(128, 128), "up0": vmem(192, 256),
        "ie1": vmem(12, 16, 256), "e2": vmem(24, 32, 128), "ie2": vmem(24, 32, 128),
        "f3": vmem(8, 16, 128), "w3": vmem(8, 16, 128), "cx3": vmem(9, 16, 128),
        "cy3": vmem(8, 16, 128), "cz3": vmem(8, 16, 128),
    }
    shapes = {"0": (16, 24, 384), "1": (12, 16, 256), "2": (24, 32, 128)}
    for level, shape in shapes.items():
        for name in ("f", "cx", "cy", "cz", "d", "w", "a", "b"):
            table[name + level] = vmem(*shape)
    table["e0"] = vmem(16, 24, 384)
    for name, number in (("c0", 28), ("v0", 18), ("e1", 26), ("f1b", 26), ("v1", 8), ("ge", 2), ("gf", 2)):
        table[name + "_s"] = pltpu.SemaphoreType.DMA((number,))
        table[name + "_r"] = pltpu.SemaphoreType.DMA((number,))
    return table


NAMES = list(buffers())


def on_device(charge, dielectric):
    return pl.pallas_call(
        lambda f, e, o, *s: kernel(f, e, o, s),
        out_shape=jax.ShapeDtypeStruct((8, 16, 256), F32),
        in_specs=[pl.BlockSpec(memory_space=pltpu.VMEM)] * 2,
        out_specs=pl.BlockSpec(memory_space=pltpu.VMEM),
        scratch_shapes=list(buffers().values()),
        compiler_params=pltpu.CompilerParams(
            collective_id=0, has_side_effects=True, vmem_limit_bytes=40 * 2**20
        ),
    )(charge, dielectric)


def solution(mesh):
    placed = (P("gx", "gy", "gz"), P("gx", "gy", "gz"))
    return jax.shard_map(
        on_device, mesh=mesh, in_specs=placed, out_specs=P("gx", "gy", "gz"), check_vma=False
    )
```

```python
import functools
import itertools
import math

import jax
import jax.numpy as jnp
from jax import lax
from jax.experimental import pallas as pl
from jax.experimental.pallas import tpu as pltpu
from jax.sharding import PartitionSpec as P

MESH = pl.DeviceIdType.MESH
F32 = jnp.float32
BF16 = jnp.bfloat16
OMEGA = 0.8
KEEP = 1.0 - OMEGA
FOURPI = 4.0 * math.pi
COARSE_SWEEPS = 8
NX, NY, NZ = 64, 128, 1024
GX, GY, GZ = 8, 8, 4
DIRS = [d for d in itertools.product((-1, 0, 1), repeat=3) if d != (0, 0, 0)]
ASIDE = [d for d in DIRS if d[0]]
LEVEL = [d for d in DIRS if not d[0]]
EDGES = [d for d in DIRS if 0 in d]
FLAT = [d for d in itertools.product((-1, 0, 1), repeat=2) if d != (0, 0)]


def loop(start, stop, body, init):
    return lax.fori_loop(start, stop, body, init, unroll=True)


def roll(values, shift, axis):
    return pltpu.roll(values, shift % values.shape[axis], axis)


def halves(values):
    high = values.astype(BF16)
    return high, (values - high.astype(F32)).astype(BF16)


def dot(a, b):
    if b.dtype == BF16:
        high, low = halves(a)
        return jnp.dot(high, b, preferred_element_type=F32) + jnp.dot(
            low, b, preferred_element_type=F32
        )
    high, low = halves(b)
    a = a.astype(BF16)
    return jnp.dot(a, high, preferred_element_type=F32) + jnp.dot(
        a, low, preferred_element_type=F32
    )


def place(index, own, size):
    half = (size - own) // 2
    return jnp.where(index < own + half, index, index - size)


def iota(shape, axis):
    return lax.broadcasted_iota(jnp.int32, shape, axis)


def restrict_z(own, size, out_own, out_size, weight):
    shape = (size, out_size)
    p = place(iota(shape, 0), own, size)
    q = place(iota(shape, 1), out_own, out_size)
    return jnp.where((p >> 1) == q, weight, 0.0).astype(BF16)


def pair_rows(groups, own, weight):
    shape = (groups * own // 2, groups * own)
    return jnp.where((iota(shape, 1) >> 1) == iota(shape, 0), weight, 0.0).astype(F32)


def spread(q, p):
    parent = p >> 1
    other = jnp.where((p & 1) == 0, parent - 1, parent + 1)
    return jnp.where(q == parent, 0.75, jnp.where(q == other, 0.25, 0.0)).astype(F32)


def prolong_z(own, size, out_own, out_size):
    shape = (size, out_size)
    weights = spread(place(iota(shape, 0), own, size), place(iota(shape, 1), out_own, out_size))
    return weights.astype(BF16)


def prolong_y(own, size, out_own, out_size):
    shape = (out_size, size)
    return spread(place(iota(shape, 1), own, size), place(iota(shape, 0), out_own, out_size))


def kernel(f_hbm, e_hbm, out, s):
    s = dict(zip(NAMES, s, strict=True))
    f_in, e_in = s["f_in"], s["e_in"]
    loads = [
        pltpu.make_async_copy(f_hbm, f_in, s["in_s"].at[0]),
        pltpu.make_async_copy(e_hbm, e_in, s["in_s"].at[1]),
    ]
    for load in loads:
        load.start()
    gx, gy, gz = (lax.axis_index(a) for a in ("gx", "gy", "gz"))
    core = gy & 1
    column = gx * 4 + (gy >> 1)
    has = [
        {-1: gx > 0, 0: True, 1: gx < GX - 1},
        {-1: gy > 0, 0: True, 1: gy < GY - 1},
        {-1: gz > 0, 0: True, 1: gz < GZ - 1},
    ]

    def there(d):
        found = [has[i][c] for i, c in enumerate(d) if c]
        return functools.reduce(jnp.logical_and, found)

    def peer(d):
        return (gx + d[0], gy + d[1], gz + (d[2] if len(d) > 2 else 0))

    def flip(d):
        return tuple(-c for c in d)

    sibling = (gx, gy + 1 - 2 * core, gz)

    barrier = pltpu.get_barrier_semaphore()

    def greet(device):
        pl.semaphore_signal(barrier, inc=1, device_id=device, device_id_type=MESH)

    order = sorted(DIRS, key=lambda d: (-abs(d[0]), abs(d[1]) + abs(d[2])))
    aside = [d for d in order if d[0]]
    for d in order:
        pl.when(there(d))(functools.partial(greet, peer(d)))

    def count(i):
        return 1 + has[i][-1].astype(jnp.int32) + has[i][1].astype(jnp.int32)

    lane128 = iota((16, 128), 1)
    row256 = iota((8, 256), 0)

    def mixed(side, x):
        f, e = f_in[x], e_in[x]
        if side == 0:
            return jnp.where(lane128 < 64, f[:, :128], roll(e[:, :128], 64, 1))
        return jnp.where(lane128 >= 64, f[:, 128:], roll(e[:, 128:], 64, 1))

    for load in loads:
        load.wait()
    share, part = lane128 >> 4, lane128 & 15
    share8 = iota((8, 128), 1) >> 4
    for zs in range(2):
        tile = jnp.zeros((16, 128), F32)
        lanes = slice(128 * zs, 128 * zs + 128)
        for x in range(8):
            f, e = f_in[x][:, lanes], e_in[x][:, lanes]
            f, e = roll(f, 16 * x + 8 * zs, 1), roll(e, 16 * x + 8 + 8 * zs, 1)
            tile = jnp.where(share == x, jnp.where(part < 8, f, e), tile)
        s["sz"][zs] = tile
    for ys in range(2):
        tiles = [jnp.zeros((8, 128), F32)] * 2
        for x in range(8):
            f, e = f_in[x], e_in[x]
            if ys == 0:
                rows = jnp.where(row256 < 4, f[:8], roll(e[:8], 4, 0))
            else:
                rows = jnp.where(row256 >= 4, f[8:], roll(e[8:], 4, 0))
            s["sy"][ys, x] = rows
            for zs in range(2):
                turned = roll(rows[:, 128 * zs : 128 * zs + 128], 16 * x + 16 * zs, 1)
                tiles[zs] = jnp.where(share8 == x, turned, tiles[zs])
        for zs in range(2):
            s["syz"][ys, zs] = tiles[zs]

    row8 = iota((8, 256), 0)
    for xs in range(2):
        one, two = (0, 1) if xs == 0 else (7, 6)
        near = slice(0, 1), slice(15, 16)
        s["ey"][xs, 0] = jnp.where(
            (row8 == 2) | (row8 == 3), roll(s["sy"][0, two], -2, 0), s["sy"][0, one]
        )
        s["ey"][xs, 1] = jnp.where(
            (row8 == 4) | (row8 == 5), roll(s["sy"][1, two], 2, 0), s["sy"][1, one]
        )
        s["ez"][xs, 0] = jnp.where(
            (lane128 >= 32) & (lane128 < 64), roll(mixed(0, two), -32, 1), mixed(0, one)
        )
        s["ez"][xs, 1] = jnp.where(
            (lane128 >= 64) & (lane128 < 96), roll(mixed(1, two), 32, 1), mixed(1, one)
        )
        for ys in range(2):
            s["ec"][xs, ys, 0] = e_in[one, near[ys], :128]
            s["ec"][xs, ys, 1] = e_in[one, near[ys], 128:]

    pl.semaphore_wait(barrier, count(0) * count(1) * count(2) - 1)

    def send(src, dst, name, index, device):
        return pltpu.make_async_remote_copy(
            src_ref=src,
            dst_ref=dst,
            send_sem=s[name + "_s"].at[index],
            recv_sem=s[name + "_r"].at[index],
            device_id=device,
            device_id_type=MESH,
        )

    def cut(dx, n, whole, base):
        if dx == 0:
            return pl.ds(0, whole), pl.ds(base, whole)
        if dx < 0:
            return pl.ds(0, n), pl.ds(base + whole, n)
        return pl.ds(whole - n, n), pl.ds(base - n, n)

    def round0(d):
        dx, dy, dz = d
        index = DIRS.index(d)
        xs, ys, zs = (int(c > 0) for c in d)
        if dy == 0 and dz == 0:
            a, b = cut(dx, 2, 8, 4)
            own = (pl.ds(0, 16), pl.ds(0, 256))
            first = send(f_in.at[a], s["f0"].at[(b, *own)], "c0", index, peer(d))
            a, b = cut(dx, 3, 8, 4)
            second = send(e_in.at[a], s["e0"].at[(b, *own)], "c0", 26 + (dx > 0), peer(d))
            return [first, second]
        if dx and dy and dz:
            source, target = s["ec"].at[xs, ys, zs], s["rec"].at[1 - xs, 1 - ys, 1 - zs]
        elif dx and dy:
            source, target = s["ey"].at[xs, ys], s["rey"].at[1 - xs, 1 - ys]
        elif dx:
            source, target = s["ez"].at[xs, zs], s["rez"].at[1 - xs, 1 - zs]
        elif dy and dz:
            source, target = s["syz"].at[ys, zs], s["ryz"].at[1 - ys, 1 - zs]
        elif dy:
            source, target = s["sy"].at[ys], s["ry"].at[1 - ys]
        else:
            source, target = s["sz"].at[zs], s["rz"].at[1 - zs]
        return [send(source, target, "c0", index, peer(d))]

    def iterate0(d):
        dx, dy, dz = d
        xs, ys, zs = (int(c > 0) for c in d)
        name = "v" + "x" * (dx != 0) + "y" * (dy != 0) + "z" * (dz != 0)
        slot = tuple(1 - i for i, c in zip((xs, ys, zs), d) if c)
        if dx and not dy:
            wide = 1 if dz else 2
            x = pl.ds(12 - wide if dx > 0 else 4, wide)
            lanes = pl.ds(128 * zs, 128) if dz else pl.ds(0, 256)
            source = s["b0"].at[x, pl.ds(0, 16), lanes]
        else:
            source = s["p" + name].at[tuple(1 - i for i in slot)]
        return [send(source, s[name].at[slot], "v0", EDGES.index(d), peer(d))]

    def pack_iterate0():
        row = iota((8, 256), 0)
        row_c = iota((8, 128), 0)
        for zs in range(2):
            tile = jnp.zeros((16, 128), F32)
            for k in range(8):
                v = s["b0"][4 + k, :16, 128 * zs : 128 * zs + 128]
                tile = jnp.where(share == k, roll(v, 16 * k + 16 * zs, 1), tile)
            s["pvz"][zs] = tile
        for ys in range(2):
            corner = jnp.zeros((8, 256), F32)
            tiles = [jnp.zeros((8, 256), F32)] * 2
            for k in range(8):
                v = s["b0"][4 + k, 8 * ys : 8 * ys + 8, :256]
                j = k & 3
                tiles[k >> 2] = jnp.where(
                    (row >> 1) == j, roll(v, 2 * j + 2 * ys, 0), tiles[k >> 2]
                )
                corner = jnp.where(row == k, roll(v, k + ys, 0), corner)
            s["pvy"][ys, 0], s["pvy"][ys, 1] = tiles
            s["pvyz"][ys, 0], s["pvyz"][ys, 1] = corner[:, :128], corner[:, 128:]
            near = slice(15, 16) if ys else slice(0, 1)
            s["pvxy"][0, ys] = s["b0"][4, near, :256]
            s["pvxy"][1, ys] = s["b0"][11, near, :256]

    def shrink(name, slab):
        width = slab(0).shape[1]
        row = iota((8, width), 0)
        for xs in range(2):
            one, two, three = (slab(k if xs == 0 else 3 - k) for k in range(3))
            tile = jnp.where(row >= 3, roll(two, 3, 0), one)
            s[name][xs, 0] = jnp.where(row >= 5, roll(three, 5, 0), tile)
            tile = jnp.where(row <= 4, roll(two, -3, 0), one)
            s[name][xs, 1] = jnp.where(row <= 2, roll(three, -5, 0), tile)

    def grow(tile, ys, distance):
        shift = (0, 3, 5)[distance - 1]
        return roll(tile, -shift if ys else shift, 0) if shift else tile

    def block1(name, wide):
        def copies(d):
            dx, dy, dz = d
            index = DIRS.index(d)
            if dx and dy:
                xs, ys = int(dx > 0), int(dy > 0)
                source, target = s["p" + name].at[xs, ys], s["r" + name].at[1 - xs, 1 - ys, 1 - dz]
                return [send(source, target, name, index, peer(d))]
            a, b = cut(dx, wide, 4, 4)
            own = pl.ds(4 + a.start, a.size)
            slot = (1 - dy) * 3 + 1 - dz
            buffer = s[name]
            return [send(buffer.at[4, own], buffer.at[slot, b], name, index, peer(d))]

        return copies

    def narrow1(d):
        dx, dy, dz = d
        xs, ys, zs = (int(c > 0) for c in d)
        if dy:
            source, target = s["ny"].at[xs, ys], s["rny"].at[1 - xs, 1 - ys, 1 - dz]
        elif dz:
            source, target = s["nz"].at[xs, zs], s["rnz"].at[1 - xs, 1 - zs]
        else:
            source, target = s["f1b"].at[4, pl.ds(6 if xs else 4, 2)], s["rn"].at[1 - xs]
        return [send(source, target, "n1", ASIDE.index(d), peer(d))]

    def flat1(d):
        dx, dy = d
        if dx and dy:
            xs, ys = int(dx > 0), int(dy > 0)
            source, target = s["pv1"].at[xs, ys], s["rv1"].at[1 - xs, 1 - ys]
            return [send(source, target, "v1", FLAT.index(d), peer(d))]
        a, b = cut(dx, 4, 4, 4)
        own = pl.ds(4 + a.start, a.size)
        return [send(s["v1"].at[1, own], s["v1"].at[1 - dy, b], "v1", FLAT.index(d), peer(d))]

    def start_all(dirs, copies):
        for d in dirs:

            @pl.when(there(d))
            def _(d=d):
                for copy in copies(d):
                    copy.start()

    def arrive_all(dirs, copies):
        for d in dirs:

            @pl.when(there(flip(d)))
            def _(d=d):
                for copy in copies(d):
                    copy.wait_recv()

    def leave_all(dirs, copies):
        for d in dirs:

            @pl.when(there(d))
            def _(d=d):
                for copy in copies(d):
                    copy.wait_send()

    def step_away(g, c, far):
        return (g + far * c >= 0) & (g + far * c < 8) if c else True

    def found(d, far):
        return jnp.logical_and(step_away(gx, d[0], far), step_away(gy, d[1], far))

    def tell(index, device):
        pl.semaphore_signal(s["tell"].at[index], inc=1, device_id=device, device_id_type=MESH)

    def tell_around(index, far):
        for d in FLAT:
            device = (gx + far * d[0], gy + far * d[1], gz)
            pl.when(found(d, far))(functools.partial(tell, index, device))

    def told_around(index, far):
        told = [found(d, far).astype(jnp.int32) for d in FLAT]
        pl.semaphore_wait(s["tell"].at[index], functools.reduce(jnp.add, told))

    def tell_plane():
        for device in ((gx ^ 4, gy, gz), (gx, gy ^ 4, gz), (gx ^ 4, gy ^ 4, gz)):
            tell(2, device)

    def all_told():
        pl.semaphore_wait(s["tell"].at[2], 3)

    far = 1 - (gx >> 2)

    def column_device(c):
        return (c >> 2, ((c & 3) << 1) + core, gz)

    def gather_start(name):
        mine = s[name].at[core, column]

        def one(k, carry):
            send(mine, mine, name, 1, column_device(16 * far + ((column + k) & 15))).start()
            return carry

        def other(k, carry):
            send(mine, mine, name, 0, column_device(16 * (1 - far) + ((column + k) & 15))).start()
            return carry

        lax.fori_loop(0, 16, one, 0)
        lax.fori_loop(1, 16, other, 0)

    def gathered(name, part):
        block = s[name].at[core, pl.ds(0, 15 + part)]
        return send(block, block, name, part, sibling)

    def handed(name, part, side):
        half = far if part else 1 - far
        block = s[name].at[side, pl.ds(16 * half, 16)]
        return send(block, block, name, 2 + part, sibling)

    start_all(order, round0)
    tell_around(0, 1)

    s["my1"][...] = pair_rows(2, 8, 0.5)
    s["mz1"][...] = restrict_z(128, 256, 64, 128, 1.0)
    s["my2"][...] = pair_rows(1, 32, 0.5)
    s["mz2"][...] = restrict_z(64, 128, 32, 128, 1.0)
    s["pz3"][...] = prolong_z(32, 128, 64, 128)
    s["py3"][...] = prolong_y(16, 16, 32, 32)
    s["pz2"][...] = prolong_z(64, 128, 128, 256)
    fine = place(iota((16, 32), 0), 8, 16) + 8 * gy
    s["py2"][...] = spread(iota((16, 32), 1), fine)
    s["pz1"][...] = prolong_z(128, 256, 256, 384)
    s["py1"][...] = prolong_y(8, 16, 16, 24)

    def inside(shape, own, index, total, axis):
        p = place(iota(shape, axis), own, shape[axis]) + own * index
        return (p >= 0) & (p < total)

    def x_inside(x, own, total):
        p = x + own * gx
        return (p >= 0) & (p < total)

    def mask(shape, own_y, own_z, total_y, total_z):
        return inside(shape, own_y, gy, total_y, 0) & inside(shape, own_z, gz, total_z, 1)

    def both(a, flag):
        return jnp.logical_and(a, jnp.broadcast_to(flag, a.shape))

    def beside(v, cx_low, cx, cy, cz, low, high):
        total = cx_low * low + cx * high
        total = total + cy * roll(v, -1, 0) + roll(cy * v, 1, 0)
        return total + cz * roll(v, -1, 1) + roll(cz * v, 1, 1)

    arrive_all(LEVEL, round0)
    told_around(0, 1)
    tell_around(1, 2)
    s["my0"][...] = pair_rows(4, 16, 0.5)
    s["mz0"][...] = restrict_z(256, 256, 128, 128, 1.0)
    for k in range(4):
        s["rs0"][16 * k : 16 * k + 16] = e_in[2 * k] + e_in[2 * k + 1]
    own_e1 = (dot(dot(s["my0"][...], s["rs0"][...]), s["mz0"][...]) * 0.25).reshape(4, 8, 128)
    s["e1"][4, 4:8] = own_e1
    shrink("pe1", lambda k: own_e1[k])
    start_all(order, block1("e1", 4))
    m0 = mask((24, 384), 16, 256, NY, NZ)
    ones0 = jnp.ones((24, 384), F32)
    low_lane = iota((16, 128), 1) < 64
    low_lane8 = iota((8, 128), 1) < 64
    low_row = iota((8, 256), 0) < 4
    low_row8 = iota((8, 128), 0) < 4

    def fill(x):
        m = both(m0, x_inside(x - 4, 8, NX))
        if 4 <= x < 12:
            distance, xs, f_own, e_own = 0, 0, f_in[x - 4], e_in[x - 4]
            k = x - 4
            y0, y1 = s["ry"][0, k], s["ry"][1, k]
            z0, z1 = s["rz"][0], s["rz"][1]
            f_z = jnp.where(low_lane, roll(z1, -16 * k, 1), roll(z0, -16 * k - 8, 1))
            e_z = jnp.where(low_lane, roll(z1, -16 * k - 8, 1), roll(z0, -16 * k - 16, 1))
        else:
            xs, distance = (0, 4 - x) if x < 4 else (1, x - 11)
            f_own, e_own = s["f0"][x, :16, :256], s["e0"][x, :16, :256]
            if distance == 3:
                e = jnp.concatenate([e_own, jnp.ones((16, 128), F32)], 1)
                e = jnp.concatenate([e, jnp.ones((8, 384), F32)], 0)
                s["e0"][x] = 1.0 / jnp.where(m, e, 1.0)
                return
            z0, z1, y0, y1 = s["rez"][xs, 0], s["rez"][xs, 1], s["rey"][xs, 0], s["rey"][xs, 1]
            if distance == 2:
                z0, z1, y0, y1 = roll(z0, -32, 1), roll(z1, 32, 1), roll(y0, -2, 0), roll(y1, 2, 0)
        if distance:
            f_z = jnp.where(low_lane, z1, z0)
            e_z = roll(jnp.where(low_lane, z0, z1), 64, 1)
        f_y = jnp.where(low_row, y1, y0)
        e_y = roll(jnp.where(low_row, y0, y1), 4, 0)
        f_c = jnp.zeros((8, 128), F32)
        e_c = jnp.ones((8, 128), F32)
        if distance == 0:
            c0, c1 = (
                jnp.where(
                    low_lane8,
                    roll(s["ryz"][i, 1], -16 * k, 1),
                    roll(s["ryz"][i, 0], -16 * k - 16, 1),
                )
                for i in range(2)
            )
            f_c = jnp.where(low_row8, c1, c0)
            e_c = roll(jnp.where(low_row8, c0, c1), 4, 0)
        elif distance == 1:
            c = s["rec"]
            c0 = jnp.where(low_lane8, c[xs, 0, 1], c[xs, 0, 0])
            c1 = jnp.where(low_lane8, c[xs, 1, 1], c[xs, 1, 0])
            e_c = jnp.where(low_row8, c1, c0)

        f, e = join(f_own, f_z, f_y, f_c), join(e_own, e_z, e_y, e_c)
        s["f0"][x] = jnp.where(m, f, 0.0) * FOURPI
        s["e0"][x] = 1.0 / jnp.where(m, e, 1.0)

    def join(own, z, y, c):
        top = jnp.concatenate([own, z], 1)
        return jnp.concatenate([top, jnp.concatenate([y, c], 1)], 0)

    def faces(here, after):
        return 2.0 / (here + after)

    def lateral(x):
        ic = s["e0"][x]
        cy, cz = faces(ic, roll(ic, -1, 0)), faces(ic, roll(ic, -1, 1))
        s["cy0"][x], s["cz0"][x] = cy, cz
        s["d0"][x] = cy + roll(cy, 1, 0) + cz + roll(cz, 1, 1)

    def along(x):
        s["cx0"][x] = faces(s["e0"][x], s["e0"][x + 1])

    def weigh(x):
        m = both(m0, x_inside(x - 4, 8, NX))
        diagonal = s["d0"][x] + s["cx0"][x] + s["cx0"][x - 1]
        weight = jnp.where(m, OMEGA / diagonal, 0.0)
        s["d0"][x], s["w0"][x] = diagonal, weight
        s["a0"][x] = weight * s["f0"][x]

    def total(level, src, x):
        c = str(level)
        v = s[src][x]
        return v, s["f" + c][x] + beside(
            v, s["cx" + c][x - 1], s["cx" + c][x], s["cy" + c][x], s["cz" + c][x],
            s[src][x - 1], s[src][x + 1],
        )

    def sweeps(level, src, dst, start, stop):
        def one(x, carry):
            v, u = total(level, src, x)
            s[dst][x] = KEEP * v + s[f"w{level}"][x] * u
            return carry

        loop(start, stop, one, 0)

    def residue(level, src, x):
        v, u = total(level, src, x)
        return u - s[f"d{level}"][x] * v

    for x in range(4, 12):
        fill(x)
        lateral(x)
    for x in range(4, 11):
        along(x)
    for x in range(5, 11):
        weigh(x)
    sweeps(0, "a0", "b0", 6, 10)

    arrive_all(aside, round0)
    told_around(1, 2)
    tell_plane()
    for x in (1, 2, 3, 12, 13, 14):
        fill(x)
    for x in (2, 3, 12, 13):
        lateral(x)
    for x in (1, 2, 3, 11, 12, 13):
        along(x)
    for x in (2, 3, 4, 11, 12, 13):
        weigh(x)
    sweeps(0, "a0", "b0", 3, 6)
    sweeps(0, "a0", "b0", 10, 13)

    def pairs0(k, carry):
        r = residue(0, "b0", 4 + 2 * k) + residue(0, "b0", 5 + 2 * k)
        s["rs0"][pl.ds(pl.multiple_of(k * 16, 16), 16)] = r[:16, :256]
        return carry

    loop(0, 4, pairs0, 0)
    own_f1 = dot(dot(s["my0"][...], s["rs0"][...]), s["mz0"][...]).reshape(4, 8, 128)
    s["f1b"][4, 4:8] = own_f1
    lane8 = iota((8, 128), 1)
    for xs in range(2):
        one, two = (own_f1[0], own_f1[1]) if xs == 0 else (own_f1[3], own_f1[2])
        two = roll(two, 64, 1)
        s["nz"][xs, 0] = jnp.where(lane8 < 64, one, two)
        s["nz"][xs, 1] = jnp.where(lane8 >= 64, one, two)
        s["ny"][xs, 0], s["ny"][xs, 1] = one[0:1], one[7:8]
    start_all(aside, narrow1)
    start_all(LEVEL, block1("f1b", 3))
    shrink("pf1b", lambda k: own_f1[k])
    start_all(aside, block1("f1b", 3))
    pack_iterate0()
    start_all(EDGES, iterate0)

    def coefficients(ie, x, m, ic, cx_low):
        inext = ie[x + 1]
        cx = 2.0 / (ic + inext)
        cy = 2.0 / (ic + roll(ic, -1, 0))
        cz = 2.0 / (ic + roll(ic, -1, 1))
        diagonal = cx + cx_low + cy + roll(cy, 1, 0) + cz + roll(cz, 1, 1)
        weight = jnp.where(m, OMEGA / diagonal, 0.0)
        return inext, cx, cy, cz, diagonal, weight

    m1 = mask((16, 256), 8, 128, NY // 2, NZ // 2)

    def join1(name, x, other, reach):
        b = s[name]
        distance = 4 - x if x < 4 else x - 7 if x > 7 else 0

        def across(y):
            tiles = [b[y * 3 + i, x] for i in range(3)]
            if distance and y != 1:
                r, xs, ys = s["r" + name], int(x > 7), int(y == 2)
                tiles = [grow(r[xs, ys, i], ys, distance) for i in range(3)]
            return jnp.concatenate([tiles[1], jnp.where(low_lane8, tiles[2], tiles[0])], 1)

        under = jnp.full((8, 256), other, F32)
        if distance < reach:
            under = jnp.where(low_row, across(2), across(0))
        both_rows = jnp.concatenate([across(1), under], 0)
        return jnp.where(both(m1, x_inside(x - 4, 4, NX // 2)), both_rows, other)

    arrive_all(order, block1("e1", 4))
    for x in range(12):
        e = join1("e1", x, 1.0, 4)
        s["ie1"][x] = 1.0 / e
        if 4 <= x < 8:
            half = (x - 4) // 2 * 8
            if x % 2 == 0:
                s["rs1"][half : half + 8] = e[:8]
            else:
                s["rs1"][half : half + 8] += e[:8]
    s["ge"][core, column] = dot(dot(s["my1"][...], s["rs1"][...]), s["mz1"][...]) * 0.25
    all_told()
    gather_start("ge")
    s["cx1"][0] = 2.0 / (s["ie1"][0] + s["ie1"][1])

    def make1(x, carry):
        ic, cx_low = carry
        m = both(m1, x_inside(x - 4, 4, NX // 2))
        ic, cx, cy, cz, diagonal, weight = coefficients(s["ie1"], x, m, ic, cx_low)
        s["cx1"][x], s["cy1"][x], s["cz1"][x] = cx, cy, cz
        s["d1"][x], s["w1"][x] = diagonal, weight
        return ic, cx

    loop(1, 11, make1, (s["ie1"][1], s["cx1"][0]))

    def beside1(x):
        xs, distance = (0, 4 - x) if x < 4 else (1, x - 7)
        own = s["rn"][xs, distance - 1 if xs else 2 - distance]
        z0, z1 = s["rnz"][xs, 0], s["rnz"][xs, 1]
        around = jnp.where(low_lane8, z1, z0)
        under = jnp.zeros((8, 256), F32)
        if distance == 2:
            around = roll(jnp.where(low_lane8, z0, z1), 64, 1)
        else:
            r = s["rny"]
            rows = [
                jnp.where(low_row8, r[xs, 1, i], r[xs, 0, i]) for i in range(3)
            ]
            under = jnp.concatenate([rows[1], jnp.where(low_lane8, rows[2], rows[0])], 1)
        values = jnp.concatenate([jnp.concatenate([own, around], 1), under], 0)
        return jnp.where(both(m1, x_inside(x - 4, 4, NX // 2)), values, 0.0)

    arrive_all(LEVEL, block1("f1b", 3))
    for x in range(4, 8):
        s["f1"][x] = join1("f1b", x, 0.0, 3)
        s["a1"][x] = s["w1"][x] * s["f1"][x]
    arrive_all(aside, narrow1)
    for x in (2, 3, 8, 9):
        f = beside1(x)
        s["f1"][x] = f
        s["a1"][x] = s["w1"][x] * f
    sweeps(1, "a1", "b1", 3, 9)
    for k in range(2):
        r = residue(1, "b1", 4 + 2 * k) + residue(1, "b1", 5 + 2 * k)
        s["rs1"][8 * k : 8 * k + 8] = r[:8]
    s["gf"][core, column] = dot(dot(s["my1"][...], s["rs1"][...]), s["mz1"][...])
    gather_start("gf")
    for x in range(4, 8):
        s["v1"][1, x] = s["b1"][x, :8]
    shrink("pv1", lambda k: s["v1"][1, 4 + k])
    start_all(FLAT, flat1)

    row8 = iota((8, 128), 0) < 4

    def arrange(name, half, write):
        def one(k, carry):
            k = 16 * half + k
            even, odd = s[name][0, k], s[name][1, k]
            x = 2 * (k >> 2)
            rows = pl.ds(pl.multiple_of((k & 3) * 8, 8), 8)
            write(x + 4, rows, jnp.where(row8, even, roll(odd, 4, 0)))
            write(x + 5, rows, jnp.where(row8, roll(even, 4, 0), odd))
            return carry

        loop(0, 16, one, 0)

    def collect(name, write):
        for part in range(2):
            gathered(name, part).wait_recv()
            handed(name, part, core).start()
        for part in range(2):
            handed(name, part, 1 - core).wait_recv()
            arrange(name, far if part else 1 - far, write)

    def put_e2(x, rows, values):
        s["e2"][x, rows] = values
        s["ie2"][x, rows] = 1.0 / values

    collect("ge", put_e2)
    shape2 = (32, 128)
    last2, first2 = iota(shape2, 0) == 31, iota(shape2, 0) == 0
    in_z2 = inside(shape2, 64, gz, NZ // 4, 1)
    s["ie2"][3] = jnp.ones(shape2, F32)
    s["ie2"][20] = jnp.ones(shape2, F32)

    def edge_faces(ic, first, last):
        cy = 2.0 / (ic + jnp.where(last, 1.0, roll(ic, -1, 0)))
        below = jnp.where(first, 2.0 / (ic + 1.0), roll(cy, 1, 0))
        return cy, below

    s["cx2"][3] = 2.0 / (1.0 + s["ie2"][4])

    def make2(x, carry):
        ic, cx_low = carry
        inext = s["ie2"][x + 1]
        cx = 2.0 / (ic + inext)
        cy, below = edge_faces(ic, first2, last2)
        cz = 2.0 / (ic + roll(ic, -1, 1))
        diagonal = cx + cx_low + cy + below + cz + roll(cz, 1, 1)
        s["cx2"][x], s["cz2"][x] = cx, cz
        s["cy2"][x] = jnp.where(last2, 0.0, cy)
        s["d2"][x] = diagonal
        s["w2"][x] = jnp.where(in_z2, OMEGA / diagonal, 0.0)
        return inext, cx

    loop(4, 20, make2, (s["ie2"][4], s["cx2"][3]))
    for x in range(4):
        for name in ("a2", "b2"):
            s[name][x] = jnp.zeros(shape2, F32)
            s[name][20 + x] = jnp.zeros(shape2, F32)

    def down3(pair):
        def one(k, carry):
            rows = pl.ds(pl.multiple_of(k * 16, 16), 16)
            s["rs3"][rows] = dot(s["my2"][...], pair(k))
            return carry

        loop(0, 8, one, 0)
        return dot(s["rs3"][...], s["mz2"][...]).reshape(8, 16, 128)

    shape3 = (8, 16, 128)
    p3 = place(iota(shape3, 2), 32, 128)
    near3 = (p3 >= -16) & (p3 < 48)
    e3 = down3(lambda k: s["e2"][4 + 2 * k] + s["e2"][5 + 2 * k]) * 0.25
    ie3 = 1.0 / jnp.where(near3, e3, 1.0)
    first3, last3 = iota(shape3, 1) == 0, iota(shape3, 1) == 15
    edge = jnp.ones((1, 16, 128), F32)
    none = jnp.zeros((1, 16, 128), F32)

    def roll3(values, shift, axis):
        return roll(values.reshape(128, 128), shift, 1).reshape(shape3) if axis == 2 else jnp.stack(
            [roll(values[k], shift, 0) for k in range(8)]
        )

    around = jnp.concatenate([edge, ie3, edge], 0)
    cx3 = 2.0 / (around[1:] + around[:-1])
    cy3 = 2.0 / (ie3 + jnp.where(last3, 1.0, roll3(ie3, -1, 1)))
    below3 = jnp.where(first3, 2.0 / (ie3 + 1.0), roll3(cy3, 1, 1))
    cz3 = 2.0 / (ie3 + roll3(ie3, -1, 2))
    d3 = cx3[1:] + cx3[:-1] + cy3 + below3 + cz3 + roll3(cz3, 1, 2)
    q3 = p3 + 32 * gz
    s["w3"][...] = jnp.where((q3 >= 0) & (q3 < NZ // 8), OMEGA / d3, 0.0)
    s["cx3"][...] = cx3
    s["cy3"][...] = jnp.where(last3, 0.0, cy3)
    s["cz3"][...] = cz3

    leave_all(order, round0)
    leave_all(order, block1("e1", 4))
    leave_all(aside, narrow1)
    leave_all(LEVEL, block1("f1b", 3))
    def put_f2(x, rows, values):
        s["f2"][x, rows] = values
        s["a2"][x, rows] = s["w2"][x, rows] * values

    collect("gf", put_f2)
    sweeps(2, "a2", "b2", 4, 20)
    f3 = down3(lambda k: residue(2, "b2", 4 + 2 * k) + residue(2, "b2", 5 + 2 * k))
    s["f3"][...] = f3

    def coarse(_, v):
        cx, cy, cz = s["cx3"][...], s["cy3"][...], s["cz3"][...]
        after = jnp.concatenate([v[1:], none], 0)
        before = jnp.concatenate([none, v[:-1]], 0)
        u = s["f3"][...] + cx[1:] * after + cx[:-1] * before
        u = u + cy * roll3(v, -1, 1) + roll3(cy * v, 1, 1)
        u = u + cz * roll3(v, -1, 2) + roll3(cz * v, 1, 2)
        return KEEP * v + s["w3"][...] * u

    v3 = loop(0, COARSE_SWEEPS - 1, coarse, s["w3"][...] * f3)

    wide = dot(v3.reshape(128, 128), s["pz3"][...]).reshape(8, 16, 128)
    rows3 = [dot(s["py3"][...], wide[k]) for k in range(8)]
    nothing = jnp.zeros(shape2, F32)
    for k in range(8):
        low = rows3[k - 1] if k else nothing
        high = rows3[k + 1] if k < 7 else nothing
        for i, other in ((0, low), (1, high)):
            x = 4 + 2 * k + i
            add = 0.75 * rows3[k] + 0.25 * other
            s["b2"][x] += jnp.where(in_z2, add, 0.0)
    sweeps(2, "b2", "a2", 4, 20)
    sweeps(2, "a2", "b2", 4, 20)

    for k in range(8):
        s["up1"][16 * k : 16 * k + 16] = dot(s["py2"][...], s["b2"][2 * gx + 1 + k])
    up1 = dot(s["up1"][...], s["pz2"][...])
    arrive_all(FLAT, flat1)
    arrive_all(aside, block1("f1b", 3))
    for x in (1, 2, 3, 8, 9, 10):
        s["f1"][x] = join1("f1b", x, 0.0, 3)
    up1 = up1.reshape(8, 16, 256)
    for x in range(12):
        k = (x - 4) // 2 + 3
        other = up1[k - 1] if x % 2 == 0 else up1[k + 1]
        add = 0.75 * up1[k] + 0.25 * other
        distance = 4 - x if x < 4 else x - 7 if x > 7 else 0
        under = jnp.zeros((8, 256), F32)
        if distance == 0:
            under = jnp.where(low_row, s["v1"][2, x], s["v1"][0, x])
        elif distance < 4:
            r = s["rv1"]
            after, before = (grow(r[int(x > 7), ys], ys, distance) for ys in (1, 0))
            under = jnp.where(low_row, after, before)
        v = jnp.concatenate([s["v1"][1, x], under], 0) + add
        s["a1"][x] = jnp.where(both(m1, x_inside(x - 4, 4, NX // 2)), v, 0.0)
    sweeps(1, "a1", "b1", 1, 11)
    sweeps(1, "b1", "a1", 2, 10)

    arrive_all(EDGES, iterate0)

    def whole0(x):
        nothing = [jnp.zeros(shape, F32) for shape in ((16, 128), (8, 256), (8, 128))]
        if 4 <= x < 12:
            k = x - 4
            z = jnp.where(
                low_lane, roll(s["vz"][1], -16 * k, 1), roll(s["vz"][0], -16 * k - 16, 1)
            )
            i, j = k >> 2, 2 * (k & 3)
            y = jnp.where(
                low_row, roll(s["vy"][1, i], -j, 0), roll(s["vy"][0, i], -j - 2, 0)
            )
            c = [jnp.where(low_lane8, s["vyz"][i, 1], s["vyz"][i, 0]) for i in range(2)]
            c = [roll(c[0], -k - 1, 0), roll(c[1], -k, 0)]
            return join(s["b0"][x, :16, :256], z, y, jnp.where(low_row8, c[1], c[0]))
        xs, distance = (0, 4 - x) if x < 4 else (1, x - 11)
        own = s["vx"][xs, 2 - distance if xs == 0 else distance - 1]
        if distance == 2:
            return join(own, *nothing)
        z = jnp.where(low_lane, s["vxz"][xs, 1, 0], s["vxz"][xs, 0, 0])
        y = jnp.where(low_row, s["vxy"][xs, 1], s["vxy"][xs, 0])
        return join(own, z, y, nothing[2])

    for k in range(8):
        s["up0"][24 * k : 24 * k + 24] = dot(s["py1"][...], s["a1"][2 + k])
    up0 = dot(s["up0"][...], s["pz1"][...]).reshape(8, 24, 384)
    for x in range(2, 14):
        k = (x - 4) // 2 + 2
        other = up0[k - 1] if x % 2 == 0 else up0[k + 1]
        add = 0.75 * up0[k] + 0.25 * other
        v = whole0(x) + add
        s["a0"][x] = jnp.where(both(m0, x_inside(x - 4, 8, NX)), v, 0.0)
    sweeps(0, "a0", "g0", 3, 13)

    def finish(x, carry):
        v, u = total(0, "g0", x)
        out[x - 4] = (KEEP * v + s["w0"][x] * u)[:16, :256]
        return carry

    loop(4, 12, finish, 0)

    leave_all(aside, block1("f1b", 3))
    leave_all(FLAT, flat1)
    leave_all(EDGES, iterate0)
    for name in ("ge", "gf"):
        for part in range(2):
            gathered(name, 1 - part).wait_send()
            handed(name, part, core).wait_send()


def buffers():
    def vmem(*shape):
        return pltpu.VMEM(shape, F32)

    def half(*shape):
        return pltpu.VMEM(shape, BF16)

    table = {
        "sz": vmem(2, 16, 128), "rz": vmem(2, 16, 128),
        "sy": vmem(2, 8, 8, 256), "ry": vmem(2, 8, 8, 256),
        "syz": vmem(2, 2, 8, 128), "ryz": vmem(2, 2, 8, 128),
        "ey": vmem(2, 2, 8, 256), "rey": vmem(2, 2, 8, 256),
        "ez": vmem(2, 2, 16, 128), "rez": vmem(2, 2, 16, 128),
        "ec": vmem(2, 2, 2, 1, 128), "rec": vmem(2, 2, 2, 1, 128),
        "vx": vmem(2, 2, 16, 256), "vy": vmem(2, 2, 8, 256), "vz": vmem(2, 16, 128),
        "pvy": vmem(2, 2, 8, 256), "pvz": vmem(2, 16, 128), "pvxy": vmem(2, 2, 1, 256),
        "vxy": vmem(2, 2, 1, 256), "vxz": vmem(2, 2, 1, 16, 128), "vyz": vmem(2, 2, 8, 128),
        "pvyz": vmem(2, 2, 8, 128),
        "pe1": vmem(2, 2, 8, 128), "re1": vmem(2, 2, 3, 8, 128),
        "ny": vmem(2, 2, 1, 128), "rny": vmem(2, 2, 3, 1, 128),
        "nz": vmem(2, 2, 8, 128), "rnz": vmem(2, 2, 8, 128), "rn": vmem(2, 2, 8, 128),
        "pf1b": vmem(2, 2, 8, 128), "rf1b": vmem(2, 2, 3, 8, 128),
        "pv1": vmem(2, 2, 8, 256), "rv1": vmem(2, 2, 8, 256), "g0": vmem(16, 24, 384),
        "e1": vmem(9, 12, 8, 128), "f1b": vmem(9, 12, 8, 128), "v1": vmem(3, 12, 8, 256),
        "ge": vmem(2, 32, 8, 128), "gf": vmem(2, 32, 8, 128),
        "my0": vmem(32, 64), "mz0": half(256, 128), "my1": vmem(8, 16), "mz1": half(256, 128),
        "my2": vmem(16, 32), "mz2": half(128, 128), "pz3": half(128, 128), "py3": vmem(32, 16),
        "pz2": half(128, 256), "py2": vmem(16, 32), "pz1": half(256, 384), "py1": vmem(24, 16),
        "rs0": vmem(64, 256), "rs1": vmem(16, 256), "rs3": vmem(128, 128),
        "up1": vmem(128, 128), "up0": vmem(192, 256),
        "ie1": vmem(12, 16, 256), "e2": vmem(24, 32, 128), "ie2": vmem(24, 32, 128),
        "f3": vmem(8, 16, 128), "w3": vmem(8, 16, 128), "cx3": vmem(9, 16, 128),
        "cy3": vmem(8, 16, 128), "cz3": vmem(8, 16, 128),
    }
    shapes = {"0": (16, 24, 384), "1": (12, 16, 256), "2": (24, 32, 128)}
    for level, shape in shapes.items():
        for name in ("f", "cx", "cy", "cz", "d", "w", "a", "b"):
            table[name + level] = vmem(*shape)
    table["f_in"], table["e_in"] = vmem(8, 16, 256), vmem(8, 16, 256)
    table["tell"] = pltpu.SemaphoreType.REGULAR((3,))
    table["in_s"] = pltpu.SemaphoreType.DMA((2,))
    table["e0"] = vmem(16, 24, 384)
    for name, number in (("c0", 28), ("v0", 18), ("n1", 18), ("e1", 26), ("f1b", 26), ("v1", 8), ("ge", 4), ("gf", 4)):
        table[name + "_s"] = pltpu.SemaphoreType.DMA((number,))
        table[name + "_r"] = pltpu.SemaphoreType.DMA((number,))
    return table


NAMES = list(buffers())


def on_device(charge, dielectric):
    return pl.pallas_call(
        lambda f, e, o, *s: kernel(f, e, o, s),
        out_shape=jax.ShapeDtypeStruct((8, 16, 256), F32),
        in_specs=[pl.BlockSpec(memory_space=pltpu.HBM)] * 2,
        out_specs=pl.BlockSpec(memory_space=pltpu.VMEM),
        scratch_shapes=list(buffers().values()),
        compiler_params=pltpu.CompilerParams(
            collective_id=0, has_side_effects=True, vmem_limit_bytes=60 * 2**20
        ),
    )(charge, dielectric)


def solution(mesh):
    placed = (P("gx", "gy", "gz"), P("gx", "gy", "gz"))
    return jax.shard_map(
        on_device, mesh=mesh, in_specs=placed, out_specs=P("gx", "gy", "gz"), check_vma=False
    )
```

```python
import functools
import itertools
import math

import jax
import jax.numpy as jnp
from jax import lax
from jax.experimental import pallas as pl
from jax.experimental.pallas import tpu as pltpu
from jax.sharding import PartitionSpec as P

MESH = pl.DeviceIdType.MESH
F32 = jnp.float32
BF16 = jnp.bfloat16
OMEGA = 0.8
KEEP = 1.0 - OMEGA
FOURPI = 4.0 * math.pi
COARSE_SWEEPS = 8
NX, NY, NZ = 64, 128, 1024
GX, GY, GZ = 8, 8, 4
DIRS = [d for d in itertools.product((-1, 0, 1), repeat=3) if d != (0, 0, 0)]
ASIDE = [d for d in DIRS if d[0]]
LEVEL = [d for d in DIRS if not d[0]]
EDGES = [d for d in DIRS if 0 in d]
FLAT = [d for d in itertools.product((-1, 0, 1), repeat=2) if d != (0, 0)]


def loop(start, stop, body, init):
    return lax.fori_loop(start, stop, body, init, unroll=True)


def roll(values, shift, axis):
    return pltpu.roll(values, shift % values.shape[axis], axis)


def halves(values):
    high = values.astype(BF16)
    return high, (values - high.astype(F32)).astype(BF16)


def dot(a, b):
    if b.dtype == BF16:
        high, low = halves(a)
        return jnp.dot(high, b, preferred_element_type=F32) + jnp.dot(
            low, b, preferred_element_type=F32
        )
    high, low = halves(b)
    a = a.astype(BF16)
    return jnp.dot(a, high, preferred_element_type=F32) + jnp.dot(
        a, low, preferred_element_type=F32
    )


def place(index, own, size):
    half = (size - own) // 2
    return jnp.where(index < own + half, index, index - size)


def iota(shape, axis):
    return lax.broadcasted_iota(jnp.int32, shape, axis)


def restrict_z(own, size, out_own, out_size, weight):
    shape = (size, out_size)
    p = place(iota(shape, 0), own, size)
    q = place(iota(shape, 1), out_own, out_size)
    return jnp.where((p >> 1) == q, weight, 0.0).astype(BF16)


def pair_rows(groups, own, weight):
    shape = (groups * own // 2, groups * own)
    return jnp.where((iota(shape, 1) >> 1) == iota(shape, 0), weight, 0.0).astype(F32)


def spread(q, p):
    parent = p >> 1
    other = jnp.where((p & 1) == 0, parent - 1, parent + 1)
    return jnp.where(q == parent, 0.75, jnp.where(q == other, 0.25, 0.0)).astype(F32)


def prolong_z(own, size, out_own, out_size):
    shape = (size, out_size)
    weights = spread(place(iota(shape, 0), own, size), place(iota(shape, 1), out_own, out_size))
    return weights.astype(BF16)


def prolong_y(own, size, out_own, out_size):
    shape = (out_size, size)
    return spread(place(iota(shape, 1), own, size), place(iota(shape, 0), out_own, out_size))


def kernel(f_hbm, e_hbm, out, s):
    s = dict(zip(NAMES, s, strict=True))
    f_in, e_in = s["f_in"], s["e_in"]
    loads = [
        pltpu.make_async_copy(f_hbm, f_in, s["in_s"].at[0]),
        pltpu.make_async_copy(e_hbm, e_in, s["in_s"].at[1]),
    ]
    for load in loads:
        load.start()
    gx, gy, gz = (lax.axis_index(a) for a in ("gx", "gy", "gz"))
    core = gy & 1
    column = gx * 4 + (gy >> 1)
    has = [
        {-1: gx > 0, 0: True, 1: gx < GX - 1},
        {-1: gy > 0, 0: True, 1: gy < GY - 1},
        {-1: gz > 0, 0: True, 1: gz < GZ - 1},
    ]

    def there(d):
        found = [has[i][c] for i, c in enumerate(d) if c]
        return functools.reduce(jnp.logical_and, found)

    def peer(d):
        return (gx + d[0], gy + d[1], gz + (d[2] if len(d) > 2 else 0))

    def flip(d):
        return tuple(-c for c in d)

    sibling = (gx, gy + 1 - 2 * core, gz)

    barrier = pltpu.get_barrier_semaphore()

    def greet(device):
        pl.semaphore_signal(barrier, inc=1, device_id=device, device_id_type=MESH)

    order = sorted(DIRS, key=lambda d: (-abs(d[0]), abs(d[1]) + abs(d[2])))
    aside = [d for d in order if d[0]]
    for d in order:
        pl.when(there(d))(functools.partial(greet, peer(d)))

    def count(i):
        return 1 + has[i][-1].astype(jnp.int32) + has[i][1].astype(jnp.int32)

    lane128 = iota((16, 128), 1)
    row256 = iota((8, 256), 0)

    def mixed(side, x):
        f, e = f_in[x], e_in[x]
        if side == 0:
            return jnp.where(lane128 < 64, f[:, :128], roll(e[:, :128], 64, 1))
        return jnp.where(lane128 >= 64, f[:, 128:], roll(e[:, 128:], 64, 1))

    for load in loads:
        load.wait()
    share, within = lane128 >> 4, lane128 & 15
    share8 = iota((8, 128), 1) >> 4
    for zs in range(2):
        tile = jnp.zeros((16, 128), F32)
        lanes = slice(128 * zs, 128 * zs + 128)
        for x in range(8):
            f, e = f_in[x][:, lanes], e_in[x][:, lanes]
            f, e = roll(f, 16 * x + 8 * zs, 1), roll(e, 16 * x + 8 + 8 * zs, 1)
            tile = jnp.where(share == x, jnp.where(within < 8, f, e), tile)
        s["sz"][zs] = tile
    for ys in range(2):
        tiles = [jnp.zeros((8, 128), F32)] * 2
        for x in range(8):
            f, e = f_in[x], e_in[x]
            if ys == 0:
                rows = jnp.where(row256 < 4, f[:8], roll(e[:8], 4, 0))
            else:
                rows = jnp.where(row256 >= 4, f[8:], roll(e[8:], 4, 0))
            s["sy"][ys, x] = rows
            for zs in range(2):
                turned = roll(rows[:, 128 * zs : 128 * zs + 128], 16 * x + 16 * zs, 1)
                tiles[zs] = jnp.where(share8 == x, turned, tiles[zs])
        for zs in range(2):
            s["syz"][ys, zs] = tiles[zs]

    row8 = iota((8, 256), 0)
    for xs in range(2):
        one, two = (0, 1) if xs == 0 else (7, 6)
        near = slice(0, 1), slice(15, 16)
        s["ey"][xs, 0] = jnp.where(
            (row8 == 2) | (row8 == 3), roll(s["sy"][0, two], -2, 0), s["sy"][0, one]
        )
        s["ey"][xs, 1] = jnp.where(
            (row8 == 4) | (row8 == 5), roll(s["sy"][1, two], 2, 0), s["sy"][1, one]
        )
        s["ez"][xs, 0] = jnp.where(
            (lane128 >= 32) & (lane128 < 64), roll(mixed(0, two), -32, 1), mixed(0, one)
        )
        s["ez"][xs, 1] = jnp.where(
            (lane128 >= 64) & (lane128 < 96), roll(mixed(1, two), 32, 1), mixed(1, one)
        )
        for ys in range(2):
            s["ec"][xs, ys, 0] = e_in[one, near[ys], :128]
            s["ec"][xs, ys, 1] = e_in[one, near[ys], 128:]

    pl.semaphore_wait(barrier, count(0) * count(1) * count(2) - 1)

    def send(src, dst, name, index, device):
        return pltpu.make_async_remote_copy(
            src_ref=src,
            dst_ref=dst,
            send_sem=s[name + "_s"].at[index],
            recv_sem=s[name + "_r"].at[index],
            device_id=device,
            device_id_type=MESH,
        )

    def cut(dx, n, whole, base):
        if dx == 0:
            return pl.ds(0, whole), pl.ds(base, whole)
        if dx < 0:
            return pl.ds(0, n), pl.ds(base + whole, n)
        return pl.ds(whole - n, n), pl.ds(base - n, n)

    def round0(d):
        dx, dy, dz = d
        index = DIRS.index(d)
        xs, ys, zs = (int(c > 0) for c in d)
        if dy == 0 and dz == 0:
            a, b = cut(dx, 2, 8, 4)
            own = (pl.ds(0, 16), pl.ds(0, 256))
            first = send(f_in.at[a], s["f0"].at[(b, *own)], "c0", index, peer(d))
            a, b = cut(dx, 3, 8, 4)
            second = send(e_in.at[a], s["e0"].at[(b, *own)], "c0", 26 + (dx > 0), peer(d))
            return [first, second]
        if dx and dy and dz:
            source, target = s["ec"].at[xs, ys, zs], s["rec"].at[1 - xs, 1 - ys, 1 - zs]
        elif dx and dy:
            source, target = s["ey"].at[xs, ys], s["rey"].at[1 - xs, 1 - ys]
        elif dx:
            source, target = s["ez"].at[xs, zs], s["rez"].at[1 - xs, 1 - zs]
        elif dy and dz:
            source, target = s["syz"].at[ys, zs], s["ryz"].at[1 - ys, 1 - zs]
        elif dy:
            source, target = s["sy"].at[ys], s["ry"].at[1 - ys]
        else:
            source, target = s["sz"].at[zs], s["rz"].at[1 - zs]
        return [send(source, target, "c0", index, peer(d))]

    def iterate0(d):
        dx, dy, dz = d
        xs, ys, zs = (int(c > 0) for c in d)
        name = "v" + "x" * (dx != 0) + "y" * (dy != 0) + "z" * (dz != 0)
        slot = tuple(1 - i for i, c in zip((xs, ys, zs), d) if c)
        if dx and not dy:
            wide = 1 if dz else 2
            x = pl.ds(12 - wide if dx > 0 else 4, wide)
            lanes = pl.ds(128 * zs, 128) if dz else pl.ds(0, 256)
            source = s["b0"].at[x, pl.ds(0, 16), lanes]
        else:
            source = s["p" + name].at[tuple(1 - i for i in slot)]
        return [send(source, s[name].at[slot], "v0", EDGES.index(d), peer(d))]

    def pack_iterate0():
        row = iota((8, 256), 0)
        row_c = iota((8, 128), 0)
        for zs in range(2):
            tile = jnp.zeros((16, 128), F32)
            for k in range(8):
                v = s["b0"][4 + k, :16, 128 * zs : 128 * zs + 128]
                tile = jnp.where(share == k, roll(v, 16 * k + 16 * zs, 1), tile)
            s["pvz"][zs] = tile
        for ys in range(2):
            corner = jnp.zeros((8, 256), F32)
            tiles = [jnp.zeros((8, 256), F32)] * 2
            for k in range(8):
                v = s["b0"][4 + k, 8 * ys : 8 * ys + 8, :256]
                j = k & 3
                tiles[k >> 2] = jnp.where(
                    (row >> 1) == j, roll(v, 2 * j + 2 * ys, 0), tiles[k >> 2]
                )
                corner = jnp.where(row == k, roll(v, k + ys, 0), corner)
            s["pvy"][ys, 0], s["pvy"][ys, 1] = tiles
            s["pvyz"][ys, 0], s["pvyz"][ys, 1] = corner[:, :128], corner[:, 128:]
            near = slice(15, 16) if ys else slice(0, 1)
            s["pvxy"][0, ys] = s["b0"][4, near, :256]
            s["pvxy"][1, ys] = s["b0"][11, near, :256]

    def shrink(name, slab):
        width = slab(0).shape[1]
        row = iota((8, width), 0)
        for xs in range(2):
            one, two, three = (slab(k if xs == 0 else 3 - k) for k in range(3))
            tile = jnp.where(row >= 3, roll(two, 3, 0), one)
            s[name][xs, 0] = jnp.where(row >= 5, roll(three, 5, 0), tile)
            tile = jnp.where(row <= 4, roll(two, -3, 0), one)
            s[name][xs, 1] = jnp.where(row <= 2, roll(three, -5, 0), tile)

    def grow(tile, ys, distance):
        shift = (0, 3, 5)[distance - 1]
        return roll(tile, -shift if ys else shift, 0) if shift else tile

    def pair(name, slab):
        half = iota((8, slab(0).shape[1]), 0) >= 4
        for xs in range(2):
            from_edge = [slab(k if xs == 0 else 3 - k) for k in range(4)]
            for t in range(2):
                one, two = from_edge[2 * t], roll(from_edge[2 * t + 1], 4, 0)
                s[name][xs, 0, t] = jnp.where(half, two, one)
                s[name][xs, 1, t] = jnp.where(half, one, two)

    def part(tiles, distance):
        tile = tiles[(distance - 1) >> 1]
        return tile if distance & 1 else roll(tile, 4, 0)

    def block1(name, wide):
        def copies(d):
            dx, dy, dz = d
            index = DIRS.index(d)
            if dx and dy:
                xs, ys = int(dx > 0), int(dy > 0)
                source, target = s["p" + name].at[xs, ys], s["r" + name].at[1 - xs, 1 - ys, 1 - dz]
                return [send(source, target, name, index, peer(d))]
            a, b = cut(dx, wide, 4, 4)
            own = pl.ds(4 + a.start, a.size)
            slot = (1 - dy) * 3 + 1 - dz
            buffer = s[name]
            return [send(buffer.at[4, own], buffer.at[slot, b], name, index, peer(d))]

        return copies

    def narrow1(d):
        dx, dy, dz = d
        xs, ys, zs = (int(c > 0) for c in d)
        if dy:
            source, target = s["ny"].at[xs, ys], s["rny"].at[1 - xs, 1 - ys, 1 - dz]
        elif dz:
            source, target = s["nz"].at[xs, zs], s["rnz"].at[1 - xs, 1 - zs]
        else:
            source, target = s["f1b"].at[4, pl.ds(6 if xs else 4, 2)], s["rn"].at[1 - xs]
        return [send(source, target, "n1", ASIDE.index(d), peer(d))]

    def flat1(d):
        dx, dy = d
        if dx and dy:
            xs, ys = int(dx > 0), int(dy > 0)
            source, target = s["pv1"].at[xs, ys], s["rv1"].at[1 - xs, 1 - ys]
            return [send(source, target, "v1", FLAT.index(d), peer(d))]
        a, b = cut(dx, 4, 4, 4)
        own = pl.ds(4 + a.start, a.size)
        return [send(s["v1"].at[1, own], s["v1"].at[1 - dy, b], "v1", FLAT.index(d), peer(d))]

    def start_all(dirs, copies):
        for d in dirs:

            @pl.when(there(d))
            def _(d=d):
                for copy in copies(d):
                    copy.start()

    def arrive_all(dirs, copies):
        for d in dirs:

            @pl.when(there(flip(d)))
            def _(d=d):
                for copy in copies(d):
                    copy.wait_recv()

    def leave_all(dirs, copies):
        for d in dirs:

            @pl.when(there(d))
            def _(d=d):
                for copy in copies(d):
                    copy.wait_send()

    def step_away(g, c, far):
        return (g + far * c >= 0) & (g + far * c < 8) if c else True

    def found(d, far):
        return jnp.logical_and(step_away(gx, d[0], far), step_away(gy, d[1], far))

    def tell(index, device):
        pl.semaphore_signal(s["tell"].at[index], inc=1, device_id=device, device_id_type=MESH)

    def tell_around(index, far):
        for d in FLAT:
            device = (gx + far * d[0], gy + far * d[1], gz)
            pl.when(found(d, far))(functools.partial(tell, index, device))

    def told_around(index, far):
        told = [found(d, far).astype(jnp.int32) for d in FLAT]
        pl.semaphore_wait(s["tell"].at[index], functools.reduce(jnp.add, told))

    def tell_plane():
        for device in ((gx ^ 4, gy, gz), (gx, gy ^ 4, gz), (gx ^ 4, gy ^ 4, gz)):
            tell(2, device)

    def all_told():
        pl.semaphore_wait(s["tell"].at[2], 3)

    far = 1 - (gx >> 2)

    def column_device(c):
        return (c >> 2, ((c & 3) << 1) + core, gz)

    def gather_start(name):
        mine = s[name].at[core, column]

        def one(k, carry):
            send(mine, mine, name, 1, column_device(16 * far + ((column + k) & 15))).start()
            return carry

        def other(k, carry):
            send(mine, mine, name, 0, column_device(16 * (1 - far) + ((column + k) & 15))).start()
            return carry

        lax.fori_loop(0, 16, one, 0)
        lax.fori_loop(1, 16, other, 0)

    def gathered(name, part):
        block = s[name].at[core, pl.ds(0, 15 + part)]
        return send(block, block, name, part, sibling)

    def handed(name, part, side):
        half = far if part else 1 - far
        block = s[name].at[side, pl.ds(16 * half, 16)]
        return send(block, block, name, 2 + part, sibling)

    start_all(order, round0)
    tell_around(0, 1)

    s["my1"][...] = pair_rows(2, 8, 0.5)
    s["mz1"][...] = restrict_z(128, 256, 64, 128, 1.0)
    s["my2"][...] = pair_rows(1, 32, 0.5)
    s["mz2"][...] = restrict_z(64, 128, 32, 128, 1.0)
    s["pz3"][...] = prolong_z(32, 128, 64, 128)
    s["py3"][...] = prolong_y(16, 16, 32, 32)
    s["pz2"][...] = prolong_z(64, 128, 128, 256)
    fine = place(iota((16, 32), 0), 8, 16) + 8 * gy
    s["py2"][...] = spread(iota((16, 32), 1), fine)
    s["pz1"][...] = prolong_z(128, 256, 256, 384)
    s["py1"][...] = prolong_y(8, 16, 16, 24)

    def inside(shape, own, index, total, axis):
        p = place(iota(shape, axis), own, shape[axis]) + own * index
        return (p >= 0) & (p < total)

    def x_inside(x, own, total):
        p = x + own * gx
        return (p >= 0) & (p < total)

    def mask(shape, own_y, own_z, total_y, total_z):
        return inside(shape, own_y, gy, total_y, 0) & inside(shape, own_z, gz, total_z, 1)

    def both(a, flag):
        return jnp.logical_and(a, jnp.broadcast_to(flag, a.shape))

    def beside(v, cx_low, cx, cy, cz, low, high):
        total = cx_low * low + cx * high
        total = total + cy * roll(v, -1, 0) + roll(cy * v, 1, 0)
        return total + cz * roll(v, -1, 1) + roll(cz * v, 1, 1)

    arrive_all(LEVEL, round0)
    told_around(0, 1)
    tell_around(1, 2)
    s["my0"][...] = pair_rows(4, 16, 0.5)
    s["mz0"][...] = restrict_z(256, 256, 128, 128, 1.0)
    for k in range(4):
        s["rs0"][16 * k : 16 * k + 16] = e_in[2 * k] + e_in[2 * k + 1]
    own_e1 = (dot(dot(s["my0"][...], s["rs0"][...]), s["mz0"][...]) * 0.25).reshape(4, 8, 128)
    s["e1"][4, 4:8] = own_e1
    pair("pe1", lambda k: own_e1[k])
    start_all(order, block1("e1", 4))
    m0 = mask((24, 384), 16, 256, NY, NZ)
    ones0 = jnp.ones((24, 384), F32)
    low_lane = iota((16, 128), 1) < 64
    low_lane8 = iota((8, 128), 1) < 64
    low_row = iota((8, 256), 0) < 4
    low_row8 = iota((8, 128), 0) < 4

    def fill(x):
        m = both(m0, x_inside(x - 4, 8, NX))
        if 4 <= x < 12:
            distance, xs, f_own, e_own = 0, 0, f_in[x - 4], e_in[x - 4]
            k = x - 4
            y0, y1 = s["ry"][0, k], s["ry"][1, k]
            z0, z1 = s["rz"][0], s["rz"][1]
            f_z = jnp.where(low_lane, roll(z1, -16 * k, 1), roll(z0, -16 * k - 8, 1))
            e_z = jnp.where(low_lane, roll(z1, -16 * k - 8, 1), roll(z0, -16 * k - 16, 1))
        else:
            xs, distance = (0, 4 - x) if x < 4 else (1, x - 11)
            f_own, e_own = s["f0"][x, :16, :256], s["e0"][x, :16, :256]
            if distance == 3:
                e = jnp.concatenate([e_own, jnp.ones((16, 128), F32)], 1)
                e = jnp.concatenate([e, jnp.ones((8, 384), F32)], 0)
                s["e0"][x] = 1.0 / jnp.where(m, e, 1.0)
                return
            z0, z1, y0, y1 = s["rez"][xs, 0], s["rez"][xs, 1], s["rey"][xs, 0], s["rey"][xs, 1]
            if distance == 2:
                z0, z1, y0, y1 = roll(z0, -32, 1), roll(z1, 32, 1), roll(y0, -2, 0), roll(y1, 2, 0)
        if distance:
            f_z = jnp.where(low_lane, z1, z0)
            e_z = roll(jnp.where(low_lane, z0, z1), 64, 1)
        f_y = jnp.where(low_row, y1, y0)
        e_y = roll(jnp.where(low_row, y0, y1), 4, 0)
        f_c = jnp.zeros((8, 128), F32)
        e_c = jnp.ones((8, 128), F32)
        if distance == 0:
            c0, c1 = (
                jnp.where(
                    low_lane8,
                    roll(s["ryz"][i, 1], -16 * k, 1),
                    roll(s["ryz"][i, 0], -16 * k - 16, 1),
                )
                for i in range(2)
            )
            f_c = jnp.where(low_row8, c1, c0)
            e_c = roll(jnp.where(low_row8, c0, c1), 4, 0)
        elif distance == 1:
            c = s["rec"]
            c0 = jnp.where(low_lane8, c[xs, 0, 1], c[xs, 0, 0])
            c1 = jnp.where(low_lane8, c[xs, 1, 1], c[xs, 1, 0])
            e_c = jnp.where(low_row8, c1, c0)

        f, e = join(f_own, f_z, f_y, f_c), join(e_own, e_z, e_y, e_c)
        s["f0"][x] = jnp.where(m, f, 0.0) * FOURPI
        s["e0"][x] = 1.0 / jnp.where(m, e, 1.0)

    def join(own, z, y, c):
        top = jnp.concatenate([own, z], 1)
        return jnp.concatenate([top, jnp.concatenate([y, c], 1)], 0)

    def faces(here, after):
        return 2.0 / (here + after)

    def lateral(x):
        ic = s["e0"][x]
        cy, cz = faces(ic, roll(ic, -1, 0)), faces(ic, roll(ic, -1, 1))
        s["cy0"][x], s["cz0"][x] = cy, cz
        s["d0"][x] = cy + roll(cy, 1, 0) + cz + roll(cz, 1, 1)

    def along(x):
        s["cx0"][x] = faces(s["e0"][x], s["e0"][x + 1])

    def weigh(x):
        m = both(m0, x_inside(x - 4, 8, NX))
        diagonal = s["d0"][x] + s["cx0"][x] + s["cx0"][x - 1]
        weight = jnp.where(m, OMEGA / diagonal, 0.0)
        s["d0"][x], s["w0"][x] = diagonal, weight
        s["a0"][x] = weight * s["f0"][x]

    def total(level, src, x):
        c = str(level)
        v = s[src][x]
        return v, s["f" + c][x] + beside(
            v, s["cx" + c][x - 1], s["cx" + c][x], s["cy" + c][x], s["cz" + c][x],
            s[src][x - 1], s[src][x + 1],
        )

    def sweeps(level, src, dst, start, stop):
        def one(x, carry):
            v, u = total(level, src, x)
            s[dst][x] = KEEP * v + s[f"w{level}"][x] * u
            return carry

        loop(start, stop, one, 0)

    def residue(level, src, x):
        v, u = total(level, src, x)
        return u - s[f"d{level}"][x] * v

    for x in range(4, 12):
        fill(x)
        lateral(x)
    for x in range(4, 11):
        along(x)
    for x in range(5, 11):
        weigh(x)
    sweeps(0, "a0", "b0", 6, 10)

    arrive_all(aside, round0)
    told_around(1, 2)
    tell_plane()
    for x in (1, 2, 3, 12, 13, 14):
        fill(x)
    for x in (2, 3, 12, 13):
        lateral(x)
    for x in (1, 2, 3, 11, 12, 13):
        along(x)
    for x in (2, 3, 4, 11, 12, 13):
        weigh(x)
    sweeps(0, "a0", "b0", 3, 6)
    sweeps(0, "a0", "b0", 10, 13)

    def pairs0(k, carry):
        r = residue(0, "b0", 4 + 2 * k) + residue(0, "b0", 5 + 2 * k)
        s["rs0"][pl.ds(pl.multiple_of(k * 16, 16), 16)] = r[:16, :256]
        return carry

    loop(0, 4, pairs0, 0)
    own_f1 = dot(dot(s["my0"][...], s["rs0"][...]), s["mz0"][...]).reshape(4, 8, 128)
    s["f1b"][4, 4:8] = own_f1
    lane8 = iota((8, 128), 1)
    for xs in range(2):
        one, two = (own_f1[0], own_f1[1]) if xs == 0 else (own_f1[3], own_f1[2])
        two = roll(two, 64, 1)
        s["nz"][xs, 0] = jnp.where(lane8 < 64, one, two)
        s["nz"][xs, 1] = jnp.where(lane8 >= 64, one, two)
        s["ny"][xs, 0], s["ny"][xs, 1] = one[0:1], one[7:8]
    start_all(aside, narrow1)
    start_all(LEVEL, block1("f1b", 3))
    shrink("pf1b", lambda k: own_f1[k])
    start_all(aside, block1("f1b", 3))
    pack_iterate0()
    start_all(EDGES, iterate0)

    def coefficients(ie, x, m, ic, cx_low):
        inext = ie[x + 1]
        cx = 2.0 / (ic + inext)
        cy = 2.0 / (ic + roll(ic, -1, 0))
        cz = 2.0 / (ic + roll(ic, -1, 1))
        diagonal = cx + cx_low + cy + roll(cy, 1, 0) + cz + roll(cz, 1, 1)
        weight = jnp.where(m, OMEGA / diagonal, 0.0)
        return inext, cx, cy, cz, diagonal, weight

    m1 = mask((16, 256), 8, 128, NY // 2, NZ // 2)

    def join1(name, x, other, reach):
        b = s[name]
        distance = 4 - x if x < 4 else x - 7 if x > 7 else 0

        def across(y):
            tiles = [b[y * 3 + i, x] for i in range(3)]
            if distance and y != 1:
                r, xs, ys = s["r" + name], int(x > 7), int(y == 2)
                if name == "e1":
                    tiles = [part(r[xs, ys, i], distance) for i in range(3)]
                else:
                    tiles = [grow(r[xs, ys, i], ys, distance) for i in range(3)]
            return jnp.concatenate([tiles[1], jnp.where(low_lane8, tiles[2], tiles[0])], 1)

        under = jnp.full((8, 256), other, F32)
        if distance < reach:
            under = jnp.where(low_row, across(2), across(0))
        both_rows = jnp.concatenate([across(1), under], 0)
        return jnp.where(both(m1, x_inside(x - 4, 4, NX // 2)), both_rows, other)

    arrive_all(order, block1("e1", 4))
    for x in range(12):
        e = join1("e1", x, 1.0, 5)
        s["ie1"][x] = 1.0 / e
        if 4 <= x < 8:
            half = (x - 4) // 2 * 8
            if x % 2 == 0:
                s["rs1"][half : half + 8] = e[:8]
            else:
                s["rs1"][half : half + 8] += e[:8]
    s["ge"][core, column] = dot(dot(s["my1"][...], s["rs1"][...]), s["mz1"][...]) * 0.25
    all_told()
    gather_start("ge")
    s["cx1"][0] = 2.0 / (s["ie1"][0] + s["ie1"][1])

    def make1(x, carry):
        ic, cx_low = carry
        m = both(m1, x_inside(x - 4, 4, NX // 2))
        ic, cx, cy, cz, diagonal, weight = coefficients(s["ie1"], x, m, ic, cx_low)
        s["cx1"][x], s["cy1"][x], s["cz1"][x] = cx, cy, cz
        s["d1"][x], s["w1"][x] = diagonal, weight
        return ic, cx

    loop(1, 11, make1, (s["ie1"][1], s["cx1"][0]))

    def beside1(x):
        xs, distance = (0, 4 - x) if x < 4 else (1, x - 7)
        own = s["rn"][xs, distance - 1 if xs else 2 - distance]
        z0, z1 = s["rnz"][xs, 0], s["rnz"][xs, 1]
        around = jnp.where(low_lane8, z1, z0)
        under = jnp.zeros((8, 256), F32)
        if distance == 2:
            around = roll(jnp.where(low_lane8, z0, z1), 64, 1)
        else:
            r = s["rny"]
            rows = [
                jnp.where(low_row8, r[xs, 1, i], r[xs, 0, i]) for i in range(3)
            ]
            under = jnp.concatenate([rows[1], jnp.where(low_lane8, rows[2], rows[0])], 1)
        values = jnp.concatenate([jnp.concatenate([own, around], 1), under], 0)
        return jnp.where(both(m1, x_inside(x - 4, 4, NX // 2)), values, 0.0)

    arrive_all(LEVEL, block1("f1b", 3))
    for x in range(4, 8):
        s["f1"][x] = join1("f1b", x, 0.0, 4)
        s["a1"][x] = s["w1"][x] * s["f1"][x]
    arrive_all(aside, narrow1)
    for x in (2, 3, 8, 9):
        f = beside1(x)
        s["f1"][x] = f
        s["a1"][x] = s["w1"][x] * f
    sweeps(1, "a1", "b1", 3, 9)
    for k in range(2):
        r = residue(1, "b1", 4 + 2 * k) + residue(1, "b1", 5 + 2 * k)
        s["rs1"][8 * k : 8 * k + 8] = r[:8]
    s["gf"][core, column] = dot(dot(s["my1"][...], s["rs1"][...]), s["mz1"][...])
    gather_start("gf")
    for x in range(4, 8):
        s["v1"][1, x] = s["b1"][x, :8]
    pair("pv1", lambda k: s["v1"][1, 4 + k])
    start_all(FLAT, flat1)

    row8 = iota((8, 128), 0) < 4

    def arrange(name, half, write):
        def one(k, carry):
            k = 16 * half + k
            even, odd = s[name][0, k], s[name][1, k]
            x = 2 * (k >> 2)
            rows = pl.ds(pl.multiple_of((k & 3) * 8, 8), 8)
            write(x + 4, rows, jnp.where(row8, even, roll(odd, 4, 0)))
            write(x + 5, rows, jnp.where(row8, roll(even, 4, 0), odd))
            return carry

        loop(0, 16, one, 0)

    def collect(name, write):
        for part in range(2):
            gathered(name, part).wait_recv()
            handed(name, part, core).start()
        for part in range(2):
            handed(name, part, 1 - core).wait_recv()
            arrange(name, far if part else 1 - far, write)

    def put_e2(x, rows, values):
        s["e2"][x, rows] = values
        s["ie2"][x, rows] = 1.0 / values

    collect("ge", put_e2)
    shape2 = (32, 128)
    last2, first2 = iota(shape2, 0) == 31, iota(shape2, 0) == 0
    in_z2 = inside(shape2, 64, gz, NZ // 4, 1)
    s["ie2"][3] = jnp.ones(shape2, F32)
    s["ie2"][20] = jnp.ones(shape2, F32)

    def edge_faces(ic, first, last):
        cy = 2.0 / (ic + jnp.where(last, 1.0, roll(ic, -1, 0)))
        below = jnp.where(first, 2.0 / (ic + 1.0), roll(cy, 1, 0))
        return cy, below

    s["cx2"][3] = 2.0 / (1.0 + s["ie2"][4])

    def make2(x, carry):
        ic, cx_low = carry
        inext = s["ie2"][x + 1]
        cx = 2.0 / (ic + inext)
        cy, below = edge_faces(ic, first2, last2)
        cz = 2.0 / (ic + roll(ic, -1, 1))
        diagonal = cx + cx_low + cy + below + cz + roll(cz, 1, 1)
        s["cx2"][x], s["cz2"][x] = cx, cz
        s["cy2"][x] = jnp.where(last2, 0.0, cy)
        s["d2"][x] = diagonal
        s["w2"][x] = jnp.where(in_z2, OMEGA / diagonal, 0.0)
        return inext, cx

    loop(4, 20, make2, (s["ie2"][4], s["cx2"][3]))
    for x in range(4):
        for name in ("a2", "b2"):
            s[name][x] = jnp.zeros(shape2, F32)
            s[name][20 + x] = jnp.zeros(shape2, F32)

    def down3(pair):
        def one(k, carry):
            rows = pl.ds(pl.multiple_of(k * 16, 16), 16)
            s["rs3"][rows] = dot(s["my2"][...], pair(k))
            return carry

        loop(0, 8, one, 0)
        return dot(s["rs3"][...], s["mz2"][...]).reshape(8, 16, 128)

    shape3 = (8, 16, 128)
    p3 = place(iota(shape3, 2), 32, 128)
    near3 = (p3 >= -16) & (p3 < 48)
    e3 = down3(lambda k: s["e2"][4 + 2 * k] + s["e2"][5 + 2 * k]) * 0.25
    ie3 = 1.0 / jnp.where(near3, e3, 1.0)
    first3, last3 = iota(shape3, 1) == 0, iota(shape3, 1) == 15
    edge = jnp.ones((1, 16, 128), F32)
    none = jnp.zeros((1, 16, 128), F32)

    def roll3(values, shift, axis):
        return roll(values.reshape(128, 128), shift, 1).reshape(shape3) if axis == 2 else jnp.stack(
            [roll(values[k], shift, 0) for k in range(8)]
        )

    around = jnp.concatenate([edge, ie3, edge], 0)
    cx3 = 2.0 / (around[1:] + around[:-1])
    cy3 = 2.0 / (ie3 + jnp.where(last3, 1.0, roll3(ie3, -1, 1)))
    below3 = jnp.where(first3, 2.0 / (ie3 + 1.0), roll3(cy3, 1, 1))
    cz3 = 2.0 / (ie3 + roll3(ie3, -1, 2))
    d3 = cx3[1:] + cx3[:-1] + cy3 + below3 + cz3 + roll3(cz3, 1, 2)
    q3 = p3 + 32 * gz
    s["w3"][...] = jnp.where((q3 >= 0) & (q3 < NZ // 8), OMEGA / d3, 0.0)
    s["cx3"][...] = cx3
    s["cy3"][...] = jnp.where(last3, 0.0, cy3)
    s["cz3"][...] = cz3

    leave_all(order, round0)
    leave_all(order, block1("e1", 4))
    leave_all(aside, narrow1)
    leave_all(LEVEL, block1("f1b", 3))
    def put_f2(x, rows, values):
        s["f2"][x, rows] = values
        s["a2"][x, rows] = s["w2"][x, rows] * values

    collect("gf", put_f2)
    sweeps(2, "a2", "b2", 4, 20)
    f3 = down3(lambda k: residue(2, "b2", 4 + 2 * k) + residue(2, "b2", 5 + 2 * k))
    s["f3"][...] = f3

    def coarse(_, v):
        cx, cy, cz = s["cx3"][...], s["cy3"][...], s["cz3"][...]
        after = jnp.concatenate([v[1:], none], 0)
        before = jnp.concatenate([none, v[:-1]], 0)
        u = s["f3"][...] + cx[1:] * after + cx[:-1] * before
        u = u + cy * roll3(v, -1, 1) + roll3(cy * v, 1, 1)
        u = u + cz * roll3(v, -1, 2) + roll3(cz * v, 1, 2)
        return KEEP * v + s["w3"][...] * u

    v3 = loop(0, COARSE_SWEEPS - 1, coarse, s["w3"][...] * f3)

    wide = dot(v3.reshape(128, 128), s["pz3"][...]).reshape(8, 16, 128)
    rows3 = [dot(s["py3"][...], wide[k]) for k in range(8)]
    nothing = jnp.zeros(shape2, F32)
    for k in range(8):
        low = rows3[k - 1] if k else nothing
        high = rows3[k + 1] if k < 7 else nothing
        for i, other in ((0, low), (1, high)):
            x = 4 + 2 * k + i
            add = 0.75 * rows3[k] + 0.25 * other
            s["b2"][x] += jnp.where(in_z2, add, 0.0)
    sweeps(2, "b2", "a2", 4, 20)
    sweeps(2, "a2", "b2", 4, 20)

    for k in range(8):
        s["up1"][16 * k : 16 * k + 16] = dot(s["py2"][...], s["b2"][2 * gx + 1 + k])
    up1 = dot(s["up1"][...], s["pz2"][...])
    arrive_all(FLAT, flat1)
    arrive_all(aside, block1("f1b", 3))
    for x in (1, 2, 3, 8, 9, 10):
        s["f1"][x] = join1("f1b", x, 0.0, 4)
    up1 = up1.reshape(8, 16, 256)
    for x in range(12):
        k = (x - 4) // 2 + 3
        other = up1[k - 1] if x % 2 == 0 else up1[k + 1]
        add = 0.75 * up1[k] + 0.25 * other
        distance = 4 - x if x < 4 else x - 7 if x > 7 else 0
        if distance == 0:
            under = jnp.where(low_row, s["v1"][2, x], s["v1"][0, x])
        else:
            r = s["rv1"]
            after, before = (part(r[int(x > 7), ys], distance) for ys in (1, 0))
            under = jnp.where(low_row, after, before)
        v = jnp.concatenate([s["v1"][1, x], under], 0) + add
        s["a1"][x] = jnp.where(both(m1, x_inside(x - 4, 4, NX // 2)), v, 0.0)
    sweeps(1, "a1", "b1", 1, 11)
    sweeps(1, "b1", "a1", 2, 10)

    arrive_all(EDGES, iterate0)

    def whole0(x):
        nothing = [jnp.zeros(shape, F32) for shape in ((16, 128), (8, 256), (8, 128))]
        if 4 <= x < 12:
            k = x - 4
            z = jnp.where(
                low_lane, roll(s["vz"][1], -16 * k, 1), roll(s["vz"][0], -16 * k - 16, 1)
            )
            i, j = k >> 2, 2 * (k & 3)
            y = jnp.where(
                low_row, roll(s["vy"][1, i], -j, 0), roll(s["vy"][0, i], -j - 2, 0)
            )
            c = [jnp.where(low_lane8, s["vyz"][i, 1], s["vyz"][i, 0]) for i in range(2)]
            c = [roll(c[0], -k - 1, 0), roll(c[1], -k, 0)]
            return join(s["b0"][x, :16, :256], z, y, jnp.where(low_row8, c[1], c[0]))
        xs, distance = (0, 4 - x) if x < 4 else (1, x - 11)
        own = s["vx"][xs, 2 - distance if xs == 0 else distance - 1]
        if distance == 2:
            return join(own, *nothing)
        z = jnp.where(low_lane, s["vxz"][xs, 1, 0], s["vxz"][xs, 0, 0])
        y = jnp.where(low_row, s["vxy"][xs, 1], s["vxy"][xs, 0])
        return join(own, z, y, nothing[2])

    for k in range(8):
        s["up0"][24 * k : 24 * k + 24] = dot(s["py1"][...], s["a1"][2 + k])
    up0 = dot(s["up0"][...], s["pz1"][...]).reshape(8, 24, 384)
    for x in range(2, 14):
        k = (x - 4) // 2 + 2
        other = up0[k - 1] if x % 2 == 0 else up0[k + 1]
        add = 0.75 * up0[k] + 0.25 * other
        v = whole0(x) + add
        s["a0"][x] = jnp.where(both(m0, x_inside(x - 4, 8, NX)), v, 0.0)
    sweeps(0, "a0", "g0", 3, 13)

    def finish(x, carry):
        v, u = total(0, "g0", x)
        out[x - 4] = (KEEP * v + s["w0"][x] * u)[:16, :256]
        return carry

    loop(4, 12, finish, 0)

    leave_all(aside, block1("f1b", 3))
    leave_all(FLAT, flat1)
    leave_all(EDGES, iterate0)
    for name in ("ge", "gf"):
        for part in range(2):
            gathered(name, 1 - part).wait_send()
            handed(name, part, core).wait_send()


def buffers():
    def vmem(*shape):
        return pltpu.VMEM(shape, F32)

    def half(*shape):
        return pltpu.VMEM(shape, BF16)

    table = {
        "sz": vmem(2, 16, 128), "rz": vmem(2, 16, 128),
        "sy": vmem(2, 8, 8, 256), "ry": vmem(2, 8, 8, 256),
        "syz": vmem(2, 2, 8, 128), "ryz": vmem(2, 2, 8, 128),
        "ey": vmem(2, 2, 8, 256), "rey": vmem(2, 2, 8, 256),
        "ez": vmem(2, 2, 16, 128), "rez": vmem(2, 2, 16, 128),
        "ec": vmem(2, 2, 2, 1, 128), "rec": vmem(2, 2, 2, 1, 128),
        "vx": vmem(2, 2, 16, 256), "vy": vmem(2, 2, 8, 256), "vz": vmem(2, 16, 128),
        "pvy": vmem(2, 2, 8, 256), "pvz": vmem(2, 16, 128), "pvxy": vmem(2, 2, 1, 256),
        "vxy": vmem(2, 2, 1, 256), "vxz": vmem(2, 2, 1, 16, 128), "vyz": vmem(2, 2, 8, 128),
        "pvyz": vmem(2, 2, 8, 128),
        "pe1": vmem(2, 2, 2, 8, 128), "re1": vmem(2, 2, 3, 2, 8, 128),
        "ny": vmem(2, 2, 1, 128), "rny": vmem(2, 2, 3, 1, 128),
        "nz": vmem(2, 2, 8, 128), "rnz": vmem(2, 2, 8, 128), "rn": vmem(2, 2, 8, 128),
        "pf1b": vmem(2, 2, 8, 128), "rf1b": vmem(2, 2, 3, 8, 128),
        "pv1": vmem(2, 2, 2, 8, 256), "rv1": vmem(2, 2, 2, 8, 256), "g0": vmem(16, 24, 384),
        "e1": vmem(9, 12, 8, 128), "f1b": vmem(9, 12, 8, 128), "v1": vmem(3, 12, 8, 256),
        "ge": vmem(2, 32, 8, 128), "gf": vmem(2, 32, 8, 128),
        "my0": vmem(32, 64), "mz0": half(256, 128), "my1": vmem(8, 16), "mz1": half(256, 128),
        "my2": vmem(16, 32), "mz2": half(128, 128), "pz3": half(128, 128), "py3": vmem(32, 16),
        "pz2": half(128, 256), "py2": vmem(16, 32), "pz1": half(256, 384), "py1": vmem(24, 16),
        "rs0": vmem(64, 256), "rs1": vmem(16, 256), "rs3": vmem(128, 128),
        "up1": vmem(128, 128), "up0": vmem(192, 256),
        "ie1": vmem(12, 16, 256), "e2": vmem(24, 32, 128), "ie2": vmem(24, 32, 128),
        "f3": vmem(8, 16, 128), "w3": vmem(8, 16, 128), "cx3": vmem(9, 16, 128),
        "cy3": vmem(8, 16, 128), "cz3": vmem(8, 16, 128),
    }
    shapes = {"0": (16, 24, 384), "1": (12, 16, 256), "2": (24, 32, 128)}
    for level, shape in shapes.items():
        for name in ("f", "cx", "cy", "cz", "d", "w", "a", "b"):
            table[name + level] = vmem(*shape)
    table["f_in"], table["e_in"] = vmem(8, 16, 256), vmem(8, 16, 256)
    table["tell"] = pltpu.SemaphoreType.REGULAR((3,))
    table["in_s"] = pltpu.SemaphoreType.DMA((2,))
    table["e0"] = vmem(16, 24, 384)
    for name, number in (("c0", 28), ("v0", 18), ("n1", 18), ("e1", 26), ("f1b", 26), ("v1", 8), ("ge", 4), ("gf", 4)):
        table[name + "_s"] = pltpu.SemaphoreType.DMA((number,))
        table[name + "_r"] = pltpu.SemaphoreType.DMA((number,))
    return table


NAMES = list(buffers())


def on_device(charge, dielectric):
    return pl.pallas_call(
        lambda f, e, o, *s: kernel(f, e, o, s),
        out_shape=jax.ShapeDtypeStruct((8, 16, 256), F32),
        in_specs=[pl.BlockSpec(memory_space=pltpu.HBM)] * 2,
        out_specs=pl.BlockSpec(memory_space=pltpu.VMEM),
        scratch_shapes=list(buffers().values()),
        compiler_params=pltpu.CompilerParams(
            collective_id=0, has_side_effects=True, vmem_limit_bytes=60 * 2**20
        ),
    )(charge, dielectric)


def solution(mesh):
    placed = (P("gx", "gy", "gz"), P("gx", "gy", "gz"))
    return jax.shard_map(
        on_device, mesh=mesh, in_specs=placed, out_specs=P("gx", "gy", "gz"), check_vma=False
    )
```

```python
import functools
import itertools
import math

import jax
import jax.numpy as jnp
from jax import lax
from jax.experimental import pallas as pl
from jax.experimental.pallas import tpu as pltpu
from jax.sharding import PartitionSpec as P

MESH = pl.DeviceIdType.MESH
F32 = jnp.float32
BF16 = jnp.bfloat16
OMEGA = 0.8
KEEP = 1.0 - OMEGA
FOURPI = 4.0 * math.pi
COARSE_SWEEPS = 8
NX, NY, NZ = 64, 128, 1024
GX, GY, GZ = 8, 8, 4
DIRS = [d for d in itertools.product((-1, 0, 1), repeat=3) if d != (0, 0, 0)]
ASIDE = [d for d in DIRS if d[0]]
LEVEL = [d for d in DIRS if not d[0]]
EDGES = [d for d in DIRS if 0 in d]
FLAT = [d for d in itertools.product((-1, 0, 1), repeat=2) if d != (0, 0)]


def loop(start, stop, body, init):
    return lax.fori_loop(start, stop, body, init, unroll=True)


def roll(values, shift, axis):
    return pltpu.roll(values, shift % values.shape[axis], axis)


def halves(values):
    high = values.astype(BF16)
    return high, (values - high.astype(F32)).astype(BF16)


def dot(a, b):
    if b.dtype == BF16:
        high, low = halves(a)
        return jnp.dot(high, b, preferred_element_type=F32) + jnp.dot(
            low, b, preferred_element_type=F32
        )
    high, low = halves(b)
    a = a.astype(BF16)
    return jnp.dot(a, high, preferred_element_type=F32) + jnp.dot(
        a, low, preferred_element_type=F32
    )


def place(index, own, size):
    half = (size - own) // 2
    return jnp.where(index < own + half, index, index - size)


def iota(shape, axis):
    return lax.broadcasted_iota(jnp.int32, shape, axis)


def restrict_z(own, size, out_own, out_size, weight):
    shape = (size, out_size)
    p = place(iota(shape, 0), own, size)
    q = place(iota(shape, 1), out_own, out_size)
    return jnp.where((p >> 1) == q, weight, 0.0).astype(BF16)


def pair_rows(groups, own, weight):
    shape = (groups * own // 2, groups * own)
    return jnp.where((iota(shape, 1) >> 1) == iota(shape, 0), weight, 0.0).astype(F32)


def spread(q, p):
    parent = p >> 1
    other = jnp.where((p & 1) == 0, parent - 1, parent + 1)
    return jnp.where(q == parent, 0.75, jnp.where(q == other, 0.25, 0.0)).astype(F32)


def prolong_z(own, size, out_own, out_size):
    shape = (size, out_size)
    weights = spread(place(iota(shape, 0), own, size), place(iota(shape, 1), out_own, out_size))
    return weights.astype(BF16)


def prolong_y(own, size, out_own, out_size):
    shape = (out_size, size)
    return spread(place(iota(shape, 1), own, size), place(iota(shape, 0), out_own, out_size))


def kernel(f_hbm, e_hbm, out, s):
    s = dict(zip(NAMES, s, strict=True))
    f_in, e_in = s["f_in"], s["e_in"]
    loads = [
        pltpu.make_async_copy(f_hbm, f_in, s["in_s"].at[0]),
        pltpu.make_async_copy(e_hbm, e_in, s["in_s"].at[1]),
    ]
    for load in loads:
        load.start()
    gx, gy, gz = (lax.axis_index(a) for a in ("gx", "gy", "gz"))
    core = gy & 1
    column = gx * 4 + (gy >> 1)
    has = [
        {-1: gx > 0, 0: True, 1: gx < GX - 1},
        {-1: gy > 0, 0: True, 1: gy < GY - 1},
        {-1: gz > 0, 0: True, 1: gz < GZ - 1},
    ]

    def there(d):
        found = [has[i][c] for i, c in enumerate(d) if c]
        return functools.reduce(jnp.logical_and, found)

    def peer(d):
        return (gx + d[0], gy + d[1], gz + (d[2] if len(d) > 2 else 0))

    def flip(d):
        return tuple(-c for c in d)

    sibling = (gx, gy + 1 - 2 * core, gz)

    barrier = pltpu.get_barrier_semaphore()

    def greet(device):
        pl.semaphore_signal(barrier, inc=1, device_id=device, device_id_type=MESH)

    order = sorted(DIRS, key=lambda d: (-abs(d[0]), abs(d[1]) + abs(d[2])))
    aside = [d for d in order if d[0]]
    for d in order:
        pl.when(there(d))(functools.partial(greet, peer(d)))

    def count(i):
        return 1 + has[i][-1].astype(jnp.int32) + has[i][1].astype(jnp.int32)

    lane128 = iota((16, 128), 1)
    row256 = iota((8, 256), 0)

    def mixed(side, x):
        f, e = f_in[x], e_in[x]
        if side == 0:
            return jnp.where(lane128 < 64, f[:, :128], roll(e[:, :128], 64, 1))
        return jnp.where(lane128 >= 64, f[:, 128:], roll(e[:, 128:], 64, 1))

    for load in loads:
        load.wait()
    share, within = lane128 >> 4, lane128 & 15
    share8 = iota((8, 128), 1) >> 4
    for zs in range(2):
        tile = jnp.zeros((16, 128), F32)
        lanes = slice(128 * zs, 128 * zs + 128)
        for x in range(8):
            f, e = f_in[x][:, lanes], e_in[x][:, lanes]
            f, e = roll(f, 16 * x + 8 * zs, 1), roll(e, 16 * x + 8 + 8 * zs, 1)
            tile = jnp.where(share == x, jnp.where(within < 8, f, e), tile)
        s["sz"][zs] = tile
    for ys in range(2):
        tiles = [jnp.zeros((8, 128), F32)] * 2
        for x in range(8):
            f, e = f_in[x], e_in[x]
            if ys == 0:
                rows = jnp.where(row256 < 4, f[:8], roll(e[:8], 4, 0))
            else:
                rows = jnp.where(row256 >= 4, f[8:], roll(e[8:], 4, 0))
            s["sy"][ys, x] = rows
            for zs in range(2):
                turned = roll(rows[:, 128 * zs : 128 * zs + 128], 16 * x + 16 * zs, 1)
                tiles[zs] = jnp.where(share8 == x, turned, tiles[zs])
        for zs in range(2):
            s["syz"][ys, zs] = tiles[zs]

    row8 = iota((8, 256), 0)
    for xs in range(2):
        one, two = (0, 1) if xs == 0 else (7, 6)
        near = slice(0, 1), slice(15, 16)
        s["ey"][xs, 0] = jnp.where(
            (row8 == 2) | (row8 == 3), roll(s["sy"][0, two], -2, 0), s["sy"][0, one]
        )
        s["ey"][xs, 1] = jnp.where(
            (row8 == 4) | (row8 == 5), roll(s["sy"][1, two], 2, 0), s["sy"][1, one]
        )
        s["ez"][xs, 0] = jnp.where(
            (lane128 >= 32) & (lane128 < 64), roll(mixed(0, two), -32, 1), mixed(0, one)
        )
        s["ez"][xs, 1] = jnp.where(
            (lane128 >= 64) & (lane128 < 96), roll(mixed(1, two), 32, 1), mixed(1, one)
        )
        for ys in range(2):
            s["ec"][xs, ys, 0] = e_in[one, near[ys], :128]
            s["ec"][xs, ys, 1] = e_in[one, near[ys], 128:]

    pl.semaphore_wait(barrier, count(0) * count(1) * count(2) - 1)

    def send(src, dst, name, index, device):
        return pltpu.make_async_remote_copy(
            src_ref=src,
            dst_ref=dst,
            send_sem=s[name + "_s"].at[index],
            recv_sem=s[name + "_r"].at[index],
            device_id=device,
            device_id_type=MESH,
        )

    def cut(dx, n, whole, base):
        if dx == 0:
            return pl.ds(0, whole), pl.ds(base, whole)
        if dx < 0:
            return pl.ds(0, n), pl.ds(base + whole, n)
        return pl.ds(whole - n, n), pl.ds(base - n, n)

    def round0(d):
        dx, dy, dz = d
        index = DIRS.index(d)
        xs, ys, zs = (int(c > 0) for c in d)
        if dy == 0 and dz == 0:
            a, b = cut(dx, 2, 8, 4)
            own = (pl.ds(0, 16), pl.ds(0, 256))
            first = send(f_in.at[a], s["f0"].at[(b, *own)], "c0", index, peer(d))
            a, b = cut(dx, 3, 8, 4)
            second = send(e_in.at[a], s["e0"].at[(b, *own)], "c0", 26 + (dx > 0), peer(d))
            return [first, second]
        if dx and dy and dz:
            source, target = s["ec"].at[xs, ys, zs], s["rec"].at[1 - xs, 1 - ys, 1 - zs]
        elif dx and dy:
            source, target = s["ey"].at[xs, ys], s["rey"].at[1 - xs, 1 - ys]
        elif dx:
            source, target = s["ez"].at[xs, zs], s["rez"].at[1 - xs, 1 - zs]
        elif dy and dz:
            source, target = s["syz"].at[ys, zs], s["ryz"].at[1 - ys, 1 - zs]
        elif dy:
            source, target = s["sy"].at[ys], s["ry"].at[1 - ys]
        else:
            source, target = s["sz"].at[zs], s["rz"].at[1 - zs]
        return [send(source, target, "c0", index, peer(d))]

    def iterate0(d):
        dx, dy, dz = d
        xs, ys, zs = (int(c > 0) for c in d)
        name = "v" + "x" * (dx != 0) + "y" * (dy != 0) + "z" * (dz != 0)
        slot = tuple(1 - i for i, c in zip((xs, ys, zs), d) if c)
        if dx and not dy:
            wide = 1 if dz else 2
            x = pl.ds(12 - wide if dx > 0 else 4, wide)
            lanes = pl.ds(128 * zs, 128) if dz else pl.ds(0, 256)
            source = s["b0"].at[x, pl.ds(0, 16), lanes]
        else:
            source = s["p" + name].at[tuple(1 - i for i in slot)]
        return [send(source, s[name].at[slot], "v0", EDGES.index(d), peer(d))]

    def pack_iterate0():
        row = iota((8, 256), 0)
        row_c = iota((8, 128), 0)
        for zs in range(2):
            tile = jnp.zeros((16, 128), F32)
            for k in range(8):
                v = s["b0"][4 + k, :16, 128 * zs : 128 * zs + 128]
                tile = jnp.where(share == k, roll(v, 16 * k + 16 * zs, 1), tile)
            s["pvz"][zs] = tile
        for ys in range(2):
            corner = jnp.zeros((8, 256), F32)
            tiles = [jnp.zeros((8, 256), F32)] * 2
            for k in range(8):
                v = s["b0"][4 + k, 8 * ys : 8 * ys + 8, :256]
                j = k & 3
                tiles[k >> 2] = jnp.where(
                    (row >> 1) == j, roll(v, 2 * j + 2 * ys, 0), tiles[k >> 2]
                )
                corner = jnp.where(row == k, roll(v, k + ys, 0), corner)
            s["pvy"][ys, 0], s["pvy"][ys, 1] = tiles
            s["pvyz"][ys, 0], s["pvyz"][ys, 1] = corner[:, :128], corner[:, 128:]
            near = slice(15, 16) if ys else slice(0, 1)
            s["pvxy"][0, ys] = s["b0"][4, near, :256]
            s["pvxy"][1, ys] = s["b0"][11, near, :256]

    def shrink(name, slab):
        width = slab(0).shape[1]
        row = iota((8, width), 0)
        for xs in range(2):
            one, two, three = (slab(k if xs == 0 else 3 - k) for k in range(3))
            tile = jnp.where(row >= 3, roll(two, 3, 0), one)
            s[name][xs, 0] = jnp.where(row >= 5, roll(three, 5, 0), tile)
            tile = jnp.where(row <= 4, roll(two, -3, 0), one)
            s[name][xs, 1] = jnp.where(row <= 2, roll(three, -5, 0), tile)

    def grow(tile, ys, distance):
        shift = (0, 3, 5)[distance - 1]
        return roll(tile, -shift if ys else shift, 0) if shift else tile

    def pair(name, slab):
        half = iota((8, slab(0).shape[1]), 0) >= 4
        for xs in range(2):
            from_edge = [slab(k if xs == 0 else 3 - k) for k in range(4)]
            for t in range(2):
                one, two = from_edge[2 * t], roll(from_edge[2 * t + 1], 4, 0)
                s[name][xs, 0, t] = jnp.where(half, two, one)
                s[name][xs, 1, t] = jnp.where(half, one, two)

    def part(tiles, distance):
        tile = tiles[(distance - 1) >> 1]
        return tile if distance & 1 else roll(tile, 4, 0)

    def block1(name, wide):
        def copies(d):
            dx, dy, dz = d
            index = DIRS.index(d)
            if dx and dy:
                xs, ys = int(dx > 0), int(dy > 0)
                source, target = s["p" + name].at[xs, ys], s["r" + name].at[1 - xs, 1 - ys, 1 - dz]
                return [send(source, target, name, index, peer(d))]
            a, b = cut(dx, wide, 4, 4)
            own = pl.ds(4 + a.start, a.size)
            slot = (1 - dy) * 3 + 1 - dz
            buffer = s[name]
            return [send(buffer.at[4, own], buffer.at[slot, b], name, index, peer(d))]

        return copies

    def narrow1(d):
        dx, dy, dz = d
        xs, ys, zs = (int(c > 0) for c in d)
        if dy:
            source, target = s["ny"].at[xs, ys], s["rny"].at[1 - xs, 1 - ys, 1 - dz]
        elif dz:
            source, target = s["nz"].at[xs, zs], s["rnz"].at[1 - xs, 1 - zs]
        else:
            source, target = s["f1b"].at[4, pl.ds(6 if xs else 4, 2)], s["rn"].at[1 - xs]
        return [send(source, target, "n1", ASIDE.index(d), peer(d))]

    def flat1(d):
        dx, dy = d
        if dx and dy:
            xs, ys = int(dx > 0), int(dy > 0)
            source, target = s["pv1"].at[xs, ys], s["rv1"].at[1 - xs, 1 - ys]
            return [send(source, target, "v1", FLAT.index(d), peer(d))]
        a, b = cut(dx, 4, 4, 4)
        own = pl.ds(4 + a.start, a.size)
        return [send(s["v1"].at[1, own], s["v1"].at[1 - dy, b], "v1", FLAT.index(d), peer(d))]

    def start_all(dirs, copies):
        for d in dirs:

            @pl.when(there(d))
            def _(d=d):
                for copy in copies(d):
                    copy.start()

    def arrive_all(dirs, copies):
        for d in dirs:

            @pl.when(there(flip(d)))
            def _(d=d):
                for copy in copies(d):
                    copy.wait_recv()

    def leave_all(dirs, copies):
        for d in dirs:

            @pl.when(there(d))
            def _(d=d):
                for copy in copies(d):
                    copy.wait_send()

    def step_away(g, c, far):
        return (g + far * c >= 0) & (g + far * c < 8) if c else True

    def found(d, far):
        return jnp.logical_and(step_away(gx, d[0], far), step_away(gy, d[1], far))

    def tell(index, device):
        pl.semaphore_signal(s["tell"].at[index], inc=1, device_id=device, device_id_type=MESH)

    def tell_around(index, far):
        for d in FLAT:
            device = (gx + far * d[0], gy + far * d[1], gz)
            pl.when(found(d, far))(functools.partial(tell, index, device))

    def told_around(index, far):
        told = [found(d, far).astype(jnp.int32) for d in FLAT]
        pl.semaphore_wait(s["tell"].at[index], functools.reduce(jnp.add, told))

    def tell_plane():
        for device in ((gx ^ 4, gy, gz), (gx, gy ^ 4, gz), (gx ^ 4, gy ^ 4, gz)):
            tell(2, device)

    def all_told():
        pl.semaphore_wait(s["tell"].at[2], 3)

    far = 1 - (gx >> 2)

    def column_device(c):
        return (c >> 2, ((c & 3) << 1) + core, gz)

    def gather_start(name):
        mine = s[name].at[core, column]

        def one(k, carry):
            send(mine, mine, name, 1, column_device(16 * far + ((column + k) & 15))).start()
            return carry

        def other(k, carry):
            send(mine, mine, name, 0, column_device(16 * (1 - far) + ((column + k) & 15))).start()
            return carry

        lax.fori_loop(0, 16, one, 0)
        lax.fori_loop(1, 16, other, 0)

    def gathered(name, part):
        block = s[name].at[core, pl.ds(0, 15 + part)]
        return send(block, block, name, part, sibling)

    def handed(name, part, side):
        half = far if part else 1 - far
        block = s[name].at[side, pl.ds(16 * half, 16)]
        return send(block, block, name, 2 + part, sibling)

    start_all(order, round0)
    tell_around(0, 1)

    s["my1"][...] = pair_rows(2, 8, 0.5)
    s["mz1"][...] = restrict_z(128, 256, 64, 128, 1.0)
    s["my2"][...] = pair_rows(1, 32, 0.5)
    s["mz2"][...] = restrict_z(64, 128, 32, 128, 1.0)
    s["pz3"][...] = prolong_z(32, 128, 64, 128)
    s["py3"][...] = prolong_y(16, 16, 32, 32)
    s["pz2"][...] = prolong_z(64, 128, 128, 256)
    fine = place(iota((16, 32), 0), 8, 16) + 8 * gy
    s["py2"][...] = spread(iota((16, 32), 1), fine)
    s["pz1"][...] = prolong_z(128, 256, 256, 384)
    s["py1"][...] = prolong_y(8, 16, 16, 24)

    def inside(shape, own, index, total, axis):
        p = place(iota(shape, axis), own, shape[axis]) + own * index
        return (p >= 0) & (p < total)

    def x_inside(x, own, total):
        p = x + own * gx
        return (p >= 0) & (p < total)

    def mask(shape, own_y, own_z, total_y, total_z):
        return inside(shape, own_y, gy, total_y, 0) & inside(shape, own_z, gz, total_z, 1)

    def both(a, flag):
        return jnp.logical_and(a, jnp.broadcast_to(flag, a.shape))

    def beside(v, cx_low, cx, cy, cz, low, high):
        total = cx_low * low + cx * high
        total = total + cy * roll(v, -1, 0) + roll(cy * v, 1, 0)
        return total + cz * roll(v, -1, 1) + roll(cz * v, 1, 1)

    arrive_all(LEVEL, round0)
    told_around(0, 1)
    tell_around(1, 2)
    s["my0"][...] = pair_rows(4, 16, 0.5)
    s["mz0"][...] = restrict_z(256, 256, 128, 128, 1.0)
    for k in range(4):
        s["rs0"][16 * k : 16 * k + 16] = e_in[2 * k] + e_in[2 * k + 1]
    own_e1 = (dot(dot(s["my0"][...], s["rs0"][...]), s["mz0"][...]) * 0.25).reshape(4, 8, 128)
    s["e1"][4, 4:8] = own_e1
    pair("pe1", lambda k: own_e1[k])
    start_all(LEVEL, block1("e1", 4))
    m0 = mask((24, 384), 16, 256, NY, NZ)
    ones0 = jnp.ones((24, 384), F32)
    low_lane = iota((16, 128), 1) < 64
    low_lane8 = iota((8, 128), 1) < 64
    low_row = iota((8, 256), 0) < 4
    low_row8 = iota((8, 128), 0) < 4

    def fill(x):
        m = both(m0, x_inside(x - 4, 8, NX))
        if 4 <= x < 12:
            distance, xs, f_own, e_own = 0, 0, f_in[x - 4], e_in[x - 4]
            k = x - 4
            y0, y1 = s["ry"][0, k], s["ry"][1, k]
            z0, z1 = s["rz"][0], s["rz"][1]
            f_z = jnp.where(low_lane, roll(z1, -16 * k, 1), roll(z0, -16 * k - 8, 1))
            e_z = jnp.where(low_lane, roll(z1, -16 * k - 8, 1), roll(z0, -16 * k - 16, 1))
        else:
            xs, distance = (0, 4 - x) if x < 4 else (1, x - 11)
            f_own, e_own = s["f0"][x, :16, :256], s["e0"][x, :16, :256]
            if distance == 3:
                e = jnp.concatenate([e_own, jnp.ones((16, 128), F32)], 1)
                e = jnp.concatenate([e, jnp.ones((8, 384), F32)], 0)
                s["e0"][x] = 1.0 / jnp.where(m, e, 1.0)
                return
            z0, z1, y0, y1 = s["rez"][xs, 0], s["rez"][xs, 1], s["rey"][xs, 0], s["rey"][xs, 1]
            if distance == 2:
                z0, z1, y0, y1 = roll(z0, -32, 1), roll(z1, 32, 1), roll(y0, -2, 0), roll(y1, 2, 0)
        if distance:
            f_z = jnp.where(low_lane, z1, z0)
            e_z = roll(jnp.where(low_lane, z0, z1), 64, 1)
        f_y = jnp.where(low_row, y1, y0)
        e_y = roll(jnp.where(low_row, y0, y1), 4, 0)
        f_c = jnp.zeros((8, 128), F32)
        e_c = jnp.ones((8, 128), F32)
        if distance == 0:
            c0, c1 = (
                jnp.where(
                    low_lane8,
                    roll(s["ryz"][i, 1], -16 * k, 1),
                    roll(s["ryz"][i, 0], -16 * k - 16, 1),
                )
                for i in range(2)
            )
            f_c = jnp.where(low_row8, c1, c0)
            e_c = roll(jnp.where(low_row8, c0, c1), 4, 0)
        elif distance == 1:
            c = s["rec"]
            c0 = jnp.where(low_lane8, c[xs, 0, 1], c[xs, 0, 0])
            c1 = jnp.where(low_lane8, c[xs, 1, 1], c[xs, 1, 0])
            e_c = jnp.where(low_row8, c1, c0)

        f, e = join(f_own, f_z, f_y, f_c), join(e_own, e_z, e_y, e_c)
        s["f0"][x] = jnp.where(m, f, 0.0) * FOURPI
        s["e0"][x] = 1.0 / jnp.where(m, e, 1.0)

    def join(own, z, y, c):
        top = jnp.concatenate([own, z], 1)
        return jnp.concatenate([top, jnp.concatenate([y, c], 1)], 0)

    def faces(here, after):
        return 2.0 / (here + after)

    def lateral(x):
        ic = s["e0"][x]
        cy, cz = faces(ic, roll(ic, -1, 0)), faces(ic, roll(ic, -1, 1))
        s["cy0"][x], s["cz0"][x] = cy, cz
        s["d0"][x] = cy + roll(cy, 1, 0) + cz + roll(cz, 1, 1)

    def along(x):
        s["cx0"][x] = faces(s["e0"][x], s["e0"][x + 1])

    def weigh(x):
        m = both(m0, x_inside(x - 4, 8, NX))
        diagonal = s["d0"][x] + s["cx0"][x] + s["cx0"][x - 1]
        weight = jnp.where(m, OMEGA / diagonal, 0.0)
        s["d0"][x], s["w0"][x] = diagonal, weight
        s["a0"][x] = weight * s["f0"][x]

    def total(level, src, x):
        c = str(level)
        v = s[src][x]
        return v, s["f" + c][x] + beside(
            v, s["cx" + c][x - 1], s["cx" + c][x], s["cy" + c][x], s["cz" + c][x],
            s[src][x - 1], s[src][x + 1],
        )

    def sweeps(level, src, dst, start, stop):
        def one(x, carry):
            v, u = total(level, src, x)
            s[dst][x] = KEEP * v + s[f"w{level}"][x] * u
            return carry

        loop(start, stop, one, 0)

    def residue(level, src, x):
        v, u = total(level, src, x)
        return u - s[f"d{level}"][x] * v

    for x in range(4, 12):
        fill(x)
        lateral(x)
    for x in range(4, 11):
        along(x)
    for x in range(5, 11):
        weigh(x)
    sweeps(0, "a0", "b0", 6, 10)

    start_all(aside, block1("e1", 4))
    arrive_all(aside, round0)
    told_around(1, 2)
    tell_plane()
    for x in (1, 2, 3, 12, 13, 14):
        fill(x)
    for x in (2, 3, 12, 13):
        lateral(x)
    for x in (1, 2, 3, 11, 12, 13):
        along(x)
    for x in (2, 3, 4, 11, 12, 13):
        weigh(x)
    sweeps(0, "a0", "b0", 3, 6)
    sweeps(0, "a0", "b0", 10, 13)

    def pairs0(k, carry):
        r = residue(0, "b0", 4 + 2 * k) + residue(0, "b0", 5 + 2 * k)
        s["rs0"][pl.ds(pl.multiple_of(k * 16, 16), 16)] = r[:16, :256]
        return carry

    loop(0, 4, pairs0, 0)
    own_f1 = dot(dot(s["my0"][...], s["rs0"][...]), s["mz0"][...]).reshape(4, 8, 128)
    s["f1b"][4, 4:8] = own_f1
    lane8 = iota((8, 128), 1)
    for xs in range(2):
        one, two = (own_f1[0], own_f1[1]) if xs == 0 else (own_f1[3], own_f1[2])
        two = roll(two, 64, 1)
        s["nz"][xs, 0] = jnp.where(lane8 < 64, one, two)
        s["nz"][xs, 1] = jnp.where(lane8 >= 64, one, two)
        s["ny"][xs, 0], s["ny"][xs, 1] = one[0:1], one[7:8]
    start_all(aside, narrow1)
    start_all(LEVEL, block1("f1b", 3))
    pack_iterate0()
    start_all(EDGES, iterate0)
    shrink("pf1b", lambda k: own_f1[k])
    start_all(aside, block1("f1b", 3))

    def coefficients(ie, x, m, ic, cx_low):
        inext = ie[x + 1]
        cx = 2.0 / (ic + inext)
        cy = 2.0 / (ic + roll(ic, -1, 0))
        cz = 2.0 / (ic + roll(ic, -1, 1))
        diagonal = cx + cx_low + cy + roll(cy, 1, 0) + cz + roll(cz, 1, 1)
        weight = jnp.where(m, OMEGA / diagonal, 0.0)
        return inext, cx, cy, cz, diagonal, weight

    m1 = mask((16, 256), 8, 128, NY // 2, NZ // 2)

    def join1(name, x, other, reach):
        b = s[name]
        distance = 4 - x if x < 4 else x - 7 if x > 7 else 0

        def across(y):
            tiles = [b[y * 3 + i, x] for i in range(3)]
            if distance and y != 1:
                r, xs, ys = s["r" + name], int(x > 7), int(y == 2)
                if name == "e1":
                    tiles = [part(r[xs, ys, i], distance) for i in range(3)]
                else:
                    tiles = [grow(r[xs, ys, i], ys, distance) for i in range(3)]
            return jnp.concatenate([tiles[1], jnp.where(low_lane8, tiles[2], tiles[0])], 1)

        under = jnp.full((8, 256), other, F32)
        if distance < reach:
            under = jnp.where(low_row, across(2), across(0))
        both_rows = jnp.concatenate([across(1), under], 0)
        return jnp.where(both(m1, x_inside(x - 4, 4, NX // 2)), both_rows, other)

    arrive_all(order, block1("e1", 4))
    for x in range(12):
        e = join1("e1", x, 1.0, 5)
        s["ie1"][x] = 1.0 / e
        if 4 <= x < 8:
            half = (x - 4) // 2 * 8
            if x % 2 == 0:
                s["rs1"][half : half + 8] = e[:8]
            else:
                s["rs1"][half : half + 8] += e[:8]
    s["ge"][core, column] = dot(dot(s["my1"][...], s["rs1"][...]), s["mz1"][...]) * 0.25
    all_told()
    gather_start("ge")
    s["cx1"][0] = 2.0 / (s["ie1"][0] + s["ie1"][1])

    def make1(x, carry):
        ic, cx_low = carry
        m = both(m1, x_inside(x - 4, 4, NX // 2))
        ic, cx, cy, cz, diagonal, weight = coefficients(s["ie1"], x, m, ic, cx_low)
        s["cx1"][x], s["cy1"][x], s["cz1"][x] = cx, cy, cz
        s["d1"][x], s["w1"][x] = diagonal, weight
        return ic, cx

    loop(1, 11, make1, (s["ie1"][1], s["cx1"][0]))

    def beside1(x):
        xs, distance = (0, 4 - x) if x < 4 else (1, x - 7)
        own = s["rn"][xs, distance - 1 if xs else 2 - distance]
        z0, z1 = s["rnz"][xs, 0], s["rnz"][xs, 1]
        around = jnp.where(low_lane8, z1, z0)
        under = jnp.zeros((8, 256), F32)
        if distance == 2:
            around = roll(jnp.where(low_lane8, z0, z1), 64, 1)
        else:
            r = s["rny"]
            rows = [
                jnp.where(low_row8, r[xs, 1, i], r[xs, 0, i]) for i in range(3)
            ]
            under = jnp.concatenate([rows[1], jnp.where(low_lane8, rows[2], rows[0])], 1)
        values = jnp.concatenate([jnp.concatenate([own, around], 1), under], 0)
        return jnp.where(both(m1, x_inside(x - 4, 4, NX // 2)), values, 0.0)

    arrive_all(LEVEL, block1("f1b", 3))
    for x in range(4, 8):
        s["f1"][x] = join1("f1b", x, 0.0, 4)
        s["a1"][x] = s["w1"][x] * s["f1"][x]
    arrive_all(aside, narrow1)
    for x in (2, 3, 8, 9):
        f = beside1(x)
        s["f1"][x] = f
        s["a1"][x] = s["w1"][x] * f
    sweeps(1, "a1", "b1", 3, 9)
    for k in range(2):
        r = residue(1, "b1", 4 + 2 * k) + residue(1, "b1", 5 + 2 * k)
        s["rs1"][8 * k : 8 * k + 8] = r[:8]
    s["gf"][core, column] = dot(dot(s["my1"][...], s["rs1"][...]), s["mz1"][...])
    gather_start("gf")
    for x in range(4, 8):
        s["v1"][1, x] = s["b1"][x, :8]
    pair("pv1", lambda k: s["v1"][1, 4 + k])
    start_all(FLAT, flat1)

    row8 = iota((8, 128), 0) < 4

    def arrange(name, half, write):
        def one(k, carry):
            k = 16 * half + k
            even, odd = s[name][0, k], s[name][1, k]
            x = 2 * (k >> 2)
            rows = pl.ds(pl.multiple_of((k & 3) * 8, 8), 8)
            write(x + 4, rows, jnp.where(row8, even, roll(odd, 4, 0)))
            write(x + 5, rows, jnp.where(row8, roll(even, 4, 0), odd))
            return carry

        loop(0, 16, one, 0)

    def collect(name, write):
        for part in range(2):
            gathered(name, part).wait_recv()
            handed(name, part, core).start()
        for part in range(2):
            handed(name, part, 1 - core).wait_recv()
            arrange(name, far if part else 1 - far, write)

    def put_e2(x, rows, values):
        s["e2"][x, rows] = values
        s["ie2"][x, rows] = 1.0 / values

    collect("ge", put_e2)
    shape2 = (32, 128)
    last2, first2 = iota(shape2, 0) == 31, iota(shape2, 0) == 0
    in_z2 = inside(shape2, 64, gz, NZ // 4, 1)
    s["ie2"][3] = jnp.ones(shape2, F32)
    s["ie2"][20] = jnp.ones(shape2, F32)

    def edge_faces(ic, first, last):
        cy = 2.0 / (ic + jnp.where(last, 1.0, roll(ic, -1, 0)))
        below = jnp.where(first, 2.0 / (ic + 1.0), roll(cy, 1, 0))
        return cy, below

    s["cx2"][3] = 2.0 / (1.0 + s["ie2"][4])

    def make2(x, carry):
        ic, cx_low = carry
        inext = s["ie2"][x + 1]
        cx = 2.0 / (ic + inext)
        cy, below = edge_faces(ic, first2, last2)
        cz = 2.0 / (ic + roll(ic, -1, 1))
        diagonal = cx + cx_low + cy + below + cz + roll(cz, 1, 1)
        s["cx2"][x], s["cz2"][x] = cx, cz
        s["cy2"][x] = jnp.where(last2, 0.0, cy)
        s["d2"][x] = diagonal
        s["w2"][x] = jnp.where(in_z2, OMEGA / diagonal, 0.0)
        return inext, cx

    loop(4, 20, make2, (s["ie2"][4], s["cx2"][3]))
    for x in range(4):
        for name in ("a2", "b2"):
            s[name][x] = jnp.zeros(shape2, F32)
            s[name][20 + x] = jnp.zeros(shape2, F32)

    def down3(pair):
        def one(k, carry):
            rows = pl.ds(pl.multiple_of(k * 16, 16), 16)
            s["rs3"][rows] = dot(s["my2"][...], pair(k))
            return carry

        loop(0, 8, one, 0)
        return dot(s["rs3"][...], s["mz2"][...]).reshape(8, 16, 128)

    shape3 = (8, 16, 128)
    p3 = place(iota(shape3, 2), 32, 128)
    near3 = (p3 >= -16) & (p3 < 48)
    e3 = down3(lambda k: s["e2"][4 + 2 * k] + s["e2"][5 + 2 * k]) * 0.25
    ie3 = 1.0 / jnp.where(near3, e3, 1.0)
    first3, last3 = iota(shape3, 1) == 0, iota(shape3, 1) == 15
    edge = jnp.ones((1, 16, 128), F32)
    none = jnp.zeros((1, 16, 128), F32)

    def roll3(values, shift, axis):
        return roll(values.reshape(128, 128), shift, 1).reshape(shape3) if axis == 2 else jnp.stack(
            [roll(values[k], shift, 0) for k in range(8)]
        )

    around = jnp.concatenate([edge, ie3, edge], 0)
    cx3 = 2.0 / (around[1:] + around[:-1])
    cy3 = 2.0 / (ie3 + jnp.where(last3, 1.0, roll3(ie3, -1, 1)))
    below3 = jnp.where(first3, 2.0 / (ie3 + 1.0), roll3(cy3, 1, 1))
    cz3 = 2.0 / (ie3 + roll3(ie3, -1, 2))
    d3 = cx3[1:] + cx3[:-1] + cy3 + below3 + cz3 + roll3(cz3, 1, 2)
    q3 = p3 + 32 * gz
    s["w3"][...] = jnp.where((q3 >= 0) & (q3 < NZ // 8), OMEGA / d3, 0.0)
    s["cx3"][...] = cx3
    s["cy3"][...] = jnp.where(last3, 0.0, cy3)
    s["cz3"][...] = cz3

    leave_all(order, round0)
    leave_all(order, block1("e1", 4))
    leave_all(aside, narrow1)
    leave_all(LEVEL, block1("f1b", 3))
    def put_f2(x, rows, values):
        s["f2"][x, rows] = values
        s["a2"][x, rows] = s["w2"][x, rows] * values

    collect("gf", put_f2)
    sweeps(2, "a2", "b2", 4, 20)
    f3 = down3(lambda k: residue(2, "b2", 4 + 2 * k) + residue(2, "b2", 5 + 2 * k))
    s["f3"][...] = f3

    def coarse(_, v):
        cx, cy, cz = s["cx3"][...], s["cy3"][...], s["cz3"][...]
        after = jnp.concatenate([v[1:], none], 0)
        before = jnp.concatenate([none, v[:-1]], 0)
        u = s["f3"][...] + cx[1:] * after + cx[:-1] * before
        u = u + cy * roll3(v, -1, 1) + roll3(cy * v, 1, 1)
        u = u + cz * roll3(v, -1, 2) + roll3(cz * v, 1, 2)
        return KEEP * v + s["w3"][...] * u

    v3 = loop(0, COARSE_SWEEPS - 1, coarse, s["w3"][...] * f3)

    wide = dot(v3.reshape(128, 128), s["pz3"][...]).reshape(8, 16, 128)
    rows3 = [dot(s["py3"][...], wide[k]) for k in range(8)]
    nothing = jnp.zeros(shape2, F32)
    for k in range(8):
        low = rows3[k - 1] if k else nothing
        high = rows3[k + 1] if k < 7 else nothing
        for i, other in ((0, low), (1, high)):
            x = 4 + 2 * k + i
            add = 0.75 * rows3[k] + 0.25 * other
            s["b2"][x] += jnp.where(in_z2, add, 0.0)
    sweeps(2, "b2", "a2", 4, 20)
    sweeps(2, "a2", "b2", 4, 20)

    for k in range(8):
        s["up1"][16 * k : 16 * k + 16] = dot(s["py2"][...], s["b2"][2 * gx + 1 + k])
    up1 = dot(s["up1"][...], s["pz2"][...])
    arrive_all(FLAT, flat1)
    arrive_all(aside, block1("f1b", 3))
    for x in (1, 2, 3, 8, 9, 10):
        s["f1"][x] = join1("f1b", x, 0.0, 4)
    up1 = up1.reshape(8, 16, 256)
    for x in range(12):
        k = (x - 4) // 2 + 3
        other = up1[k - 1] if x % 2 == 0 else up1[k + 1]
        add = 0.75 * up1[k] + 0.25 * other
        distance = 4 - x if x < 4 else x - 7 if x > 7 else 0
        if distance == 0:
            under = jnp.where(low_row, s["v1"][2, x], s["v1"][0, x])
        else:
            r = s["rv1"]
            after, before = (part(r[int(x > 7), ys], distance) for ys in (1, 0))
            under = jnp.where(low_row, after, before)
        v = jnp.concatenate([s["v1"][1, x], under], 0) + add
        s["a1"][x] = jnp.where(both(m1, x_inside(x - 4, 4, NX // 2)), v, 0.0)
    sweeps(1, "a1", "b1", 1, 11)
    sweeps(1, "b1", "a1", 2, 10)

    arrive_all(EDGES, iterate0)

    def whole0(x):
        nothing = [jnp.zeros(shape, F32) for shape in ((16, 128), (8, 256), (8, 128))]
        if 4 <= x < 12:
            k = x - 4
            z = jnp.where(
                low_lane, roll(s["vz"][1], -16 * k, 1), roll(s["vz"][0], -16 * k - 16, 1)
            )
            i, j = k >> 2, 2 * (k & 3)
            y = jnp.where(
                low_row, roll(s["vy"][1, i], -j, 0), roll(s["vy"][0, i], -j - 2, 0)
            )
            c = [jnp.where(low_lane8, s["vyz"][i, 1], s["vyz"][i, 0]) for i in range(2)]
            c = [roll(c[0], -k - 1, 0), roll(c[1], -k, 0)]
            return join(s["b0"][x, :16, :256], z, y, jnp.where(low_row8, c[1], c[0]))
        xs, distance = (0, 4 - x) if x < 4 else (1, x - 11)
        own = s["vx"][xs, 2 - distance if xs == 0 else distance - 1]
        if distance == 2:
            return join(own, *nothing)
        z = jnp.where(low_lane, s["vxz"][xs, 1, 0], s["vxz"][xs, 0, 0])
        y = jnp.where(low_row, s["vxy"][xs, 1], s["vxy"][xs, 0])
        return join(own, z, y, nothing[2])

    for k in range(8):
        s["up0"][24 * k : 24 * k + 24] = dot(s["py1"][...], s["a1"][2 + k])
    up0 = dot(s["up0"][...], s["pz1"][...]).reshape(8, 24, 384)
    for x in range(2, 14):
        k = (x - 4) // 2 + 2
        other = up0[k - 1] if x % 2 == 0 else up0[k + 1]
        add = 0.75 * up0[k] + 0.25 * other
        v = whole0(x) + add
        s["a0"][x] = jnp.where(both(m0, x_inside(x - 4, 8, NX)), v, 0.0)
    sweeps(0, "a0", "g0", 3, 13)

    def finish(x, carry):
        v, u = total(0, "g0", x)
        out[x - 4] = (KEEP * v + s["w0"][x] * u)[:16, :256]
        return carry

    loop(4, 12, finish, 0)

    leave_all(aside, block1("f1b", 3))
    leave_all(FLAT, flat1)
    leave_all(EDGES, iterate0)
    for name in ("ge", "gf"):
        for part in range(2):
            gathered(name, 1 - part).wait_send()
            handed(name, part, core).wait_send()


def buffers():
    def vmem(*shape):
        return pltpu.VMEM(shape, F32)

    def half(*shape):
        return pltpu.VMEM(shape, BF16)

    table = {
        "sz": vmem(2, 16, 128), "rz": vmem(2, 16, 128),
        "sy": vmem(2, 8, 8, 256), "ry": vmem(2, 8, 8, 256),
        "syz": vmem(2, 2, 8, 128), "ryz": vmem(2, 2, 8, 128),
        "ey": vmem(2, 2, 8, 256), "rey": vmem(2, 2, 8, 256),
        "ez": vmem(2, 2, 16, 128), "rez": vmem(2, 2, 16, 128),
        "ec": vmem(2, 2, 2, 1, 128), "rec": vmem(2, 2, 2, 1, 128),
        "vx": vmem(2, 2, 16, 256), "vy": vmem(2, 2, 8, 256), "vz": vmem(2, 16, 128),
        "pvy": vmem(2, 2, 8, 256), "pvz": vmem(2, 16, 128), "pvxy": vmem(2, 2, 1, 256),
        "vxy": vmem(2, 2, 1, 256), "vxz": vmem(2, 2, 1, 16, 128), "vyz": vmem(2, 2, 8, 128),
        "pvyz": vmem(2, 2, 8, 128),
        "pe1": vmem(2, 2, 2, 8, 128), "re1": vmem(2, 2, 3, 2, 8, 128),
        "ny": vmem(2, 2, 1, 128), "rny": vmem(2, 2, 3, 1, 128),
        "nz": vmem(2, 2, 8, 128), "rnz": vmem(2, 2, 8, 128), "rn": vmem(2, 2, 8, 128),
        "pf1b": vmem(2, 2, 8, 128), "rf1b": vmem(2, 2, 3, 8, 128),
        "pv1": vmem(2, 2, 2, 8, 256), "rv1": vmem(2, 2, 2, 8, 256), "g0": vmem(16, 24, 384),
        "e1": vmem(9, 12, 8, 128), "f1b": vmem(9, 12, 8, 128), "v1": vmem(3, 12, 8, 256),
        "ge": vmem(2, 32, 8, 128), "gf": vmem(2, 32, 8, 128),
        "my0": vmem(32, 64), "mz0": half(256, 128), "my1": vmem(8, 16), "mz1": half(256, 128),
        "my2": vmem(16, 32), "mz2": half(128, 128), "pz3": half(128, 128), "py3": vmem(32, 16),
        "pz2": half(128, 256), "py2": vmem(16, 32), "pz1": half(256, 384), "py1": vmem(24, 16),
        "rs0": vmem(64, 256), "rs1": vmem(16, 256), "rs3": vmem(128, 128),
        "up1": vmem(128, 128), "up0": vmem(192, 256),
        "ie1": vmem(12, 16, 256), "e2": vmem(24, 32, 128), "ie2": vmem(24, 32, 128),
        "f3": vmem(8, 16, 128), "w3": vmem(8, 16, 128), "cx3": vmem(9, 16, 128),
        "cy3": vmem(8, 16, 128), "cz3": vmem(8, 16, 128),
    }
    shapes = {"0": (16, 24, 384), "1": (12, 16, 256), "2": (24, 32, 128)}
    for level, shape in shapes.items():
        for name in ("f", "cx", "cy", "cz", "d", "w", "a", "b"):
            table[name + level] = vmem(*shape)
    table["f_in"], table["e_in"] = vmem(8, 16, 256), vmem(8, 16, 256)
    table["tell"] = pltpu.SemaphoreType.REGULAR((3,))
    table["in_s"] = pltpu.SemaphoreType.DMA((2,))
    table["e0"] = vmem(16, 24, 384)
    for name, number in (("c0", 28), ("v0", 18), ("n1", 18), ("e1", 26), ("f1b", 26), ("v1", 8), ("ge", 4), ("gf", 4)):
        table[name + "_s"] = pltpu.SemaphoreType.DMA((number,))
        table[name + "_r"] = pltpu.SemaphoreType.DMA((number,))
    return table


NAMES = list(buffers())


def on_device(charge, dielectric):
    return pl.pallas_call(
        lambda f, e, o, *s: kernel(f, e, o, s),
        out_shape=jax.ShapeDtypeStruct((8, 16, 256), F32),
        in_specs=[pl.BlockSpec(memory_space=pltpu.HBM)] * 2,
        out_specs=pl.BlockSpec(memory_space=pltpu.VMEM),
        scratch_shapes=list(buffers().values()),
        compiler_params=pltpu.CompilerParams(
            collective_id=0, has_side_effects=True, vmem_limit_bytes=60 * 2**20
        ),
    )(charge, dielectric)


def solution(mesh):
    placed = (P("gx", "gy", "gz"), P("gx", "gy", "gz"))
    return jax.shard_map(
        on_device, mesh=mesh, in_specs=placed, out_specs=P("gx", "gy", "gz"), check_vma=False
    )
```
